128 devices in a mesh: dp: 32 (over z, x, core), seq: 4 (over y).
Axes of the slice: x: 4, y: 4, z: 4, core: 2. Of those that a mesh axis runs over, the one named last changes fastest.
Arguments:
- glu_out: bfloat16 [64, 2048, 1536], P('dp', 'seq'), may hold values from -6 to 6
- lengths: int32 [64, 8], P('dp'), may hold values from 1 to 512, 2048 in all within a row
- kernel: float32 [31, 1536], replicated, may hold values from -1 to 1
- norm_gain: float32 [1536], replicated, may hold values from 0.1 to 1.9
- norm_bias: float32 [1536], replicated, may hold values from -3 to 3
- w_out: bfloat16 [1536, 1536], replicated, may hold values from -0.15625 to 0.15625
- cotangent: bfloat16 [64, 2048, 1536], P('dp', 'seq'), may hold values from -6 to 6
Outputs:
- layer_out: bfloat16 [64, 2048, 1536], P('dp', 'seq')
- grad_input: bfloat16 [64, 2048, 1536], P('dp', 'seq')
- grad_w_out: float32 [1536, 1536], P('seq')
- grad_kernel: float32 [31, 1536], replicated
- grad_gain: float32 [1536], replicated
- grad_bias: float32 [1536], replicated
The draws below stay inside these ranges and needn't reach their ends.
Inputs may be any that keep to these rules, and one draw needn't show every extreme that they name: Each lane's 8 utterance lengths sum to 2048, and the longest is exactly 512 frames.
All inputs are finite; a program needn't handle non-finite values.
Results may differ from the reference program's by a relative error of at most 0.0049.
Values may be sent and summed in bfloat16 or wider, within the bound.
No kernel may reach another device: no remote copies, remote signals or barrier semaphores. Data moves between devices by JAX's collectives and lax.ppermute only.
A program may use at most 128 MiB of HBM per device.

```python
import math
import jax
import jax.numpy as jnp
import numpy as np
from jax import lax

D = 1536
K = 31
UTTS = 8
LANES = 64
TIME = 2048
MOST = 512


def block_levels(own_key, dims, split, smallest, largest):
    def one(axis_at, shards_of):
        heights = jax.random.uniform(jax.random.fold_in(jax.random.fold_in(own_key, 6), axis_at), (shards_of,), jnp.float32, smallest / len(split), largest / len(split))
        return jnp.repeat(jnp.exp(heights), dims[axis_at] // shards_of).reshape((-1,) + (1,) * (len(dims) - axis_at - 1))

    level = one(*split[0])
    for cut in split[1:]:
        level = level * one(*cut)
    return level


def profile(number_of, total, most, lean):
    weights = [(1 << 20) // math.isqrt(grade ** lean) + 1 for grade in range(2, number_of + 1)]
    rest, counts = total - most - (number_of - 1), [1] * (number_of - 1)
    while rest > 0:
        candidates = [i for i in range(number_of - 1) if counts[i] < most]
        pool, left = sum([weights[i] for i in candidates]), rest
        for i in candidates:
            extra = min(most - counts[i], max(1, left * weights[i] // pool), rest)
            counts[i] = counts[i] + extra
            rest = rest - extra
    return np.array([most] + counts)


def ragged(stream_key, amount, total, limit, skew):
    if amount == 2:
        one = jax.random.randint(stream_key, (), max(1, total - limit), min(limit, total - 1) + 1)
        return jnp.stack([one, total - one])
    tallies = jnp.asarray(profile(amount, total, limit, skew), jnp.int32)
    couples = (amount - 1) // 2
    donor, receiver = tallies[1:1 + 2 * couples:2], tallies[2:2 + 2 * couples:2]
    margin = jnp.minimum(donor - 1, limit - receiver)
    moved = jax.random.randint(jax.random.fold_in(stream_key, 1), (couples,), 0, 1 << 20) % (margin + 1)
    tallies = tallies.at[1:1 + 2 * couples:2].set(donor - moved).at[2:2 + 2 * couples:2].set(receiver + moved)
    return tallies[jax.random.permutation(jax.random.fold_in(stream_key, 2), amount)]


def scatter_about(stream_key, extent, width, most, split=(), held_as=jnp.bfloat16):
    values = width * jax.random.normal(stream_key, extent, jnp.float32)
    if split:
        values = values * block_levels(stream_key, extent, split, -0.22, 0.18)
    return jnp.clip(values, -most, most).astype(held_as)


def setup_inputs(seed: int = 0) -> dict:
    arg_keys = jax.random.split(jax.random.key(seed), 8)
    return {
        "glu_out": scatter_about(arg_keys[0], (LANES, TIME, D), 1.0, 6.0, ((0, 32), (1, 4))),
        "lengths": jax.vmap(lambda own: ragged(own, UTTS, TIME, MOST, 2))(jax.random.split(arg_keys[1], LANES)).reshape((LANES, UTTS)).astype(jnp.int32),
        "kernel": scatter_about(arg_keys[2], (K, D), K ** -0.5, 1.0, (), jnp.float32),
        "norm_gain": jnp.clip(1.0 + 0.18 * jax.random.normal(arg_keys[3], (D,), jnp.float32), 0.1, 1.9),
        "norm_bias": scatter_about(arg_keys[4], (D,), 0.5, 3.0, (), jnp.float32),
        "w_out": scatter_about(arg_keys[5], (D, D), D ** -0.5, 0.15625),
        "cotangent": scatter_about(arg_keys[6], (LANES, TIME, D), 1.0, 6.0, ((0, 32), (1, 4))),
    }


EPSILON = 1e-05

def segment_of(lengths, positions):
    utter_ends = jnp.cumsum(lengths, axis=-1)
    return lax.optimization_barrier(jnp.sum((utter_ends[..., None, :] <= positions[:, None]).astype(jnp.int32), axis=-1))

def reference(glu_out, lengths, kernel, norm_gain, norm_bias, w_out, cotangent):
    taps = kernel.shape[0]
    half_width = taps // 2
    time_len = glu_out.shape[1]
    channels = glu_out.shape[2]
    positions = jnp.arange(time_len + 2 * half_width, dtype=jnp.int32) - half_width
    inside = (positions >= 0) & (positions < time_len)
    norm_scale = 1.0 / math.sqrt(glu_out.shape[0] * time_len)

    def lane_step(carry, lane):
        sum_w, sum_kernel, sum_gain, sum_bias = carry
        glu_lane, length_lane, cot_lane = lane
        segment = jnp.where(inside, segment_of(length_lane, positions), -1)
        own_segment = segment[half_width:half_width + time_len]
        padded = jnp.pad(glu_lane, ((half_width, half_width), (0, 0))).astype(jnp.float32)
        conv = jnp.zeros((time_len, channels), jnp.float32)
        for offset in range(taps):
            match = (segment[offset:offset + time_len] == own_segment).astype(jnp.float32)[:, None]
            conv = conv + kernel[offset] * padded[offset:offset + time_len] * match
        average = lax.optimization_barrier(jnp.mean(conv, axis=-1, keepdims=True))
        centred = conv - average
        variance = lax.optimization_barrier(jnp.mean(centred * centred, axis=-1, keepdims=True))
        inv_std = lax.rsqrt(variance + EPSILON)
        normed = centred * inv_std
        affine = normed * norm_gain + norm_bias
        gate_sigmoid = jax.nn.sigmoid(affine)
        swished = (affine * gate_sigmoid).astype(jnp.bfloat16)
        output_lane = jnp.dot(swished, w_out, preferred_element_type=jnp.float32).astype(jnp.bfloat16)
        sum_w = sum_w + lax.dot_general(swished, cot_lane, (((0,), (0,)), ((), ())), preferred_element_type=jnp.float32)
        grad_swish = lax.dot_general(cot_lane, w_out, (((1,), (1,)), ((), ())), preferred_element_type=jnp.float32)
        grad_affine = grad_swish * gate_sigmoid * (1.0 + affine * (1.0 - gate_sigmoid))
        sum_gain = sum_gain + lax.optimization_barrier(jnp.sum(grad_affine * normed, axis=0))
        sum_bias = sum_bias + lax.optimization_barrier(jnp.sum(grad_affine, axis=0))
        grad_normed = grad_affine * norm_gain
        grad_conv = inv_std * (grad_normed - lax.optimization_barrier(jnp.mean(grad_normed, axis=-1, keepdims=True)) - normed * lax.optimization_barrier(jnp.mean(grad_normed * normed, axis=-1, keepdims=True)))
        grad_pad = jnp.pad(grad_conv, ((half_width, half_width), (0, 0)))
        grad_lane = jnp.zeros((time_len, channels), jnp.float32)
        kernel_rows = []
        for offset in range(taps):
            back_index = 2 * half_width - offset
            back_match = (segment[back_index:back_index + time_len] == own_segment).astype(jnp.float32)[:, None]
            grad_lane = grad_lane + kernel[offset] * grad_pad[back_index:back_index + time_len] * back_match
            match = (segment[offset:offset + time_len] == own_segment).astype(jnp.float32)[:, None]
            kernel_rows.append(lax.optimization_barrier(jnp.sum(grad_conv * padded[offset:offset + time_len] * match, axis=0)))
        sum_kernel = sum_kernel + jnp.stack(kernel_rows, axis=0)
        return ((sum_w, sum_kernel, sum_gain, sum_bias), (output_lane, grad_lane.astype(jnp.bfloat16)))
    initial = (jnp.zeros((channels, channels), jnp.float32), jnp.zeros((taps, channels), jnp.float32), jnp.zeros((channels,), jnp.float32), jnp.zeros((channels,), jnp.float32))
    sums, stacked = lax.scan(lane_step, initial, (glu_out, lengths, cotangent))
    layer_out, grad_input = stacked
    return (layer_out, grad_input, sums[0] * norm_scale, sums[1] * norm_scale, sums[2] * norm_scale, sums[3] * norm_scale)
```

```python
import functools
import math

import jax
import jax.numpy as jnp
import numpy as np
from jax import lax
from jax.experimental import pallas as pl
from jax.experimental.pallas import tpu as pltpu
from jax.sharding import PartitionSpec as P

EPSILON = 1e-05
TAPS = 31
HALF = TAPS // 2
ROWS = 128
EDGE = 16
WINDOW = ROWS + 2 * EDGE
POINTS = 256
BINS = POINTS // 2
f32, bf16 = jnp.float32, jnp.bfloat16


def tables():
    place = np.arange(POINTS)
    bins = np.arange(BINS)[:, None]
    cosines = math.sqrt(2.0 / POINTS) * np.cos(2 * np.pi * ((bins * place) % POINTS) / POINTS)
    sines = math.sqrt(2.0 / POINTS) * np.sin(2 * np.pi * ((bins * place) % POINTS) / POINTS)
    cosines[0] = 1.0 / math.sqrt(POINTS)
    sines[0] = (1.0 - 2.0 * (place % 2)) / math.sqrt(POINTS)
    basis = np.concatenate([cosines, sines])
    high = basis.astype(jnp.bfloat16)
    low = (basis - high.astype(np.float64)).astype(jnp.bfloat16)
    split = np.concatenate([high, low])
    lags = np.arange(TAPS) - HALF
    turn = 2 * np.pi * ((bins * lags) % POINTS) / POINTS
    real, imag = np.cos(turn), np.sin(turn)
    other = real.copy()
    other[0] = 1.0 - 2.0 * (np.abs(lags) % 2)
    spectrum = np.concatenate([real, imag, other]).astype(np.float32)
    gather = np.concatenate([real, other, -imag]).astype(np.float32)
    return split, spectrum, gather


def gapped(lengths_ref, lane, first, shape, dim, skip):
    row = lax.broadcasted_iota(jnp.int32, shape, dim) + skip
    frame = first + row
    place, end = row, 0
    for utter in range(lengths_ref.shape[1] - 1):
        end = end + lengths_ref[lane, utter]
        place = place + jnp.where(frame >= end, jnp.where(first < end, HALF, 0), 0)
    return place


def chosen_columns(split, place):
    count = place.shape[1]
    one_hot = (lax.broadcasted_iota(jnp.int32, (POINTS, count), 0) == place).astype(f32).astype(bf16)
    return jnp.dot(split, one_hot, preferred_element_type=f32).astype(bf16)


def chosen_rows(split_t, place):
    count = place.shape[0]
    one_hot = (lax.broadcasted_iota(jnp.int32, (count, POINTS), 1) == place).astype(f32).astype(bf16)
    return jnp.dot(one_hot, split_t, preferred_element_type=f32).astype(bf16)


def dot(a, b):
    return jnp.dot(a, b, preferred_element_type=f32)


def sigmoid(a):
    return 0.5 * jnp.tanh(0.5 * a) + 0.5


def forward_kernel(blocks, meta_ref, lengths_ref, x_ref, prev_ref, next_ref, before_ref, after_ref, split_ref,
                   split_t_ref, spec_ref, gain_ref, bias_ref, sw_ref, normed_ref, istd_ref, xhat_ref, win, conv):
    step = pl.program_id(0)
    lane, block = step // blocks, step % blocks
    channels = x_ref.shape[1]
    first = meta_ref[0] + block * ROWS - EDGE
    win[EDGE : EDGE + ROWS] = x_ref[...]
    win[:EDGE] = jnp.where(block == 0, before_ref[...], prev_ref[...])
    win[EDGE + ROWS :] = jnp.where(block == blocks - 1, after_ref[...], next_ref[...])
    into = chosen_columns(split_ref[...], gapped(lengths_ref, lane, first, (1, WINDOW), 1, 0))
    back = chosen_rows(split_t_ref[...], gapped(lengths_ref, lane, first, (ROWS, 1), 0, EDGE))
    width = 512
    for at in range(0, channels, width):
        cols = slice(at, at + width)
        rows = win[:, cols]
        xhat = dot(into[:POINTS], rows) + dot(into[POINTS:], rows)
        xhat_ref[:, cols] = xhat.astype(bf16)
        real, imag = xhat[:BINS], xhat[BINS:]
        p, q, other = spec_ref[:BINS, cols], spec_ref[BINS:POINTS, cols], spec_ref[POINTS:, cols]
        zed = jnp.concatenate([real * p + imag * q, imag * other - real * q]).astype(bf16)
        conv[:, cols] = dot(back[:, :POINTS], zed) + dot(back[:, POINTS:], zed)
    gain, bias = gain_ref[...], bias_ref[...]
    strip = 16
    for at in range(0, ROWS, strip):
        rows = slice(at, at + strip)
        value = conv[rows]
        centred = value - jnp.sum(value, axis=1, keepdims=True) * (1.0 / channels)
        variance = jnp.sum(centred * centred, axis=1, keepdims=True) * (1.0 / channels)
        inv_std = lax.rsqrt(variance + EPSILON)
        normed = centred * inv_std
        affine = normed * gain + bias
        sw_ref[rows] = (affine * sigmoid(affine)).astype(bf16)
        normed_ref[rows] = normed
        istd_ref[rows] = jnp.broadcast_to(inv_std, (strip, istd_ref.shape[1]))


def backward_kernel(blocks, meta_ref, lengths_ref, cot_ref, sw_ref, normed_ref, istd_ref, xhat_ref, w_ref, split_ref,
                    split_t_ref, spec_ref, gather_ref, gain_ref, bias_ref, layer_ref, gi_ref, edge_ref, small_ref,
                    gs, g, acc, sums, pending, tail):
    step = pl.program_id(0)
    lane, block = step // blocks, step % blocks
    channels = cot_ref.shape[1]
    first = meta_ref[0] + block * ROWS - EDGE

    @pl.when(step == 0)
    def _():
        acc[...] = jnp.zeros_like(acc)
        sums[...] = jnp.zeros_like(sums)

    layer_ref[...] = dot(sw_ref[...], w_ref[...]).astype(bf16)
    gs[...] = lax.dot_general(cot_ref[...], w_ref[...], (((1,), (1,)), ((), ())), preferred_element_type=f32)
    gain, bias = gain_ref[...], bias_ref[...]
    strip = 16
    for at in range(0, ROWS, strip):
        rows = slice(at, at + strip)
        normed = normed_ref[rows]
        affine = normed * gain + bias
        gate = sigmoid(affine)
        grad = gs[rows] * gate * (1.0 + affine * (1.0 - gate))
        prod = grad * normed
        sums[:8] += prod[:8] + prod[8:]
        sums[8:] += grad[:8] + grad[8:]
        grad_normed = grad * gain
        mean = jnp.sum(grad_normed, axis=1, keepdims=True) * (1.0 / channels)
        along = jnp.sum(grad_normed * normed, axis=1, keepdims=True) * (1.0 / channels)
        out = (istd_ref[rows, :1] * (grad_normed - mean - normed * along)).astype(bf16)
        g[rows] = out
        g[ROWS + at : ROWS + at + strip] = out
    into = chosen_columns(split_ref[...], gapped(lengths_ref, lane, first, (1, ROWS), 1, EDGE))
    into = jnp.concatenate([into[:POINTS], into[POINTS:]], axis=1)
    back = chosen_rows(split_t_ref[...], gapped(lengths_ref, lane, first, (WINDOW, 1), 0, 0))
    is_first, is_last = block == 0, block == blocks - 1
    base = pl.multiple_of(step * ROWS, ROWS)
    width = 512
    for at in range(0, channels, width):
        cols = slice(at, at + width)
        ghat = dot(into, g[:, cols])
        cg, sg = ghat[:BINS], ghat[BINS:]
        cx, sx = xhat_ref[:BINS, cols].astype(f32), xhat_ref[BINS:, cols].astype(f32)
        acc[:BINS, cols] += cg * cx
        acc[BINS:POINTS, cols] += sg * sx
        acc[POINTS:, cols] += sg * cx - cg * sx
        p, q, other = spec_ref[:BINS, cols], spec_ref[BINS:POINTS, cols], spec_ref[POINTS:, cols]
        vee = jnp.concatenate([cg * p - sg * q, sg * other + cg * q]).astype(bf16)
        part = dot(back[:, :POINTS], vee) + dot(back[:, POINTS:], vee)
        own = part[EDGE : EDGE + ROWS]
        carried = jnp.where(is_first, 0.0, tail[:, cols])
        gi_ref[pl.ds(base, EDGE), cols] = (own[:EDGE] + carried).astype(bf16)
        gi_ref[pl.ds(base + EDGE, ROWS - 2 * EDGE), cols] = own[EDGE : ROWS - EDGE].astype(bf16)
        gi_ref[pl.ds(base + ROWS - EDGE, EDGE), cols] = own[ROWS - EDGE :].astype(bf16)
        head = part[:EDGE]

        @pl.when(jnp.logical_not(is_first))
        def _():
            gi_ref[pl.ds(pl.multiple_of(base - EDGE, EDGE), EDGE), cols] = (pending[:, cols] + head).astype(bf16)

        @pl.when(is_first)
        def _():
            edge_ref[pl.ds(lane * 2 * EDGE, EDGE), cols] = head.astype(bf16)

        pending[:, cols] = own[ROWS - EDGE :]
        tail[:, cols] = part[EDGE + ROWS :]

        @pl.when(is_last)
        def _():
            edge_ref[pl.ds(lane * 2 * EDGE + EDGE, EDGE), cols] = part[EDGE + ROWS :].astype(bf16)

    @pl.when(step == pl.num_programs(0) - 1)
    def _():
        table = gather_ref[...]
        table_high = table.astype(bf16)
        table_low = (table - table_high.astype(f32)).astype(bf16)
        for at in range(0, channels, width):
            cols = slice(at, at + width)
            value = acc[:, cols]
            high = value.astype(bf16)
            low = (value - high.astype(f32)).astype(bf16)
            small_ref[:32, cols] = dot(table_high, high) + dot(table_low, high) + dot(table_high, low)
        prod, grad = sums[:8], sums[8:]
        small_ref[32:40] = jnp.concatenate(
            [
                jnp.sum(prod, axis=0, keepdims=True),
                jnp.sum(grad, axis=0, keepdims=True),
                jnp.zeros((6, channels), f32),
            ]
        )


def whole(shape):
    return pl.BlockSpec(shape, lambda i: (0,) * len(shape))


SMEM = pl.BlockSpec(memory_space=pltpu.SMEM)


def forward(meta, lengths, x, before, after, split, split_t, spec, gain, bias, interpret=False):
    lanes, length, channels = x.shape
    blocks = length // ROWS
    steps = lanes * blocks
    flat = x.reshape(lanes * length, channels)
    per = ROWS // EDGE
    last = lanes * length // EDGE - 1
    row = pl.BlockSpec((ROWS, channels), lambda i: (i, 0))
    halo = pl.BlockSpec((EDGE, channels), lambda i: (i // blocks, 0))
    return pl.pallas_call(
        functools.partial(forward_kernel, blocks),
        grid=(steps,),
        in_specs=[
            SMEM,
            SMEM,
            row,
            pl.BlockSpec((EDGE, channels), lambda i: (jnp.maximum(i * per - 1, 0), 0)),
            pl.BlockSpec((EDGE, channels), lambda i: (jnp.minimum(i * per + per, last), 0)),
            halo,
            halo,
            whole(split.shape),
            whole(split_t.shape),
            whole(spec.shape),
            whole((1, channels)),
            whole((1, channels)),
        ],
        out_specs=[
            row,
            row,
            pl.BlockSpec((ROWS, 128), lambda i: (i, 0)),
            pl.BlockSpec((POINTS, channels), lambda i: (i, 0)),
        ],
        out_shape=[
            jax.ShapeDtypeStruct((lanes * length, channels), bf16),
            jax.ShapeDtypeStruct((lanes * length, channels), f32),
            jax.ShapeDtypeStruct((lanes * length, 128), f32),
            jax.ShapeDtypeStruct((steps * POINTS, channels), bf16),
        ],
        scratch_shapes=[pltpu.VMEM((WINDOW, channels), bf16), pltpu.VMEM((ROWS, channels), f32)],
        compiler_params=pltpu.CompilerParams(vmem_limit_bytes=40 << 20),
        interpret=interpret,
        name="conv_norm_swish",
    )(
        meta,
        lengths,
        flat,
        flat,
        flat,
        before.reshape(lanes * EDGE, channels),
        after.reshape(lanes * EDGE, channels),
        split,
        split_t,
        spec,
        gain,
        bias,
    )


def backward(meta, lengths, cot, sw, normed, istd, xhat, w, split, split_t, spec, gather, gain, bias, lanes,
             interpret=False):
    total, channels = cot.shape
    steps = total // ROWS
    blocks = steps // lanes
    row = pl.BlockSpec((ROWS, channels), lambda i: (i, 0))
    return pl.pallas_call(
        functools.partial(backward_kernel, blocks),
        grid=(steps,),
        in_specs=[
            SMEM,
            SMEM,
            row,
            row,
            row,
            pl.BlockSpec((ROWS, 128), lambda i: (i, 0)),
            pl.BlockSpec((POINTS, channels), lambda i: (i, 0)),
            whole(w.shape),
            whole(split.shape),
            whole(split_t.shape),
            whole(spec.shape),
            whole(gather.shape),
            whole((1, channels)),
            whole((1, channels)),
        ],
        out_specs=[row, whole((total, channels)), whole((lanes * 2 * EDGE, channels)), whole((40, channels))],
        out_shape=[
            jax.ShapeDtypeStruct((total, channels), bf16),
            jax.ShapeDtypeStruct((total, channels), bf16),
            jax.ShapeDtypeStruct((lanes * 2 * EDGE, channels), bf16),
            jax.ShapeDtypeStruct((40, channels), f32),
        ],
        scratch_shapes=[
            pltpu.VMEM((ROWS, channels), f32),
            pltpu.VMEM((2 * ROWS, channels), bf16),
            pltpu.VMEM((3 * BINS, channels), f32),
            pltpu.VMEM((16, channels), f32),
            pltpu.VMEM((EDGE, channels), f32),
            pltpu.VMEM((EDGE, channels), f32),
        ],
        compiler_params=pltpu.CompilerParams(vmem_limit_bytes=56 << 20),
        interpret=interpret,
        name="backward",
    )(meta, lengths, cot, sw, normed, istd, xhat, w, split, split_t, spec, gather, gain, bias)


def shifts(size):
    up = [(i, i + 1) for i in range(size - 1)]
    return up, [(j, i) for i, j in up]


def local(glu_out, lengths, kernel, norm_gain, norm_bias, w_out, cotangent, interpret=False):
    lanes, length, channels = glu_out.shape
    seq_count = lax.axis_size("seq")
    norm_scale = 1.0 / math.sqrt(lanes * lax.axis_size("dp") * length * seq_count)
    seq_place = lax.axis_index("seq")
    up, down = shifts(seq_count)
    before = lax.ppermute(glu_out[:, length - EDGE :], "seq", up)
    after = lax.ppermute(glu_out[:, :EDGE], "seq", down)
    split, spectrum, gather = tables()
    spec = jnp.dot(jnp.asarray(spectrum), kernel, precision=lax.Precision.HIGHEST)
    split_t = jnp.asarray(np.ascontiguousarray(split.T))
    split = jnp.asarray(split)
    table = np.zeros((32, 3 * BINS), np.float32)
    table[:TAPS] = gather.T
    gain, bias = norm_gain.reshape(1, channels), norm_bias.reshape(1, channels)
    meta = jnp.reshape(seq_place * length, (1,)).astype(jnp.int32)
    sw, normed, istd, xhat = forward(
        meta, lengths, glu_out, before, after, split, split_t, spec, gain, bias, interpret=interpret
    )
    cot = cotangent.reshape(-1, channels)
    outer = lax.dot_general(sw, cot, (((0,), (0,)), ((), ())), preferred_element_type=f32)
    summed = lax.psum(outer, ("dp", "seq"))
    share = channels // seq_count
    grad_w = lax.dynamic_slice_in_dim(summed, seq_place * share, share, 0) * norm_scale
    layer, gi, edge, small = backward(
        meta, lengths, cot, sw, normed, istd, xhat, w_out, split, split_t, spec, jnp.asarray(table), gain, bias, lanes,
        interpret=interpret,
    )
    edge = edge.reshape(lanes, 2, EDGE, channels)
    from_after = lax.ppermute(edge[:, 0], "seq", down)
    from_before = lax.ppermute(edge[:, 1], "seq", up)
    gi = gi.reshape(lanes, length, channels)
    gi = gi.at[:, :EDGE].add(from_before).at[:, length - EDGE :].add(from_after)
    small = lax.psum(small, ("dp", "seq")) * norm_scale
    return (
        layer.reshape(lanes, length, channels),
        gi,
        grad_w,
        small[:TAPS],
        small[32],
        small[33],
    )


def solution(mesh):
    in_specs = (P("dp", "seq", None), P("dp", None), P(), P(), P(), P(), P("dp", "seq", None))
    out_specs = (P("dp", "seq", None), P("dp", "seq", None), P("seq", None), P(), P(), P())
    return jax.shard_map(local, mesh=mesh, in_specs=in_specs, out_specs=out_specs, check_vma=False)
```

```python
import functools
import math

import jax
import jax.numpy as jnp
import numpy as np
from jax import lax
from jax.experimental import pallas as pl
from jax.experimental.pallas import tpu as pltpu
from jax.sharding import PartitionSpec as P

EPSILON = 1e-05
TAPS = 31
HALF = TAPS // 2
ROWS = 128
EDGE = 16
WINDOW = ROWS + 2 * EDGE
POINTS = 256
BINS = POINTS // 2
f32, bf16 = jnp.float32, jnp.bfloat16


def tables():
    place = np.arange(POINTS)
    bins = np.arange(BINS)[:, None]
    cosines = math.sqrt(2.0 / POINTS) * np.cos(2 * np.pi * ((bins * place) % POINTS) / POINTS)
    sines = math.sqrt(2.0 / POINTS) * np.sin(2 * np.pi * ((bins * place) % POINTS) / POINTS)
    cosines[0] = 1.0 / math.sqrt(POINTS)
    sines[0] = (1.0 - 2.0 * (place % 2)) / math.sqrt(POINTS)
    basis = np.concatenate([cosines, sines])
    high = basis.astype(jnp.bfloat16)
    low = (basis - high.astype(np.float64)).astype(jnp.bfloat16)
    split = np.concatenate([high, low])
    lags = np.arange(TAPS) - HALF
    turn = 2 * np.pi * ((bins * lags) % POINTS) / POINTS
    real, imag = np.cos(turn), np.sin(turn)
    other = real.copy()
    other[0] = 1.0 - 2.0 * (np.abs(lags) % 2)
    spectrum = np.concatenate([real, imag, other]).astype(np.float32)
    gather = np.concatenate([real, other, -imag]).astype(np.float32)
    wide, deep = np.zeros((3 * BINS, 32), np.float32), np.zeros((32, 3 * BINS), np.float32)
    wide[:, :TAPS], deep[:TAPS] = spectrum, gather.T
    return split, np.ascontiguousarray(split.T), wide, deep


def gapped(lengths_ref, lane, first, shape, dim, skip):
    row = lax.broadcasted_iota(jnp.int32, shape, dim) + skip
    frame = first + row
    place, end = row, 0
    for utter in range(lengths_ref.shape[1] - 1):
        end = end + lengths_ref[lane, utter]
        place = place + jnp.where(frame >= end, jnp.where(first < end, HALF, 0), 0)
    return place


def chosen_columns(split, place):
    count = place.shape[1]
    one_hot = (lax.broadcasted_iota(jnp.int32, (POINTS, count), 0) == place).astype(f32).astype(bf16)
    return jnp.dot(split, one_hot, preferred_element_type=f32).astype(bf16)


def chosen_rows(split_t, place):
    count = place.shape[0]
    one_hot = (lax.broadcasted_iota(jnp.int32, (count, POINTS), 1) == place).astype(f32).astype(bf16)
    return jnp.dot(one_hot, split_t, preferred_element_type=f32).astype(bf16)


def dot(a, b):
    return jnp.dot(a, b, preferred_element_type=f32)


def sigmoid(a):
    return 0.5 * jnp.tanh(0.5 * a) + 0.5


def forward_kernel(lane, blocks, meta_ref, lengths_ref, x_ref, prev_ref, next_ref, before_ref, after_ref, split_ref,
                   split_t_ref, spec_ref, gain_ref, bias_ref, sw_ref, normed_ref, istd_ref, xhat_ref, win, conv):
    block = pl.program_id(0)
    channels = x_ref.shape[1]
    first = meta_ref[0] + block * ROWS - EDGE
    win[EDGE : EDGE + ROWS] = x_ref[...]
    win[:EDGE] = jnp.where(block == 0, before_ref[...], prev_ref[...])
    win[EDGE + ROWS :] = jnp.where(block == blocks - 1, after_ref[...], next_ref[...])
    into = chosen_columns(split_ref[...], gapped(lengths_ref, lane, first, (1, WINDOW), 1, 0))
    back = chosen_rows(split_t_ref[...], gapped(lengths_ref, lane, first, (ROWS, 1), 0, EDGE))
    width = 512
    for at in range(0, channels, width):
        cols = slice(at, at + width)
        rows = win[:, cols]
        xhat = dot(into[:POINTS], rows) + dot(into[POINTS:], rows)
        xhat_ref[:, cols] = xhat.astype(bf16)
        real, imag = xhat[:BINS], xhat[BINS:]
        p, q, other = spec_ref[:BINS, cols], spec_ref[BINS:POINTS, cols], spec_ref[POINTS:, cols]
        zed = jnp.concatenate([real * p + imag * q, imag * other - real * q]).astype(bf16)
        conv[:, cols] = dot(back[:, :POINTS], zed) + dot(back[:, POINTS:], zed)
    gain, bias = gain_ref[...], bias_ref[...]
    strip = 16
    for at in range(0, ROWS, strip):
        rows = slice(at, at + strip)
        value = conv[rows]
        centred = value - jnp.sum(value, axis=1, keepdims=True) * (1.0 / channels)
        variance = jnp.sum(centred * centred, axis=1, keepdims=True) * (1.0 / channels)
        inv_std = lax.rsqrt(variance + EPSILON)
        normed = centred * inv_std
        affine = normed * gain + bias
        sw_ref[rows] = (affine * sigmoid(affine)).astype(bf16)
        normed_ref[rows] = normed
        istd_ref[rows] = jnp.broadcast_to(inv_std, (strip, istd_ref.shape[1]))


def backward_kernel(lane, blocks, meta_ref, lengths_ref, cot_ref, sw_ref, normed_ref, istd_ref, xhat_ref, w_ref, split_ref,
                    split_t_ref, spec_ref, gather_ref, gain_ref, bias_ref, layer_ref, gi_ref, edge_ref, small_ref,
                    gs, g, acc, sums, pending, tail):
    block = pl.program_id(0)
    channels = cot_ref.shape[1]
    first = meta_ref[0] + block * ROWS - EDGE

    @pl.when(block == 0)
    def _():
        acc[...] = jnp.zeros_like(acc)
        sums[...] = jnp.zeros_like(sums)

    layer_ref[...] = dot(sw_ref[...], w_ref[...]).astype(bf16)
    gs[...] = lax.dot_general(cot_ref[...], w_ref[...], (((1,), (1,)), ((), ())), preferred_element_type=f32)
    gain, bias = gain_ref[...], bias_ref[...]
    strip = 16
    for at in range(0, ROWS, strip):
        rows = slice(at, at + strip)
        normed = normed_ref[rows]
        affine = normed * gain + bias
        gate = sigmoid(affine)
        grad = gs[rows] * gate * (1.0 + affine * (1.0 - gate))
        prod = grad * normed
        sums[:8] += prod[:8] + prod[8:]
        sums[8:] += grad[:8] + grad[8:]
        grad_normed = grad * gain
        mean = jnp.sum(grad_normed, axis=1, keepdims=True) * (1.0 / channels)
        along = jnp.sum(grad_normed * normed, axis=1, keepdims=True) * (1.0 / channels)
        out = (istd_ref[rows, :1] * (grad_normed - mean - normed * along)).astype(bf16)
        g[rows] = out
        g[ROWS + at : ROWS + at + strip] = out
    into = chosen_columns(split_ref[...], gapped(lengths_ref, lane, first, (1, ROWS), 1, EDGE))
    into = jnp.concatenate([into[:POINTS], into[POINTS:]], axis=1)
    back = chosen_rows(split_t_ref[...], gapped(lengths_ref, lane, first, (WINDOW, 1), 0, 0))
    is_first, is_last = block == 0, block == blocks - 1
    base = pl.multiple_of(block * ROWS, ROWS)
    width = 512
    for at in range(0, channels, width):
        cols = slice(at, at + width)
        ghat = dot(into, g[:, cols])
        cg, sg = ghat[:BINS], ghat[BINS:]
        cx, sx = xhat_ref[:BINS, cols].astype(f32), xhat_ref[BINS:, cols].astype(f32)
        acc[:BINS, cols] += cg * cx
        acc[BINS:POINTS, cols] += sg * sx
        acc[POINTS:, cols] += sg * cx - cg * sx
        p, q, other = spec_ref[:BINS, cols], spec_ref[BINS:POINTS, cols], spec_ref[POINTS:, cols]
        vee = jnp.concatenate([cg * p - sg * q, sg * other + cg * q]).astype(bf16)
        part = dot(back[:, :POINTS], vee) + dot(back[:, POINTS:], vee)
        own = part[EDGE : EDGE + ROWS]
        carried = jnp.where(is_first, 0.0, tail[:, cols])
        gi_ref[pl.ds(base, EDGE), cols] = (own[:EDGE] + carried).astype(bf16)
        gi_ref[pl.ds(base + EDGE, ROWS - 2 * EDGE), cols] = own[EDGE : ROWS - EDGE].astype(bf16)
        gi_ref[pl.ds(base + ROWS - EDGE, EDGE), cols] = own[ROWS - EDGE :].astype(bf16)
        head = part[:EDGE]

        @pl.when(jnp.logical_not(is_first))
        def _():
            gi_ref[pl.ds(pl.multiple_of(base - EDGE, EDGE), EDGE), cols] = (pending[:, cols] + head).astype(bf16)

        @pl.when(is_first)
        def _():
            edge_ref[:EDGE, cols] = head.astype(bf16)

        pending[:, cols] = own[ROWS - EDGE :]
        tail[:, cols] = part[EDGE + ROWS :]

        @pl.when(is_last)
        def _():
            edge_ref[EDGE:, cols] = part[EDGE + ROWS :].astype(bf16)

    @pl.when(is_last)
    def _():
        table = gather_ref[...]
        table_high = table.astype(bf16)
        table_low = (table - table_high.astype(f32)).astype(bf16)
        for at in range(0, channels, width):
            cols = slice(at, at + width)
            value = acc[:, cols]
            high = value.astype(bf16)
            low = (value - high.astype(f32)).astype(bf16)
            small_ref[:32, cols] = dot(table_high, high) + dot(table_low, high) + dot(table_high, low)
        prod, grad = sums[:8], sums[8:]
        small_ref[32:40] = jnp.concatenate(
            [
                jnp.sum(prod, axis=0, keepdims=True),
                jnp.sum(grad, axis=0, keepdims=True),
                jnp.zeros((6, channels), f32),
            ]
        )


def halves(value):
    high = value.astype(bf16)
    return high, (value - high.astype(f32)).astype(bf16)


def spectrum_kernel(table_ref, kernel_ref, spec_ref):
    table_high, table_low = halves(table_ref[...])
    high, low = halves(kernel_ref[...])
    spec_ref[...] = dot(table_high, high) + dot(table_low, high) + dot(table_high, low)


def outer_kernel(meta_ref, sw0_ref, sw1_ref, sw2_ref, cot_ref, other_ref, acc_ref):
    rows = sw0_ref.shape[0]
    turned = (((0,), (0,)), ((), ()))
    acc_ref[...] = (
        lax.dot_general(sw0_ref[...], cot_ref[:rows], turned, preferred_element_type=f32)
        + lax.dot_general(sw1_ref[...], cot_ref[rows:], turned, preferred_element_type=f32)
        + lax.dot_general(sw2_ref[...], other_ref[...], turned, preferred_element_type=f32)
    )


def last_outer_kernel(meta_ref, acc_ref, sw_ref, cot_ref, own_ref, one_ref, two_ref, three_ref, total):
    turned = (((0,), (0,)), ((), ()))
    share = acc_ref.shape[0] // 4
    piece = share // 4
    for at in range(4):
        rows = slice(at * share, (at + 1) * share)
        total[rows] = acc_ref[rows] + lax.dot_general(
            sw_ref[:, rows], cot_ref[...], turned, preferred_element_type=f32
        )
    core, place = meta_ref[1], meta_ref[2]
    for shift, ref in enumerate((own_ref, one_ref, two_ref, three_ref)):
        chunk = lax.rem(place + shift, 4)
        for k in range(4):
            start = jnp.where(core == 0, chunk * share + k * piece, k * share + chunk * piece)
            value = total[pl.ds(pl.multiple_of(start, piece), piece)]
            ref[k * piece : (k + 1) * piece] = value.astype(ref.dtype)


def first_sum_kernel(meta_ref, a_ref, b_ref, c_ref, d_ref, own_ref, one_ref, two_ref, three_ref):
    piece = own_ref.shape[0]
    for shift, ref in enumerate((own_ref, one_ref, two_ref, three_ref)):
        rows = pl.ds(pl.multiple_of(lax.rem(meta_ref[3] + shift, 4) * piece, piece), piece)
        value = (a_ref[rows] + c_ref[rows].astype(f32)) + (b_ref[rows].astype(f32) + d_ref[rows].astype(f32))
        ref[...] = value.astype(ref.dtype)


def place_kernel(scale, meta_ref, *refs):
    out_ref = refs[-1]
    piece, width = refs[0].shape
    for side in range(2):
        core = meta_ref[1] if side == 0 else 1 - meta_ref[1]
        place = meta_ref[4] if side == 0 else meta_ref[5]
        cols = pl.ds(pl.multiple_of(core * width, width), width)
        for shift in range(4):
            rows = pl.ds(pl.multiple_of(lax.rem(place + 4 - shift, 4) * piece, piece), piece)
            out_ref[rows, cols] = refs[side * 4 + shift][...] * scale


def whole(shape):
    return pl.BlockSpec(shape, lambda *i: (0,) * len(shape))


SMEM = pl.BlockSpec(memory_space=pltpu.SMEM)
VMEM = pl.BlockSpec(memory_space=pltpu.VMEM)


def params(mebibytes):
    return pltpu.CompilerParams(vmem_limit_bytes=mebibytes << 20)


def cost(flops, moved):
    return pl.CostEstimate(flops=flops, bytes_accessed=moved, transcendentals=0)


def forward(lane, meta, lengths, flat, before, after, split, split_t, spec, gain, bias, interpret=False):
    total, channels = flat.shape
    lanes = lengths.shape[0]
    length = total // lanes
    blocks = length // ROWS
    per = ROWS // EDGE
    last = total // EDGE - 1
    at = lane * blocks
    row = pl.BlockSpec((ROWS, channels), lambda i: (i, 0))
    halo = pl.BlockSpec((EDGE, channels), lambda i: (lane, 0))
    return pl.pallas_call(
        functools.partial(forward_kernel, lane, blocks),
        grid=(blocks,),
        in_specs=[
            SMEM,
            SMEM,
            pl.BlockSpec((ROWS, channels), lambda i: (i + at, 0)),
            pl.BlockSpec((EDGE, channels), lambda i: (jnp.maximum((i + at) * per - 1, 0), 0)),
            pl.BlockSpec((EDGE, channels), lambda i: (jnp.minimum((i + at) * per + per, last), 0)),
            halo,
            halo,
            whole(split.shape),
            whole(split_t.shape),
            whole(spec.shape),
            whole((1, channels)),
            whole((1, channels)),
        ],
        out_specs=[
            row,
            row,
            pl.BlockSpec((ROWS, 128), lambda i: (i, 0)),
            pl.BlockSpec((POINTS, channels), lambda i: (i, 0)),
        ],
        out_shape=[
            jax.ShapeDtypeStruct((length, channels), bf16),
            jax.ShapeDtypeStruct((length, channels), f32),
            jax.ShapeDtypeStruct((length, 128), f32),
            jax.ShapeDtypeStruct((blocks * POINTS, channels), bf16),
        ],
        scratch_shapes=[pltpu.VMEM((WINDOW, channels), bf16), pltpu.VMEM((ROWS, channels), f32)],
        compiler_params=params(40),
        cost_estimate=cost(length * channels * 2000, length * channels * 12),
        interpret=interpret,
        name=f"conv_norm_swish_{lane}",
    )(meta, lengths, flat, flat, flat, before, after, split, split_t, spec, gain, bias)


def backward(lane, meta, lengths, cot, sw, normed, istd, xhat, w, split, split_t, spec, gather, gain, bias,
             interpret=False):
    total, channels = sw.shape
    blocks = total // ROWS
    at = lane * blocks
    row = pl.BlockSpec((ROWS, channels), lambda i: (i, 0))
    return pl.pallas_call(
        functools.partial(backward_kernel, lane, blocks),
        grid=(blocks,),
        in_specs=[
            SMEM,
            SMEM,
            pl.BlockSpec((ROWS, channels), lambda i: (i + at, 0)),
            row,
            row,
            pl.BlockSpec((ROWS, 128), lambda i: (i, 0)),
            pl.BlockSpec((POINTS, channels), lambda i: (i, 0)),
            whole(w.shape),
            whole(split.shape),
            whole(split_t.shape),
            whole(spec.shape),
            whole(gather.shape),
            whole((1, channels)),
            whole((1, channels)),
        ],
        out_specs=[row, whole((total, channels)), whole((2 * EDGE, channels)), whole((40, channels))],
        out_shape=[
            jax.ShapeDtypeStruct((total, channels), bf16),
            jax.ShapeDtypeStruct((total, channels), bf16),
            jax.ShapeDtypeStruct((2 * EDGE, channels), bf16),
            jax.ShapeDtypeStruct((40, channels), f32),
        ],
        scratch_shapes=[
            pltpu.VMEM((ROWS, channels), f32),
            pltpu.VMEM((2 * ROWS, channels), bf16),
            pltpu.VMEM((3 * BINS, channels), f32),
            pltpu.VMEM((16, channels), f32),
            pltpu.VMEM((EDGE, channels), f32),
            pltpu.VMEM((EDGE, channels), f32),
        ],
        compiler_params=params(56),
        cost_estimate=cost(total * channels * 8000, total * channels * 20),
        interpret=interpret,
        name=f"backward_{lane}",
    )(meta, lengths, cot, sw, normed, istd, xhat, w, split, split_t, spec, gather, gain, bias)


def outer(meta, sw0, sw1, sw2, cot, other):
    rows, channels = sw0.shape
    width = channels // 2
    share = channels // 4
    left = pl.BlockSpec((rows, share), lambda i, meta: (0, i))
    return pl.pallas_call(
        outer_kernel,
        grid_spec=pltpu.PrefetchScalarGridSpec(
            num_scalar_prefetch=1,
            grid=(4,),
            in_specs=[
                left,
                left,
                left,
                pl.BlockSpec((2 * rows, width), lambda i, meta: (0, meta[1])),
                pl.BlockSpec((rows, width), lambda i, meta: (0, meta[1])),
            ],
            out_specs=pl.BlockSpec((share, width), lambda i, meta: (i, 0)),
        ),
        out_shape=jax.ShapeDtypeStruct((channels, width), f32),
        compiler_params=params(40),
        cost_estimate=cost(6 * rows * channels * width, 10 * rows * channels),
        name="outer_most",
    )(meta, sw0, sw1, sw2, cot, other)


def last_outer(meta, acc, sw, cot):
    rows, channels = sw.shape
    width, share = channels // 2, channels // 4
    return pl.pallas_call(
        last_outer_kernel,
        grid_spec=pltpu.PrefetchScalarGridSpec(
            num_scalar_prefetch=1,
            grid=(1,),
            in_specs=[
                whole(acc.shape),
                whole(sw.shape),
                pl.BlockSpec((rows, width), lambda i, meta: (1, meta[1])),
            ],
            out_specs=[whole((share, width))] * 4,
            scratch_shapes=[pltpu.VMEM(acc.shape, f32)],
        ),
        out_shape=[jax.ShapeDtypeStruct((share, width), d) for d in (f32, bf16, bf16, bf16)],
        compiler_params=params(40),
        cost_estimate=cost(2 * rows * channels * width, 10 * rows * channels),
        name="outer_last",
    )(meta, acc, sw, cot)


def first_sum(meta, parts):
    share, width = parts[0].shape
    piece = share // 4
    return pl.pallas_call(
        first_sum_kernel,
        in_specs=[SMEM] + [VMEM] * 4,
        out_specs=[VMEM] * 4,
        out_shape=[jax.ShapeDtypeStruct((piece, width), d) for d in (f32, bf16, bf16, bf16)],
        compiler_params=params(32),
        name="sum_first",
    )(meta, *parts)


def place(meta, pieces, scale):
    piece, width = pieces[0].shape
    return pl.pallas_call(
        functools.partial(place_kernel, scale),
        in_specs=[SMEM] + [VMEM] * 8,
        out_specs=VMEM,
        out_shape=jax.ShapeDtypeStruct((4 * piece, 2 * width), f32),
        compiler_params=params(32),
        name="place",
    )(meta, *pieces)


def shifts(size):
    up = [(i, i + 1) for i in range(size - 1)]
    return up, [(j, i) for i, j in up]


EVERY = ("dp", "seq")


def along(axes, shift):
    pairs = []
    for device in range(128):
        where = {"y": device % 4, "c": device // 4 % 2, "x": device // 8 % 4, "z": device // 32}
        axis = axes[where["c"]]
        moved = dict(where)
        moved[axis] = (where[axis] + shift) % (2 if axis == "c" else 4)
        pairs.append((device, ((moved["z"] * 4 + moved["x"]) * 2 + moved["c"]) * 4 + moved["y"]))
    return pairs


def swap(value):
    return lax.ppermute(value, EVERY, along("cc", 1))


def spread(values, axes):
    return [lax.ppermute(value, EVERY, along(axes, s + 1)) for s, value in enumerate(values)]


def four(own, one, two, three):
    own, one, two, three = (v.astype(f32) for v in (own, one, two, three))
    return (own + two) + (one + three)


def all_four(value, axes):
    return four(value, *spread([value] * 3, axes))


def local(glu_out, lengths, kernel, norm_gain, norm_bias, w_out, cotangent, interpret=False):
    lanes, length, channels = glu_out.shape
    seq_count = lax.axis_size("seq")
    norm_scale = 1.0 / math.sqrt(lanes * lax.axis_size("dp") * length * seq_count)
    y = lax.axis_index("seq")
    dp = lax.axis_index("dp")
    core, x, z = lax.rem(dp, 2), lax.rem(lax.div(dp, 2), 4), lax.div(dp, 8)
    first = core == 0
    meta = jnp.stack(
        [
            y * length,
            core,
            jnp.where(first, y, z),
            jnp.where(first, x, y),
            jnp.where(first, x, z),
            jnp.where(first, z, x),
        ]
    ).astype(jnp.int32)
    up, down = shifts(seq_count)
    before = lax.ppermute(glu_out[:, length - EDGE :], "seq", up).reshape(lanes * EDGE, channels)
    after = lax.ppermute(glu_out[:, :EDGE], "seq", down).reshape(lanes * EDGE, channels)
    cot = cotangent.reshape(-1, channels)
    cot_other = swap(cot)
    split, split_t, wide, deep = (jnp.asarray(t) for t in tables())
    spec = pl.pallas_call(
        spectrum_kernel,
        out_shape=jax.ShapeDtypeStruct((3 * BINS, channels), f32),
        compiler_params=params(32),
        interpret=interpret,
        name="spectrum",
    )(wide, jnp.pad(kernel, ((0, 32 - TAPS), (0, 0))))
    gain, bias = norm_gain.reshape(1, channels), norm_bias.reshape(1, channels)
    flat = glu_out.reshape(lanes * length, channels)
    ahead = [
        forward(lane, meta, lengths, flat, before, after, split, split_t, spec, gain, bias, interpret=interpret)
        for lane in range(lanes)
    ]
    swished = [a[0] for a in ahead]
    other = [swap(s) for s in swished]
    acc = outer(meta, swished[0], swished[1], other[0], cot, cot_other)
    parts = last_outer(meta, acc, other[1], cot_other)
    parts = [parts[0]] + spread(parts[1:], "yz")
    back = [
        backward(lane, meta, lengths, cot, *ahead[lane], w_out, split, split_t, spec, deep, gain, bias,
                 interpret=interpret)
        for lane in range(lanes)
    ]
    pieces = first_sum(meta, parts)
    pieces = [pieces[0]] + spread(pieces[1:], "xy")
    piece = all_four(four(*pieces).astype(bf16), "zx")
    pieces = [piece] + spread([piece] * 3, "xz")
    grad_w = place(meta, pieces + [swap(p) for p in pieces], norm_scale)

    layer = jnp.stack([b[0] for b in back])
    gi = jnp.stack([b[1] for b in back])
    edge = jnp.stack([b[2] for b in back])
    from_after = lax.ppermute(edge[:, :EDGE], "seq", down)
    from_before = lax.ppermute(edge[:, EDGE:], "seq", up)
    gi = gi.at[:, :EDGE].add(from_before).at[:, length - EDGE :].add(from_after)

    small = back[0][3] + back[1][3]
    small = small + swap(small)
    half = channels // 2
    small = lax.dynamic_slice_in_dim(small, core * half, half, 1)
    for axes in ("yz", "xy", "zx"):
        small = all_four(small, axes)
    small = small * norm_scale
    away = swap(small)
    small = jnp.concatenate([jnp.where(first, small, away), jnp.where(first, away, small)], axis=1)
    return (layer, gi, grad_w, small[:TAPS], small[32], small[33])


def solution(mesh):
    in_specs = (P("dp", "seq", None), P("dp", None), P(), P(), P(), P(), P("dp", "seq", None))
    out_specs = (P("dp", "seq", None), P("dp", "seq", None), P("seq", None), P(), P(), P())
    return jax.shard_map(local, mesh=mesh, in_specs=in_specs, out_specs=out_specs, check_vma=False)
```

```python
import functools
import math

import jax
import jax.numpy as jnp
import numpy as np
from jax import lax
from jax.experimental import pallas as pl
from jax.experimental.pallas import tpu as pltpu
from jax.sharding import PartitionSpec as P

EPSILON = 1e-05
TAPS = 31
HALF = TAPS // 2
ROWS = 128
EDGE = 16
WINDOW = ROWS + 2 * EDGE
POINTS = 256
BINS = POINTS // 2
f32, bf16 = jnp.float32, jnp.bfloat16


def tables():
    place = np.arange(POINTS)
    bins = np.arange(BINS)[:, None]
    cosines = math.sqrt(2.0 / POINTS) * np.cos(2 * np.pi * ((bins * place) % POINTS) / POINTS)
    sines = math.sqrt(2.0 / POINTS) * np.sin(2 * np.pi * ((bins * place) % POINTS) / POINTS)
    cosines[0] = 1.0 / math.sqrt(POINTS)
    sines[0] = (1.0 - 2.0 * (place % 2)) / math.sqrt(POINTS)
    basis = np.concatenate([cosines, sines])
    high = basis.astype(jnp.bfloat16)
    low = (basis - high.astype(np.float64)).astype(jnp.bfloat16)
    split = np.concatenate([high, low])
    lags = np.arange(TAPS) - HALF
    turn = 2 * np.pi * ((bins * lags) % POINTS) / POINTS
    real, imag = np.cos(turn), np.sin(turn)
    other = real.copy()
    other[0] = 1.0 - 2.0 * (np.abs(lags) % 2)
    spectrum = np.concatenate([real, imag, other]).astype(np.float32)
    gather = np.concatenate([real, other, -imag]).astype(np.float32)
    wide, deep = np.zeros((3 * BINS, 32), np.float32), np.zeros((32, 3 * BINS), np.float32)
    wide[:, :TAPS], deep[:TAPS] = spectrum, gather.T
    return split, np.ascontiguousarray(split.T), wide, deep


def gapped(lengths_ref, lane, first, shape, dim, skip):
    row = lax.broadcasted_iota(jnp.int32, shape, dim) + skip
    frame = first + row
    place, end = row, 0
    for utter in range(lengths_ref.shape[1] - 1):
        end = end + lengths_ref[lane, utter]
        place = place + jnp.where(frame >= end, jnp.where(first < end, HALF, 0), 0)
    return place


def chosen_columns(split, place):
    count = place.shape[1]
    one_hot = (lax.broadcasted_iota(jnp.int32, (POINTS, count), 0) == place).astype(f32).astype(bf16)
    return jnp.dot(split, one_hot, preferred_element_type=f32).astype(bf16)


def chosen_rows(split_t, place):
    count = place.shape[0]
    one_hot = (lax.broadcasted_iota(jnp.int32, (count, POINTS), 1) == place).astype(f32).astype(bf16)
    return jnp.dot(one_hot, split_t, preferred_element_type=f32).astype(bf16)


def dot(a, b):
    return jnp.dot(a, b, preferred_element_type=f32)


def sigmoid(a):
    return 0.5 * jnp.tanh(0.5 * a) + 0.5


def forward_kernel(lane, blocks, meta_ref, lengths_ref, x_ref, before_ref, after_ref, split_ref, split_t_ref, spec_ref,
                   sw_ref, turned_ref, normed_ref, istd_ref, xhat_ref, win, conv):
    block = pl.program_id(0)
    total, channels = x_ref.shape
    first = meta_ref[0] + block * ROWS - EDGE
    start = (lane * blocks + block) * ROWS
    own = pl.ds(pl.multiple_of(block * ROWS, ROWS), ROWS)
    win[EDGE : EDGE + ROWS] = x_ref[pl.ds(pl.multiple_of(start, ROWS), ROWS)]
    halo = slice(lane * EDGE, (lane + 1) * EDGE)
    ahead = x_ref[pl.ds(pl.multiple_of(jnp.maximum(start - EDGE, 0), EDGE), EDGE)]
    behind = x_ref[pl.ds(pl.multiple_of(jnp.minimum(start + ROWS, total - EDGE), EDGE), EDGE)]
    win[:EDGE] = jnp.where(block == 0, before_ref[halo], ahead)
    win[EDGE + ROWS :] = jnp.where(block == blocks - 1, after_ref[halo], behind)
    into = chosen_columns(split_ref[...], gapped(lengths_ref, lane, first, (1, WINDOW), 1, 0))
    back = chosen_rows(split_t_ref[...], gapped(lengths_ref, lane, first, (ROWS, 1), 0, EDGE))
    spectra = pl.ds(pl.multiple_of(block * POINTS, POINTS), POINTS)
    width = 512
    for at in range(0, channels, width):
        cols = slice(at, at + width)
        rows = win[:, cols]
        xhat = dot(into[:POINTS], rows) + dot(into[POINTS:], rows)
        xhat_ref[spectra, cols] = xhat.astype(bf16)
        real, imag = xhat[:BINS], xhat[BINS:]
        p, q, other = spec_ref[:BINS, cols], spec_ref[BINS:POINTS, cols], spec_ref[POINTS : 3 * BINS, cols]
        zed = jnp.concatenate([real * p + imag * q, imag * other - real * q]).astype(bf16)
        conv[:, cols] = dot(back[:, :POINTS], zed) + dot(back[:, POINTS:], zed)
    gain, bias = spec_ref[3 * BINS : 3 * BINS + 1], spec_ref[3 * BINS + 1 : 3 * BINS + 2]
    strip = 16
    for at in range(0, ROWS, strip):
        rows = slice(at, at + strip)
        place = pl.ds(pl.multiple_of(block * ROWS + at, strip), strip)
        value = conv[rows]
        centred = value - jnp.sum(value, axis=1, keepdims=True) * (1.0 / channels)
        variance = jnp.sum(centred * centred, axis=1, keepdims=True) * (1.0 / channels)
        inv_std = lax.rsqrt(variance + EPSILON)
        normed = centred * inv_std
        affine = normed * gain + bias
        sw_ref[place] = (affine * sigmoid(affine)).astype(bf16)
        normed_ref[place] = normed
        istd_ref[place] = jnp.broadcast_to(inv_std, (strip, istd_ref.shape[1]))
    turned_ref[:, own] = sw_ref[own].T


def backward_kernel(lane, blocks, meta_ref, lengths_ref, cot_ref, sw_ref, normed_ref, istd_ref, xhat_ref, w_ref,
                    split_ref, split_t_ref, spec_ref, gather_ref, carry_ref, *rest):
    layer_ref, gi_ref, edge_ref, small_ref, gs, g, acc, sums, pending, tail = rest[-10:]
    block = pl.program_id(0)
    channels = cot_ref.shape[1]
    length = blocks * ROWS
    first = meta_ref[0] + block * ROWS - EDGE
    is_first, is_last = block == 0, block == blocks - 1

    @pl.when(is_first)
    def _():
        acc[...] = jnp.zeros_like(acc)
        sums[...] = jnp.zeros_like(sums)
        pending[...] = jnp.zeros_like(pending)
        tail[...] = jnp.zeros_like(tail)
        gs[...] = lax.dot_general(
            cot_ref[lane * length : (lane + 1) * length],
            w_ref[...],
            (((1,), (1,)), ((), ())),
            preferred_element_type=f32,
        )

    own = pl.ds(pl.multiple_of(block * ROWS, ROWS), ROWS)
    layer_ref[...] = dot(sw_ref[own], w_ref[...]).astype(bf16)
    gain, bias = spec_ref[3 * BINS : 3 * BINS + 1], spec_ref[3 * BINS + 1 : 3 * BINS + 2]
    strip = 16
    for at in range(0, ROWS, strip):
        place = pl.ds(pl.multiple_of(block * ROWS + at, strip), strip)
        normed = normed_ref[place]
        affine = normed * gain + bias
        gate = sigmoid(affine)
        grad = gs[place] * gate * (1.0 + affine * (1.0 - gate))
        prod = grad * normed
        sums[:8] += prod[:8] + prod[8:]
        sums[8:] += grad[:8] + grad[8:]
        grad_normed = grad * gain
        mean = jnp.sum(grad_normed, axis=1, keepdims=True) * (1.0 / channels)
        along = jnp.sum(grad_normed * normed, axis=1, keepdims=True) * (1.0 / channels)
        out = (istd_ref[place, :1] * (grad_normed - mean - normed * along)).astype(bf16)
        g[at : at + strip] = out
        g[ROWS + at : ROWS + at + strip] = out
    into = chosen_columns(split_ref[...], gapped(lengths_ref, lane, first, (1, ROWS), 1, EDGE))
    into = jnp.concatenate([into[:POINTS], into[POINTS:]], axis=1)
    back = chosen_rows(split_t_ref[...], gapped(lengths_ref, lane, first, (WINDOW, 1), 0, 0))
    base = pl.multiple_of(block * ROWS, ROWS)
    early = pl.ds(pl.multiple_of(jnp.maximum(base - EDGE, 0), EDGE), EDGE)
    cosines = pl.ds(pl.multiple_of(block * POINTS, POINTS), BINS)
    sines = pl.ds(pl.multiple_of(block * POINTS + BINS, BINS), BINS)
    width = 256
    for at in range(0, channels, width):
        cols = slice(at, at + width)
        ghat = dot(into, g[:, cols])
        cg, sg = ghat[:BINS], ghat[BINS:]
        cx, sx = xhat_ref[cosines, cols].astype(f32), xhat_ref[sines, cols].astype(f32)
        acc[:BINS, cols] += cg * cx
        acc[BINS:POINTS, cols] += sg * sx
        acc[POINTS:, cols] += sg * cx - cg * sx
        p, q, other = spec_ref[:BINS, cols], spec_ref[BINS:POINTS, cols], spec_ref[POINTS : 3 * BINS, cols]
        vee = jnp.concatenate([cg * p - sg * q, sg * other + cg * q]).astype(bf16)
        part = dot(back[:, :POINTS], vee) + dot(back[:, POINTS:], vee)
        head, out = part[:EDGE], part[EDGE : EDGE + ROWS]
        gi_ref[early, cols] = (pending[:, cols] + head).astype(bf16)
        gi_ref[pl.ds(base, EDGE), cols] = (out[:EDGE] + tail[:, cols]).astype(bf16)
        gi_ref[pl.ds(base + EDGE, ROWS - EDGE), cols] = out[EDGE:].astype(bf16)
        edge_ref[:EDGE, cols] = jnp.where(is_first, head.astype(bf16), edge_ref[:EDGE, cols])
        edge_ref[EDGE:, cols] = part[EDGE + ROWS :].astype(bf16)
        pending[:, cols] = out[ROWS - EDGE :]
        tail[:, cols] = part[EDGE + ROWS :]

    @pl.when(is_last)
    def _():
        table_high, table_low = halves(gather_ref[...])
        wide = 512
        for at in range(0, channels, wide):
            cols = slice(at, at + wide)
            high, low = halves(acc[:, cols])
            value = dot(table_high, high) + dot(table_low, high) + dot(table_high, low)
            small_ref[:32, cols] = value + carry_ref[:32, cols]
        prod, grad = sums[:8], sums[8:]
        small_ref[32:40] = carry_ref[32:40] + jnp.concatenate(
            [
                jnp.sum(prod, axis=0, keepdims=True),
                jnp.sum(grad, axis=0, keepdims=True),
                jnp.zeros((6, channels), f32),
            ]
        )


def halves(value):
    high = value.astype(bf16)
    return high, (value - high.astype(f32)).astype(bf16)


def spectrum_kernel(table_ref, kernel_ref, gain_ref, bias_ref, spec_ref):
    channels = kernel_ref.shape[1]
    table_high, table_low = halves(table_ref[...])
    taps = jnp.concatenate([kernel_ref[...], jnp.zeros((32 - TAPS, channels), f32)])
    high, low = halves(taps)
    spec_ref[: 3 * BINS] = dot(table_high, high) + dot(table_low, high) + dot(table_high, low)
    spec_ref[3 * BINS :] = jnp.concatenate(
        [gain_ref[...].reshape(1, channels), bias_ref[...].reshape(1, channels), jnp.zeros((6, channels), f32)]
    )


def outer_kernel(meta_ref, sw0_ref, sw1_ref, sw2_ref, cot_ref, other_ref, acc_ref):
    rows = sw0_ref.shape[1]
    share = acc_ref.shape[0] // 4
    cols = pl.ds(pl.multiple_of(meta_ref[1] * acc_ref.shape[1], acc_ref.shape[1]), acc_ref.shape[1])
    for at in range(4):
        part = slice(at * share, (at + 1) * share)
        acc_ref[part] = (
            dot(sw0_ref[part], cot_ref[:rows, cols])
            + dot(sw1_ref[part], cot_ref[rows:, cols])
            + dot(sw2_ref[part], other_ref[:rows, cols])
        )


def last_outer_kernel(meta_ref, acc_ref, sw_ref, cot_ref, own_ref, one_ref, two_ref, three_ref, total):
    share, width = acc_ref.shape[0] // 4, acc_ref.shape[1]
    piece = share // 4
    rows = sw_ref.shape[1]
    cols = pl.ds(pl.multiple_of(meta_ref[1] * width, width), width)
    for at in range(4):
        part = slice(at * share, (at + 1) * share)
        total[part] = acc_ref[part] + dot(sw_ref[part], cot_ref[rows:, cols])
    core, place = meta_ref[1], meta_ref[2]
    for shift, ref in enumerate((own_ref, one_ref, two_ref, three_ref)):
        chunk = lax.rem(place + shift, 4)
        for k in range(4):
            start = jnp.where(core == 0, chunk * share + k * piece, k * share + chunk * piece)
            value = total[pl.ds(pl.multiple_of(start, piece), piece)]
            ref[k * piece : (k + 1) * piece] = value.astype(ref.dtype)


def first_sum_kernel(meta_ref, a_ref, b_ref, c_ref, d_ref, own_ref, one_ref, two_ref, three_ref):
    piece = own_ref.shape[0]
    for shift, ref in enumerate((own_ref, one_ref, two_ref, three_ref)):
        rows = pl.ds(pl.multiple_of(lax.rem(meta_ref[3] + shift, 4) * piece, piece), piece)
        value = (a_ref[rows] + c_ref[rows].astype(f32)) + (b_ref[rows].astype(f32) + d_ref[rows].astype(f32))
        ref[...] = value.astype(ref.dtype)


def place_kernel(scale, meta_ref, *refs):
    out_ref = refs[-1]
    width = refs[0].shape[1]
    piece = out_ref.shape[0] // 4
    for side in range(2):
        core = meta_ref[1] if side == 0 else 1 - meta_ref[1]
        place = meta_ref[4] if side == 0 else meta_ref[5]
        cols = pl.ds(pl.multiple_of(core * width, width), width)
        for shift in range(4):
            rows = pl.ds(pl.multiple_of(lax.rem(place + 4 - shift, 4) * piece, piece), piece)
            out_ref[rows, cols] = refs[side * 4 + shift][:piece] * scale


def place_small_kernel(scale, meta_ref, own_ref, away_ref, taps_ref, gain_ref, bias_ref):
    first = meta_ref[1] == 0
    width = own_ref.shape[1]
    own, away = own_ref[...] * scale, away_ref[...] * scale
    for side in range(2):
        cols = slice(side * width, (side + 1) * width)
        value = jnp.where(first == (side == 0), own, away)
        taps_ref[:, cols] = value[:TAPS]
        gain_ref[cols] = value[32]
        bias_ref[cols] = value[33]


def whole(shape):
    return pl.BlockSpec(shape, lambda *i: (0,) * len(shape))


SMEM = pl.BlockSpec(memory_space=pltpu.SMEM)
VMEM = pl.BlockSpec(memory_space=pltpu.VMEM)


def params(mebibytes):
    return pltpu.CompilerParams(vmem_limit_bytes=mebibytes << 20)


def cost(flops, moved):
    return pl.CostEstimate(flops=flops, bytes_accessed=moved, transcendentals=0)


def near(*arrays):
    return [pltpu.with_memory_space_constraint(a, pltpu.VMEM) for a in arrays]


def forward(lane, meta, lengths, flat, before, after, split, split_t, spec, interpret=False):
    total, channels = flat.shape
    lanes = lengths.shape[0]
    length = total // lanes
    blocks = length // ROWS
    return pl.pallas_call(
        functools.partial(forward_kernel, lane, blocks),
        grid=(blocks,),
        in_specs=[SMEM, SMEM] + [VMEM] * 6,
        out_specs=[VMEM] * 5,
        out_shape=[
            pltpu.VMEM((length, channels), bf16),
            pltpu.VMEM((channels, length), bf16),
            pltpu.VMEM((length, channels), f32),
            pltpu.VMEM((length, 128), f32),
            pltpu.VMEM((blocks * POINTS, channels), bf16),
        ],
        scratch_shapes=[pltpu.VMEM((WINDOW, channels), bf16), pltpu.VMEM((ROWS, channels), f32)],
        compiler_params=params(12),
        cost_estimate=cost(length * channels * 2000, length * channels * 12),
        interpret=interpret,
        name=f"conv_norm_swish_{lane}",
    )(meta, lengths, *near(flat, before, after, split, split_t, spec))


def backward(lane, meta, lengths, cot, sw, normed, istd, xhat, w, split, split_t, spec, gather, carry, layer, gi,
             interpret=False):
    total, channels = cot.shape
    length = sw.shape[0]
    blocks = length // ROWS
    at = lane * blocks
    kept = [] if layer is None else [layer, gi]
    return pl.pallas_call(
        functools.partial(backward_kernel, lane, blocks),
        grid=(blocks,),
        in_specs=[SMEM, SMEM] + [VMEM] * 11 + [pl.BlockSpec(memory_space=pl.ANY)] * len(kept),
        out_specs=[
            pl.BlockSpec((ROWS, channels), lambda i: (i + at, 0)),
            pl.BlockSpec((length, channels), lambda i: (lane, 0)),
            VMEM,
            VMEM,
        ],
        out_shape=[
            jax.ShapeDtypeStruct((total, channels), bf16),
            jax.ShapeDtypeStruct((total, channels), bf16),
            pltpu.VMEM((2 * EDGE, channels), bf16),
            pltpu.VMEM((40, channels), f32),
        ],
        scratch_shapes=[
            pltpu.VMEM((length, channels), f32),
            pltpu.VMEM((2 * ROWS, channels), bf16),
            pltpu.VMEM((3 * BINS, channels), f32),
            pltpu.VMEM((16, channels), f32),
            pltpu.VMEM((EDGE, channels), f32),
            pltpu.VMEM((EDGE, channels), f32),
        ],
        input_output_aliases={13: 0, 14: 1} if kept else {},
        compiler_params=params(20),
        cost_estimate=cost(length * channels * 8000, length * channels * 20),
        interpret=interpret,
        name=f"backward_{lane}",
    )(meta, lengths, *near(cot, sw, normed, istd, xhat, w, split, split_t, spec, gather, carry), *kept)


def outer(meta, sw0, sw1, sw2, cot, other, interpret=False):
    channels, rows = sw0.shape
    width = channels // 2
    return pl.pallas_call(
        outer_kernel,
        in_specs=[SMEM] + [VMEM] * 5,
        out_specs=VMEM,
        out_shape=pltpu.VMEM((channels, width), f32),
        compiler_params=params(12),
        cost_estimate=cost(6 * rows * channels * width, 10 * rows * channels),
        interpret=interpret,
        name="outer_most",
    )(meta, *near(sw0, sw1, sw2, cot, other))


def last_outer(meta, acc, sw, cot, interpret=False):
    channels, rows = sw.shape
    width, share = channels // 2, channels // 4
    return pl.pallas_call(
        last_outer_kernel,
        in_specs=[SMEM] + [VMEM] * 3,
        out_specs=[VMEM] * 4,
        out_shape=[pltpu.VMEM((share, width), d) for d in (f32, bf16, bf16, bf16)],
        scratch_shapes=[pltpu.VMEM(acc.shape, f32)],
        compiler_params=params(12),
        cost_estimate=cost(2 * rows * channels * width, 10 * rows * channels),
        interpret=interpret,
        name="outer_last",
    )(meta, *near(acc, sw, cot))


def first_sum(meta, parts):
    share, width = parts[0].shape
    piece = share // 4
    return pl.pallas_call(
        first_sum_kernel,
        in_specs=[SMEM] + [VMEM] * 4,
        out_specs=[VMEM] * 4,
        out_shape=[pltpu.VMEM((piece, width), d) for d in (f32, bf16, bf16, bf16)],
        compiler_params=params(12),
        name="sum_first",
    )(meta, *near(*parts))


def place(meta, pieces, share, scale):
    width = pieces[0].shape[1]
    return pl.pallas_call(
        functools.partial(place_kernel, scale),
        in_specs=[SMEM] + [VMEM] * 8,
        out_specs=VMEM,
        out_shape=jax.ShapeDtypeStruct((share, 2 * width), f32),
        compiler_params=params(12),
        name="place",
    )(meta, *near(*pieces))


def place_small(meta, own, away, scale):
    width = own.shape[1]
    return pl.pallas_call(
        functools.partial(place_small_kernel, scale),
        in_specs=[SMEM] + [VMEM] * 2,
        out_specs=[VMEM] * 3,
        out_shape=[
            jax.ShapeDtypeStruct((TAPS, 2 * width), f32),
            jax.ShapeDtypeStruct((2 * width,), f32),
            jax.ShapeDtypeStruct((2 * width,), f32),
        ],
        compiler_params=params(12),
        name="place_small",
    )(meta, own, away)


def shifts(size):
    up = [(i, i + 1) for i in range(size - 1)]
    return up, [(j, i) for i, j in up]


EVERY = ("dp", "seq")


def along(axes, shift):
    pairs = []
    for device in range(128):
        where = {"y": device % 4, "c": device // 4 % 2, "x": device // 8 % 4, "z": device // 32}
        axis = axes[where["c"]]
        moved = dict(where)
        moved[axis] = (where[axis] + shift) % (2 if axis == "c" else 4)
        pairs.append((device, ((moved["z"] * 4 + moved["x"]) * 2 + moved["c"]) * 4 + moved["y"]))
    return pairs


def swap(value):
    return lax.ppermute(value, EVERY, along("cc", 1))


def spread(values, axes):
    return [lax.ppermute(value, EVERY, along(axes, s + 1)) for s, value in enumerate(values)]


def four(own, one, two, three):
    own, one, two, three = (v.astype(f32) for v in (own, one, two, three))
    return (own + two) + (one + three)


def all_four(value, axes):
    return four(value, *spread([value] * 3, axes))


def both(value):
    return jnp.concatenate(halves(value))


def joined(value):
    rows = value.shape[0] // 2
    return value[:rows].astype(f32) + value[rows:].astype(f32)


def local(glu_out, lengths, kernel, norm_gain, norm_bias, w_out, cotangent, interpret=False):
    lanes, length, channels = glu_out.shape
    seq_count = lax.axis_size("seq")
    norm_scale = 1.0 / math.sqrt(lanes * lax.axis_size("dp") * length * seq_count)
    y = lax.axis_index("seq")
    dp = lax.axis_index("dp")
    core, x, z = lax.rem(dp, 2), lax.rem(lax.div(dp, 2), 4), lax.div(dp, 8)
    first = core == 0
    meta = jnp.stack(
        [
            y * length,
            core,
            jnp.where(first, y, z),
            jnp.where(first, x, y),
            jnp.where(first, x, z),
            jnp.where(first, z, x),
        ]
    ).astype(jnp.int32)
    up, down = shifts(seq_count)
    before = lax.ppermute(glu_out[:, length - EDGE :], "seq", up).reshape(lanes * EDGE, channels)
    after = lax.ppermute(glu_out[:, :EDGE], "seq", down).reshape(lanes * EDGE, channels)
    cot = cotangent.reshape(-1, channels)
    split, split_t, wide, deep = (jnp.asarray(t) for t in tables())
    spec = pl.pallas_call(
        spectrum_kernel,
        in_specs=[VMEM] * 4,
        out_specs=VMEM,
        out_shape=pltpu.VMEM((3 * BINS + 8, channels), f32),
        compiler_params=params(12),
        interpret=interpret,
        name="spectrum",
    )(wide, kernel, norm_gain, norm_bias)
    flat = glu_out.reshape(lanes * length, channels)
    ahead = [
        forward(lane, meta, lengths, flat, before, after, split, split_t, spec, interpret=interpret)
        for lane in range(lanes)
    ]
    turned = [a[1] for a in ahead]
    share, half = channels // seq_count, channels // 2
    whole_slice = lax.axis_size("dp") == 32
    if whole_slice:
        cot_other = swap(cot)
        other = [swap(t) for t in turned]
        acc = outer(meta, turned[0], turned[1], other[0], cot, cot_other)
        parts = list(last_outer(meta, acc, other[1], cot_other))
        sent = spread(parts[1:], "yz")
        cot, parts[0] = lax.optimization_barrier((cot, parts[0]))
    else:
        grad_w = lax.psum(dot(jnp.concatenate(turned, axis=1), cot), "seq") * norm_scale
        grad_w = lax.dynamic_slice_in_dim(grad_w, y * share, share, 0)
    small, layer, gi, edges = jnp.zeros((40, channels), f32), None, None, []
    for lane in range(lanes):
        sw, _, normed, istd, xhat = ahead[lane]
        layer, gi, edge, small = backward(
            lane, meta, lengths, cot, sw, normed, istd, xhat, w_out, split, split_t, spec, deep, small, layer, gi,
            interpret=interpret,
        )
        edges.append(edge)
    heads = jnp.concatenate([e[:EDGE] for e in edges])
    tails = jnp.concatenate([e[EDGE:] for e in edges])
    if whole_slice:
        small = small + swap(small)
        small = both(lax.dynamic_slice_in_dim(small, core * half, half, 1))
        flat_small = jnp.concatenate([small[:40], small[40:]], axis=1)
        ways = [jnp.concatenate([tails, flat_small]), flat_small, jnp.concatenate([heads, flat_small])]
        one, two, three = spread(ways, "yy")
        count = lanes * EDGE
        before, after = one[:count], three[:count]

        def split_rows(v):
            return jnp.concatenate([v[:, :half], v[:, half:]])

        small = four(joined(small), *(joined(split_rows(v)) for v in (one[count:], two, three[count:])))
        pieces = first_sum(meta, [parts[0]] + sent)
        pieces = [pieces[0]] + spread(pieces[1:], "xy")
        piece = four(*pieces).astype(bf16)
        rows = piece.shape[0]
        sent = jnp.concatenate([piece, both(small)])
        got = [sent] + spread([sent] * 3, "zx")
        piece = four(*(v[:rows] for v in got))
        small = four(*(joined(v[rows:]) for v in got))
        sent = jnp.concatenate([piece, small])
        got = [sent] + spread([sent] * 3, "xz")
        small = four(*(v[rows:] for v in got))
        grad_w = place(meta, got + [swap(v[:rows]) for v in got], share, norm_scale)
        taps, gain, bias = place_small(meta, small, swap(small), norm_scale)
    else:
        before, after = lax.ppermute(tails, "seq", up), lax.ppermute(heads, "seq", down)
        small = lax.psum(small, "seq") * norm_scale
        taps, gain, bias = small[:TAPS], small[32], small[33]
    before = jnp.where(y == 0, 0.0, before.astype(f32)).astype(bf16).reshape(lanes, EDGE, channels)
    after = jnp.where(y == seq_count - 1, 0.0, after.astype(f32)).astype(bf16).reshape(lanes, EDGE, channels)
    gi = gi.reshape(lanes, length, channels)
    gi = gi.at[:, :EDGE].add(before).at[:, length - EDGE :].add(after)
    return (layer.reshape(lanes, length, channels), gi, grad_w, taps, gain, bias)


def solution(mesh):
    in_specs = (P("dp", "seq", None), P("dp", None), P(), P(), P(), P(), P("dp", "seq", None))
    out_specs = (P("dp", "seq", None), P("dp", "seq", None), P("seq", None), P(), P(), P())
    return jax.shard_map(local, mesh=mesh, in_specs=in_specs, out_specs=out_specs, check_vma=False)
```

```python
import functools
import math

import jax
import jax.numpy as jnp
import numpy as np
from jax import lax
from jax.experimental import pallas as pl
from jax.experimental.pallas import tpu as pltpu
from jax.sharding import PartitionSpec as P

EPSILON = 1e-05
TAPS = 31
HALF = TAPS // 2
ROWS = 128
EDGE = 16
WINDOW = ROWS + 2 * EDGE
POINTS = 256
BINS = POINTS // 2
f32, bf16 = jnp.float32, jnp.bfloat16


def tables():
    place = np.arange(POINTS)
    bins = np.arange(BINS)[:, None]
    cosines = math.sqrt(2.0 / POINTS) * np.cos(2 * np.pi * ((bins * place) % POINTS) / POINTS)
    sines = math.sqrt(2.0 / POINTS) * np.sin(2 * np.pi * ((bins * place) % POINTS) / POINTS)
    cosines[0] = 1.0 / math.sqrt(POINTS)
    sines[0] = (1.0 - 2.0 * (place % 2)) / math.sqrt(POINTS)
    basis = np.concatenate([cosines, sines])
    high = basis.astype(jnp.bfloat16)
    low = (basis - high.astype(np.float64)).astype(jnp.bfloat16)
    split = np.concatenate([high, low])
    lags = np.arange(TAPS) - HALF
    turn = 2 * np.pi * ((bins * lags) % POINTS) / POINTS
    real, imag = np.cos(turn), np.sin(turn)
    other = real.copy()
    other[0] = 1.0 - 2.0 * (np.abs(lags) % 2)
    spectrum = np.concatenate([real, imag, other]).astype(np.float32)
    gather = np.concatenate([real, other, -imag]).astype(np.float32)
    wide, deep = np.zeros((3 * BINS, 32), np.float32), np.zeros((32, 3 * BINS), np.float32)
    wide[:, :TAPS], deep[:TAPS] = spectrum, gather.T
    return split, np.ascontiguousarray(split.T), wide, deep


def gapped(lengths_ref, lane, first, shape, dim, skip):
    row = lax.broadcasted_iota(jnp.int32, shape, dim) + skip
    frame = first + row
    place, end = row, 0
    for utter in range(lengths_ref.shape[1] - 1):
        end = end + lengths_ref[lane, utter]
        place = place + jnp.where(frame >= end, jnp.where(first < end, HALF, 0), 0)
    return place


def chosen_columns(split, place):
    count = place.shape[1]
    one_hot = (lax.broadcasted_iota(jnp.int32, (POINTS, count), 0) == place).astype(f32).astype(bf16)
    return jnp.dot(split, one_hot, preferred_element_type=f32).astype(bf16)


def chosen_rows(split_t, place):
    count = place.shape[0]
    one_hot = (lax.broadcasted_iota(jnp.int32, (count, POINTS), 1) == place).astype(f32).astype(bf16)
    return jnp.dot(one_hot, split_t, preferred_element_type=f32).astype(bf16)


def dot(a, b):
    return jnp.dot(a, b, preferred_element_type=f32)


def sigmoid(a):
    return 0.5 * jnp.tanh(0.5 * a) + 0.5


def forward_kernel(tasks, blocks, meta_ref, lengths_ref, x_ref, before_ref, after_ref, split_ref, split_t_ref, spec_ref,
                   *rest):
    outs, (turned_ref, conv, sw, normed_all, istd, xhat_all, sems) = rest[-11:-7], rest[-7:]
    channels = x_ref.shape[1]
    gain, bias = spec_ref[3 * BINS : 3 * BINS + 1], spec_ref[3 * BINS + 1 : 3 * BINS + 2]
    strip, width = 16, channels // 2
    bases, copies = [], []
    for lane, block in tasks:
        first = meta_ref[0] + (block * ROWS - EDGE)
        into = chosen_columns(split_ref[...], gapped(lengths_ref, lane, first, (1, WINDOW), 1, 0))
        back = chosen_rows(split_t_ref[...], gapped(lengths_ref, lane, first, (ROWS, 1), 0, EDGE))
        bases.append((into, back))

    def transform(task):
        lane, block = tasks[task]
        into, back = bases[task]
        start = (lane * blocks + block) * ROWS
        halo = slice(lane * EDGE, (lane + 1) * EDGE)
        for at in range(0, channels, width):
            cols = slice(at, at + width)
            if block == 0:
                rows = jnp.concatenate([before_ref[halo, cols], x_ref[start : start + ROWS + EDGE, cols]])
            elif block == blocks - 1:
                rows = jnp.concatenate([x_ref[start - EDGE : start + ROWS, cols], after_ref[halo, cols]])
            else:
                rows = x_ref[start - EDGE : start + ROWS + EDGE, cols]
            xhat = dot(into[:POINTS], rows) + dot(into[POINTS:], rows)
            xhat_all[task * POINTS : (task + 1) * POINTS, cols] = xhat.astype(bf16)
            real, imag = xhat[:BINS], xhat[BINS:]
            p, q, other = spec_ref[:BINS, cols], spec_ref[BINS:POINTS, cols], spec_ref[POINTS : 3 * BINS, cols]
            zed = jnp.concatenate([real * p + imag * q, imag * other - real * q]).astype(bf16)
            conv[task, :, cols] = dot(back[:, :POINTS], zed) + dot(back[:, POINTS:], zed)

    def normalise(task):
        for at in range(0, ROWS, strip):
            place = slice(task * ROWS + at, task * ROWS + at + strip)
            value = conv[task, at : at + strip]
            centred = value - jnp.sum(value, axis=1, keepdims=True) * (1.0 / channels)
            variance = jnp.sum(centred * centred, axis=1, keepdims=True) * (1.0 / channels)
            inv_std = lax.rsqrt(variance + EPSILON)
            normed = centred * inv_std
            affine = normed * gain + bias
            sw[place] = (affine * sigmoid(affine)).astype(bf16)
            normed_all[place] = normed
            istd[place] = jnp.broadcast_to(inv_std, (strip, istd.shape[1]))
        own = slice(task * ROWS, (task + 1) * ROWS)
        turned_ref[:, own] = sw[own].T
        lane, block = tasks[task]
        for k, (source, target) in enumerate(zip((sw, normed_all, istd, xhat_all), outs)):
            size = POINTS if k == 3 else ROWS
            copy = pltpu.make_async_copy(
                source.at[pl.ds(task * size, size)],
                target.at[pl.ds((lane * blocks + block) * size, size)],
                sems.at[task, k],
            )
            copy.start()
            copies.append(copy)

    for task in range(len(tasks) + 1):
        if task < len(tasks):
            transform(task)
        if task > 0:
            normalise(task - 1)
    for copy in copies:
        copy.wait()


def backward_kernel(lane, blocks, meta_ref, lengths_ref, cot_ref, normed_ref, istd_ref, xhat_ref, w_ref,
                    split_ref, split_t_ref, spec_ref, gather_ref, carry_ref, *rest):
    gi_out, edge_ref, small_ref, gs, g, gi, sums, sems = rest[-8:]
    channels = cot_ref.shape[1]
    length = blocks * ROWS
    begin = lane * length
    gain, bias = spec_ref[3 * BINS : 3 * BINS + 1], spec_ref[3 * BINS + 1 : 3 * BINS + 2]
    strip, width = 16, channels // 3
    bases, copies = [], []
    for block in range(blocks):
        first = meta_ref[0] + (block * ROWS - EDGE)
        into = chosen_columns(split_ref[...], gapped(lengths_ref, lane, first, (1, ROWS), 1, EDGE))
        into = jnp.concatenate([into[:POINTS], into[POINTS:]], axis=1)
        back = chosen_rows(split_t_ref[...], gapped(lengths_ref, lane, first, (WINDOW, 1), 0, 0))
        bases.append((into, back))
    sums[...] = jnp.zeros_like(sums)
    gs[...] = lax.dot_general(
        cot_ref[begin : begin + length], w_ref[...], (((1,), (1,)), ((), ())), preferred_element_type=f32
    )
    for at in range(0, length, strip):
        place = slice(begin + at, begin + at + strip)
        normed = normed_ref[place]
        affine = normed * gain + bias
        gate = sigmoid(affine)
        grad = gs[at : at + strip] * gate * (1.0 + affine * (1.0 - gate))
        prod = grad * normed
        sums[:8] += prod[:8] + prod[8:]
        sums[8:] += grad[:8] + grad[8:]
        grad_normed = grad * gain
        mean = jnp.sum(grad_normed, axis=1, keepdims=True) * (1.0 / channels)
        along = jnp.sum(grad_normed * normed, axis=1, keepdims=True) * (1.0 / channels)
        out = (istd_ref[place, :1] * (grad_normed - mean - normed * along)).astype(bf16)
        row = at // ROWS * 2 * ROWS + at % ROWS
        g[row : row + strip] = out
        g[row + ROWS : row + ROWS + strip] = out
    table_high, table_low = halves(gather_ref[...])
    for at in range(0, channels, width):
        cols = slice(at, at + width)
        p, q, other = spec_ref[:BINS, cols], spec_ref[BINS:POINTS, cols], spec_ref[POINTS : 3 * BINS, cols]
        cross, pending, tail = None, None, None
        for block in range(blocks):
            into, back = bases[block]
            ghat = dot(into, g[block * 2 * ROWS : (block + 1) * 2 * ROWS, cols])
            cg, sg = ghat[:BINS], ghat[BINS:]
            place = (lane * blocks + block) * POINTS
            cx = xhat_ref[place : place + BINS, cols].astype(f32)
            sx = xhat_ref[place + BINS : place + POINTS, cols].astype(f32)
            terms = (cg * cx, sg * sx, sg * cx - cg * sx)
            cross = terms if cross is None else tuple(a + b for a, b in zip(cross, terms))
            vee = jnp.concatenate([cg * p - sg * q, sg * other + cg * q]).astype(bf16)
            part = dot(back[:, :POINTS], vee) + dot(back[:, POINTS:], vee)
            head, out, base = part[:EDGE], part[EDGE : EDGE + ROWS], block * ROWS
            if block == 0:
                edge_ref[:EDGE, cols] = head.astype(bf16)
                gi[:EDGE, cols] = out[:EDGE].astype(bf16)
            else:
                gi[base - EDGE : base, cols] = (pending + head).astype(bf16)
                gi[base : base + EDGE, cols] = (out[:EDGE] + tail).astype(bf16)
            gi[base + EDGE : base + ROWS - EDGE, cols] = out[EDGE : ROWS - EDGE].astype(bf16)
            pending, tail = out[ROWS - EDGE :], part[EDGE + ROWS :]
        gi[length - EDGE :, cols] = pending.astype(bf16)
        edge_ref[EDGE:, cols] = tail.astype(bf16)
        copy = pltpu.make_async_copy(gi.at[:, cols], gi_out.at[pl.ds(begin, length), cols], sems.at[at // width])
        copy.start()
        copies.append(copy)
        high, low = halves(jnp.concatenate(cross))
        value = dot(table_high, high) + dot(table_low, high) + dot(table_high, low)
        small_ref[:32, cols] = value + carry_ref[:32, cols]
    prod, grad = sums[:8], sums[8:]
    small_ref[32:40] = carry_ref[32:40] + jnp.concatenate(
        [
            jnp.sum(prod, axis=0, keepdims=True),
            jnp.sum(grad, axis=0, keepdims=True),
            jnp.zeros((6, channels), f32),
        ]
    )
    for copy in copies:
        copy.wait()


def layer_kernel(gate_ref, sw_ref, w_ref, out_ref):
    out_ref[...] = dot(sw_ref[...], w_ref[...]).astype(bf16)


def halves(value):
    high = value.astype(bf16)
    return high, (value - high.astype(f32)).astype(bf16)


def spectrum_kernel(table_ref, kernel_ref, gain_ref, bias_ref, spec_ref):
    channels = kernel_ref.shape[1]
    table_high, table_low = halves(table_ref[...])
    taps = jnp.concatenate([kernel_ref[...], jnp.zeros((32 - TAPS, channels), f32)])
    high, low = halves(taps)
    spec_ref[: 3 * BINS] = dot(table_high, high) + dot(table_low, high) + dot(table_high, low)
    spec_ref[3 * BINS :] = jnp.concatenate(
        [gain_ref[...].reshape(1, channels), bias_ref[...].reshape(1, channels), jnp.zeros((6, channels), f32)]
    )


def inner_rows(cot_ref, cols, blocks):
    lanes = cot_ref.shape[0] // (blocks * ROWS)
    return jnp.concatenate(
        [cot_ref[(k * blocks + 1) * ROWS : (k * blocks + blocks - 1) * ROWS, cols] for k in range(lanes)]
    )


def edge_rows(cot_ref, cols, blocks):
    lanes = cot_ref.shape[0] // (blocks * ROWS)
    starts = [(k * blocks + b) * ROWS for k in range(lanes) for b in (0, blocks - 1)]
    return jnp.concatenate([cot_ref[at : at + ROWS, cols] for at in starts])


def outer_kernel(blocks, meta_ref, inner_ref, edge_ref, other_ref, cot_ref, cot_other_ref, acc_ref):
    share, width = acc_ref.shape[0] // 4, acc_ref.shape[1]
    cols = pl.ds(pl.multiple_of(meta_ref[1] * width, width), width)
    inner, edge = inner_rows(cot_ref, cols, blocks), edge_rows(cot_ref, cols, blocks)
    other = inner_rows(cot_other_ref, cols, blocks)
    for at in range(4):
        part = slice(at * share, (at + 1) * share)
        acc_ref[part] = dot(inner_ref[part], inner) + dot(edge_ref[part], edge) + dot(other_ref[part], other)


def last_outer_kernel(blocks, meta_ref, acc_ref, sw_ref, cot_ref, own_ref, one_ref, two_ref, three_ref, total):
    share, width = acc_ref.shape[0] // 4, acc_ref.shape[1]
    piece = share // 4
    cols = pl.ds(pl.multiple_of(meta_ref[1] * width, width), width)
    edge = edge_rows(cot_ref, cols, blocks)
    for at in range(4):
        part = slice(at * share, (at + 1) * share)
        total[part] = acc_ref[part] + dot(sw_ref[part], edge)
    core, place = meta_ref[1], meta_ref[2]
    for shift, ref in enumerate((own_ref, one_ref, two_ref, three_ref)):
        chunk = lax.rem(place + shift, 4)
        for k in range(4):
            start = jnp.where(core == 0, chunk * share + k * piece, k * share + chunk * piece)
            value = total[pl.ds(pl.multiple_of(start, piece), piece)]
            ref[k * piece : (k + 1) * piece] = value.astype(ref.dtype)


def first_sum_kernel(meta_ref, a_ref, b_ref, c_ref, d_ref, own_ref, one_ref, two_ref, three_ref):
    piece = own_ref.shape[0]
    for shift, ref in enumerate((own_ref, one_ref, two_ref, three_ref)):
        rows = pl.ds(pl.multiple_of(lax.rem(meta_ref[3] + shift, 4) * piece, piece), piece)
        value = (a_ref[rows] + c_ref[rows].astype(f32)) + (b_ref[rows].astype(f32) + d_ref[rows].astype(f32))
        ref[...] = value.astype(ref.dtype)


def place_kernel(scale, meta_ref, *refs):
    out_ref = refs[-1]
    width = refs[0].shape[1]
    piece = out_ref.shape[0] // 4
    for side in range(2):
        core = meta_ref[1] if side == 0 else 1 - meta_ref[1]
        place = meta_ref[4] if side == 0 else meta_ref[5]
        cols = pl.ds(pl.multiple_of(core * width, width), width)
        for shift in range(4):
            rows = pl.ds(pl.multiple_of(lax.rem(place + 4 - shift, 4) * piece, piece), piece)
            out_ref[rows, cols] = refs[side * 4 + shift][:piece].astype(f32) * scale


def place_small_kernel(scale, meta_ref, own_ref, away_ref, taps_ref, gain_ref, bias_ref):
    first = meta_ref[1] == 0
    width = own_ref.shape[1]
    own, away = own_ref[...] * scale, away_ref[...] * scale
    for side in range(2):
        cols = slice(side * width, (side + 1) * width)
        value = jnp.where(first == (side == 0), own, away)
        taps_ref[:, cols] = value[:TAPS]
        gain_ref[cols] = value[32]
        bias_ref[cols] = value[33]


def whole(shape):
    return pl.BlockSpec(shape, lambda *i: (0,) * len(shape))


SMEM = pl.BlockSpec(memory_space=pltpu.SMEM)
VMEM = pl.BlockSpec(memory_space=pltpu.VMEM)


def params(mebibytes):
    return pltpu.CompilerParams(vmem_limit_bytes=mebibytes << 20)


def cost(flops, moved):
    return pl.CostEstimate(flops=flops, bytes_accessed=moved, transcendentals=0)


def near(*arrays):
    return [pltpu.with_memory_space_constraint(a, pltpu.VMEM) for a in arrays]


ANY = pl.BlockSpec(memory_space=pl.ANY)


def forward(tasks, meta, lengths, flat, before, after, split, split_t, spec, kept, name, interpret=False):
    total, channels = flat.shape
    blocks = total // lengths.shape[0] // ROWS
    count = len(tasks)
    rows = count * ROWS
    return pl.pallas_call(
        functools.partial(forward_kernel, tasks, blocks),
        in_specs=[SMEM, SMEM] + [VMEM] * 6 + [ANY] * len(kept),
        out_specs=[ANY] * 4 + [VMEM],
        out_shape=[
            pltpu.HBM((total, channels), bf16),
            pltpu.HBM((total, channels), f32),
            pltpu.HBM((total, 128), f32),
            pltpu.HBM((total // ROWS * POINTS, channels), bf16),
            pltpu.HBM((channels, rows), bf16),
        ],
        scratch_shapes=[
            pltpu.VMEM((count, ROWS, channels), f32),
            pltpu.VMEM((rows, channels), bf16),
            pltpu.VMEM((rows, channels), f32),
            pltpu.VMEM((rows, 128), f32),
            pltpu.VMEM((count * POINTS, channels), bf16),
            pltpu.SemaphoreType.DMA((count, 4)),
        ],
        input_output_aliases={8 + k: k for k in range(len(kept))},
        compiler_params=params(32),
        cost_estimate=cost(rows * channels * 2000, rows * channels * 12),
        interpret=interpret,
        name=name,
    )(meta, lengths, *near(flat, before, after, split, split_t, spec), *kept)


def backward(lane, meta, lengths, cot, normed, istd, xhat, w, split, split_t, spec, gather, carry, gi, interpret=False):
    total, channels = cot.shape
    length = total // lengths.shape[0]
    blocks = length // ROWS
    kept = [] if gi is None else [gi]
    return pl.pallas_call(
        functools.partial(backward_kernel, lane, blocks),
        in_specs=[SMEM, SMEM] + [VMEM] * 10 + [ANY] * len(kept),
        out_specs=[ANY, VMEM, VMEM],
        out_shape=[
            pltpu.HBM((total, channels), bf16),
            jax.ShapeDtypeStruct((2 * EDGE, channels), bf16),
            jax.ShapeDtypeStruct((40, channels), f32),
        ],
        scratch_shapes=[
            pltpu.VMEM((length, channels), f32),
            pltpu.VMEM((2 * length, channels), bf16),
            pltpu.VMEM((length, channels), bf16),
            pltpu.VMEM((16, channels), f32),
            pltpu.SemaphoreType.DMA((3,)),
        ],
        input_output_aliases={12: 0} if kept else {},
        compiler_params=params(24),
        cost_estimate=cost(length * channels * 8000, length * channels * 20),
        interpret=interpret,
        name=f"backward_{lane}",
    )(meta, lengths, *near(cot, normed, istd, xhat, w, split, split_t, spec, gather, carry), *kept)


def project(gate, sw, w, interpret=False):
    total, channels = sw.shape
    rows = 2 * ROWS
    row = pl.BlockSpec((rows, channels), lambda i: (i, 0))
    return pl.pallas_call(
        layer_kernel,
        grid=(total // rows,),
        in_specs=[ANY, row, VMEM],
        out_specs=row,
        out_shape=pltpu.HBM((total, channels), bf16),
        compiler_params=params(16),
        cost_estimate=cost(2 * total * channels * channels, 4 * total * channels),
        interpret=interpret,
        name="layer_out",
    )(gate, sw, *near(w))


def outer(meta, inner, edge, other, cot, cot_other, blocks):
    channels, rows = inner.shape
    width = channels // 2
    return pl.pallas_call(
        functools.partial(outer_kernel, blocks),
        in_specs=[SMEM] + [VMEM] * 5,
        out_specs=VMEM,
        out_shape=pltpu.VMEM((channels, width), f32),
        compiler_params=params(12),
        cost_estimate=cost(6 * rows * channels * width, 10 * rows * channels),
        name="outer_most",
    )(meta, *near(inner, edge, other, cot, cot_other))


def last_outer(meta, acc, other, cot_other, blocks):
    channels, rows = other.shape
    width, share = channels // 2, channels // 4
    return pl.pallas_call(
        functools.partial(last_outer_kernel, blocks),
        in_specs=[SMEM] + [VMEM] * 3,
        out_specs=[VMEM] * 4,
        out_shape=[pltpu.VMEM((share, width), f32)] + [pltpu.HBM((share, width), bf16)] * 3,
        scratch_shapes=[pltpu.VMEM(acc.shape, f32)],
        compiler_params=params(12),
        cost_estimate=cost(2 * rows * channels * width, 10 * rows * channels),
        name="outer_last",
    )(meta, *near(acc, other, cot_other))


def first_sum(meta, parts):
    share, width = parts[0].shape
    piece = share // 4
    return pl.pallas_call(
        first_sum_kernel,
        in_specs=[SMEM] + [VMEM] * 4,
        out_specs=[VMEM] * 4,
        out_shape=[pltpu.VMEM((piece, width), f32)] + [pltpu.HBM((piece, width), bf16)] * 3,
        compiler_params=params(12),
        name="sum_first",
    )(meta, *near(*parts))


def place(meta, pieces, share, scale):
    width = pieces[0].shape[1]
    return pl.pallas_call(
        functools.partial(place_kernel, scale),
        in_specs=[SMEM] + [VMEM] * 8,
        out_specs=VMEM,
        out_shape=jax.ShapeDtypeStruct((share, 2 * width), f32),
        compiler_params=params(12),
        name="place",
    )(meta, *near(*pieces))


def place_small(meta, own, away, scale):
    width = own.shape[1]
    return pl.pallas_call(
        functools.partial(place_small_kernel, scale),
        in_specs=[SMEM] + [VMEM] * 2,
        out_specs=[VMEM] * 3,
        out_shape=[
            jax.ShapeDtypeStruct((TAPS, 2 * width), f32),
            jax.ShapeDtypeStruct((2 * width,), f32),
            jax.ShapeDtypeStruct((2 * width,), f32),
        ],
        compiler_params=params(12),
        name="place_small",
    )(meta, own, away)


def shifts(size):
    up = [(i, i + 1) for i in range(size - 1)]
    return up, [(j, i) for i, j in up]


EVERY = ("dp", "seq")


def along(axes, shift):
    pairs = []
    for device in range(128):
        where = {"y": device % 4, "c": device // 4 % 2, "x": device // 8 % 4, "z": device // 32}
        axis = axes[where["c"]]
        moved = dict(where)
        moved[axis] = (where[axis] + shift) % (2 if axis == "c" else 4)
        pairs.append((device, ((moved["z"] * 4 + moved["x"]) * 2 + moved["c"]) * 4 + moved["y"]))
    return pairs


def swap(value):
    return lax.ppermute(value, EVERY, along("cc", 1))


def spread(values, axes):
    return [lax.ppermute(value, EVERY, along(axes, s + 1)) for s, value in enumerate(values)]


def four(own, one, two, three):
    own, one, two, three = (v.astype(f32) for v in (own, one, two, three))
    return (own + two) + (one + three)


def all_four(value, axes):
    return four(value, *spread([value] * 3, axes))


def both(value):
    return jnp.concatenate(halves(value))


def joined(value):
    rows = value.shape[0] // 2
    return value[:rows].astype(f32) + value[rows:].astype(f32)


def local(glu_out, lengths, kernel, norm_gain, norm_bias, w_out, cotangent, interpret=False):
    lanes, length, channels = glu_out.shape
    seq_count = lax.axis_size("seq")
    norm_scale = 1.0 / math.sqrt(lanes * lax.axis_size("dp") * length * seq_count)
    y = lax.axis_index("seq")
    dp = lax.axis_index("dp")
    core, x, z = lax.rem(dp, 2), lax.rem(lax.div(dp, 2), 4), lax.div(dp, 8)
    first = core == 0
    meta = jnp.stack(
        [
            y * length,
            core,
            jnp.where(first, y, z),
            jnp.where(first, x, y),
            jnp.where(first, x, z),
            jnp.where(first, z, x),
        ]
    ).astype(jnp.int32)
    up, down = shifts(seq_count)
    before = lax.ppermute(glu_out[:, length - EDGE :], "seq", up).reshape(lanes * EDGE, channels)
    after = lax.ppermute(glu_out[:, :EDGE], "seq", down).reshape(lanes * EDGE, channels)
    cot = cotangent.reshape(-1, channels)
    split, split_t, wide, deep = (jnp.asarray(t) for t in tables())
    spec = pl.pallas_call(
        spectrum_kernel,
        in_specs=[VMEM] * 4,
        out_specs=VMEM,
        out_shape=pltpu.VMEM((3 * BINS + 8, channels), f32),
        compiler_params=params(12),
        interpret=interpret,
        name="spectrum",
    )(wide, kernel, norm_gain, norm_bias)
    flat = glu_out.reshape(lanes * length, channels)
    blocks = length // ROWS
    inner = [(lane, block) for lane in range(lanes) for block in range(1, blocks - 1)]
    edge = [(lane, block) for lane in range(lanes) for block in (0, blocks - 1)]
    none = jnp.zeros((lanes * EDGE, channels), bf16)
    kept, turned_inner = (lambda *o: (o[:4], o[4]))(
        *forward(inner, meta, lengths, flat, none, none, split, split_t, spec, (), "conv_inner", interpret=interpret)
    )
    kept, turned_edge = (lambda *o: (o[:4], o[4]))(
        *forward(edge, meta, lengths, flat, before, after, split, split_t, spec, kept, "conv_edge", interpret=interpret)
    )
    sw, normed, istd, xhat = kept
    share, half = channels // seq_count, channels // 2
    whole_slice = lax.axis_size("dp") == 32
    if whole_slice:
        cot_other = swap(cot)
        acc = outer(meta, turned_inner, turned_edge, swap(turned_inner), cot, cot_other, blocks)
        parts = list(last_outer(meta, acc, swap(turned_edge), cot_other, blocks))
        sent = spread(parts[1:], "yz")
        cot, parts[0] = lax.optimization_barrier((cot, parts[0]))
    else:
        total_outer = dot(turned_inner, inner_rows(cot, slice(None), blocks)) + dot(
            turned_edge, edge_rows(cot, slice(None), blocks)
        )
        grad_w = lax.psum(total_outer, "seq") * norm_scale
        grad_w = lax.dynamic_slice_in_dim(grad_w, y * share, share, 0)
    small, gi, edges = jnp.zeros((40, channels), f32), None, []
    for lane in range(lanes):
        gi, ends, small = backward(
            lane, meta, lengths, cot, normed, istd, xhat, w_out, split, split_t, spec, deep, small, gi,
            interpret=interpret,
        )
        edges.append(ends)
    if whole_slice:
        pieces = list(first_sum(meta, [parts[0]] + sent))
        small, pieces[0] = lax.optimization_barrier((small, pieces[0]))
    heads = jnp.concatenate([e[:EDGE] for e in edges])
    tails = jnp.concatenate([e[EDGE:] for e in edges])
    if whole_slice:
        layer = project(pieces[0], sw, w_out)
        small = small + swap(small)
        small = both(lax.dynamic_slice_in_dim(small, core * half, half, 1))
        flat_small = jnp.concatenate([small[:40], small[40:]], axis=1)
        ways = [jnp.concatenate([tails, flat_small]), flat_small, jnp.concatenate([heads, flat_small])]
        one, two, three = spread(ways, "yy")
        count = lanes * EDGE
        before, after = one[:count], three[:count]

        def split_rows(v):
            return jnp.concatenate([v[:, :half], v[:, half:]])

        small = four(joined(small), *(joined(split_rows(v)) for v in (one[count:], two, three[count:])))
        pieces = [pieces[0]] + spread(pieces[1:], "xy")
        piece = four(*pieces).astype(bf16)
        rows = piece.shape[0]
        sent = jnp.concatenate([piece, both(small)])
        got = [sent] + spread([sent] * 3, "zx")
        piece = four(*(v[:rows] for v in got)).astype(bf16)
        small = four(*(joined(v[rows:]) for v in got))
        sent = jnp.concatenate([piece, both(small)])
        got = [sent] + spread([sent] * 3, "xz")
        small = four(*(joined(v[rows:]) for v in got))
        grad_w = place(meta, got + [swap(v) for v in got], share, norm_scale)
        taps, gain, bias = place_small(meta, small, swap(small), norm_scale)
    else:
        layer = project(sw, sw, w_out, interpret=interpret)
        before, after = lax.ppermute(tails, "seq", up), lax.ppermute(heads, "seq", down)
        small = lax.psum(small, "seq") * norm_scale
        taps, gain, bias = small[:TAPS], small[32], small[33]
    before = jnp.where(y == 0, 0.0, before.astype(f32)).astype(bf16).reshape(lanes, EDGE, channels)
    after = jnp.where(y == seq_count - 1, 0.0, after.astype(f32)).astype(bf16).reshape(lanes, EDGE, channels)
    gi = gi.reshape(lanes, length, channels)
    gi = gi.at[:, :EDGE].add(before).at[:, length - EDGE :].add(after)
    return (layer.reshape(lanes, length, channels), gi, grad_w, taps, gain, bias)


def solution(mesh):
    in_specs = (P("dp", "seq", None), P("dp", None), P(), P(), P(), P(), P("dp", "seq", None))
    out_specs = (P("dp", "seq", None), P("dp", "seq", None), P("seq", None), P(), P(), P())
    return jax.shard_map(local, mesh=mesh, in_specs=in_specs, out_specs=out_specs, check_vma=False)
```

```python
import functools
import math

import jax
import jax.numpy as jnp
import numpy as np
from jax import lax
from jax.experimental import pallas as pl
from jax.experimental.pallas import tpu as pltpu
from jax.sharding import PartitionSpec as P

EPSILON = 1e-05
TAPS = 31
HALF = TAPS // 2
ROWS = 128
EDGE = 16
WINDOW = ROWS + 2 * EDGE
POINTS = 256
BINS = POINTS // 2
f32, bf16 = jnp.float32, jnp.bfloat16


def tables():
    place = np.arange(POINTS)
    bins = np.arange(BINS)[:, None]
    cosines = math.sqrt(2.0 / POINTS) * np.cos(2 * np.pi * ((bins * place) % POINTS) / POINTS)
    sines = math.sqrt(2.0 / POINTS) * np.sin(2 * np.pi * ((bins * place) % POINTS) / POINTS)
    cosines[0] = 1.0 / math.sqrt(POINTS)
    sines[0] = (1.0 - 2.0 * (place % 2)) / math.sqrt(POINTS)
    basis = np.concatenate([cosines, sines])
    high = basis.astype(jnp.bfloat16)
    low = (basis - high.astype(np.float64)).astype(jnp.bfloat16)
    split = np.concatenate([high, low])
    lags = np.arange(TAPS) - HALF
    turn = 2 * np.pi * ((bins * lags) % POINTS) / POINTS
    real, imag = np.cos(turn), np.sin(turn)
    other = real.copy()
    other[0] = 1.0 - 2.0 * (np.abs(lags) % 2)
    spectrum = np.concatenate([real, imag, other]).astype(np.float32)
    gather = np.concatenate([real, other, -imag]).astype(np.float32)
    wide, deep = np.zeros((3 * BINS, 32), np.float32), np.zeros((32, 3 * BINS), np.float32)
    wide[:, :TAPS], deep[:TAPS] = spectrum, gather.T
    return split, np.ascontiguousarray(split.T), wide, deep


def gapped(lengths_ref, lane, first, shape, dim, skip):
    row = lax.broadcasted_iota(jnp.int32, shape, dim) + skip
    frame = first + row
    place, end = row, 0
    for utter in range(lengths_ref.shape[1] - 1):
        end = end + lengths_ref[lane, utter]
        place = place + jnp.where(frame >= end, jnp.where(first < end, HALF, 0), 0)
    return place


def chosen_columns(split, place):
    count = place.shape[1]
    one_hot = (lax.broadcasted_iota(jnp.int32, (POINTS, count), 0) == place).astype(f32).astype(bf16)
    return jnp.dot(split, one_hot, preferred_element_type=f32).astype(bf16)


def chosen_rows(split_t, place):
    count = place.shape[0]
    one_hot = (lax.broadcasted_iota(jnp.int32, (count, POINTS), 1) == place).astype(f32).astype(bf16)
    return jnp.dot(one_hot, split_t, preferred_element_type=f32).astype(bf16)


def dot(a, b):
    return jnp.dot(a, b, preferred_element_type=f32)


def sigmoid(a):
    return 0.5 * jnp.tanh(0.5 * a) + 0.5


def forward_kernel(tasks, blocks, meta_ref, lengths_ref, x_ref, before_ref, after_ref, split_ref, split_t_ref, spec_ref,
                   *rest):
    outs, (turned_ref, conv, sw, normed_all, istd, xhat_all, sems) = rest[-11:-7], rest[-7:]
    channels = x_ref.shape[1]
    gain, bias = spec_ref[3 * BINS : 3 * BINS + 1], spec_ref[3 * BINS + 1 : 3 * BINS + 2]
    strip, width = 16, channels // 2
    bases, copies = [], []
    for lane, block in tasks:
        first = meta_ref[0] + (block * ROWS - EDGE)
        into = chosen_columns(split_ref[...], gapped(lengths_ref, lane, first, (1, WINDOW), 1, 0))
        back = chosen_rows(split_t_ref[...], gapped(lengths_ref, lane, first, (ROWS, 1), 0, EDGE))
        bases.append((into, back))

    def transform(task):
        lane, block = tasks[task]
        into, back = bases[task]
        start = (lane * blocks + block) * ROWS
        halo = slice(lane * EDGE, (lane + 1) * EDGE)
        for at in range(0, channels, width):
            cols = slice(at, at + width)
            if block == 0:
                rows = jnp.concatenate([before_ref[halo, cols], x_ref[start : start + ROWS + EDGE, cols]])
            elif block == blocks - 1:
                rows = jnp.concatenate([x_ref[start - EDGE : start + ROWS, cols], after_ref[halo, cols]])
            else:
                rows = x_ref[start - EDGE : start + ROWS + EDGE, cols]
            xhat = dot(into[:POINTS], rows) + dot(into[POINTS:], rows)
            xhat_all[task * POINTS : (task + 1) * POINTS, cols] = xhat.astype(bf16)
            real, imag = xhat[:BINS], xhat[BINS:]
            p, q, other = spec_ref[:BINS, cols], spec_ref[BINS:POINTS, cols], spec_ref[POINTS : 3 * BINS, cols]
            zed = jnp.concatenate([real * p + imag * q, imag * other - real * q]).astype(bf16)
            conv[task, :, cols] = dot(back[:, :POINTS], zed) + dot(back[:, POINTS:], zed)

    def normalise(task):
        for at in range(0, ROWS, strip):
            place = slice(task * ROWS + at, task * ROWS + at + strip)
            value = conv[task, at : at + strip]
            centred = value - jnp.sum(value, axis=1, keepdims=True) * (1.0 / channels)
            variance = jnp.sum(centred * centred, axis=1, keepdims=True) * (1.0 / channels)
            inv_std = lax.rsqrt(variance + EPSILON)
            normed = centred * inv_std
            affine = normed * gain + bias
            sw[place] = (affine * sigmoid(affine)).astype(bf16)
            normed_all[place] = normed
            istd[place] = jnp.broadcast_to(inv_std, (strip, istd.shape[1]))
        own = slice(task * ROWS, (task + 1) * ROWS)
        turned_ref[:, own] = sw[own].T
        lane, block = tasks[task]
        for k, (source, target) in enumerate(zip((sw, normed_all, istd, xhat_all), outs)):
            size = POINTS if k == 3 else ROWS
            copy = pltpu.make_async_copy(
                source.at[pl.ds(task * size, size)],
                target.at[pl.ds((lane * blocks + block) * size, size)],
                sems.at[task, k],
            )
            copy.start()
            copies.append(copy)

    for task in range(len(tasks) + 1):
        if task < len(tasks):
            transform(task)
        if task > 0:
            normalise(task - 1)
    for copy in copies:
        copy.wait()


def backward_kernel(lane, blocks, meta_ref, lengths_ref, cot_ref, normed_ref, istd_ref, xhat_ref, w_ref,
                    split_ref, split_t_ref, spec_ref, gather_ref, carry_ref, *rest):
    gi_out, edge_ref, small_ref, gs, g, gi, sums, sems = rest[-8:]
    channels = cot_ref.shape[1]
    length = blocks * ROWS
    begin = lane * length
    gain, bias = spec_ref[3 * BINS : 3 * BINS + 1], spec_ref[3 * BINS + 1 : 3 * BINS + 2]
    strip, width = 16, channels // 3
    bases, copies = [], []
    for block in range(blocks):
        first = meta_ref[0] + (block * ROWS - EDGE)
        into = chosen_columns(split_ref[...], gapped(lengths_ref, lane, first, (1, ROWS), 1, EDGE))
        into = jnp.concatenate([into[:POINTS], into[POINTS:]], axis=1)
        back = chosen_rows(split_t_ref[...], gapped(lengths_ref, lane, first, (WINDOW, 1), 0, 0))
        bases.append((into, back))
    sums[...] = jnp.zeros_like(sums)
    gs[...] = lax.dot_general(
        cot_ref[begin : begin + length], w_ref[...], (((1,), (1,)), ((), ())), preferred_element_type=f32
    )
    for at in range(0, length, strip):
        place = slice(begin + at, begin + at + strip)
        normed = normed_ref[place]
        affine = normed * gain + bias
        gate = sigmoid(affine)
        grad = gs[at : at + strip] * gate * (1.0 + affine * (1.0 - gate))
        prod = grad * normed
        sums[:8] += prod[:8] + prod[8:]
        sums[8:] += grad[:8] + grad[8:]
        grad_normed = grad * gain
        mean = jnp.sum(grad_normed, axis=1, keepdims=True) * (1.0 / channels)
        along = jnp.sum(grad_normed * normed, axis=1, keepdims=True) * (1.0 / channels)
        out = (istd_ref[place, :1] * (grad_normed - mean - normed * along)).astype(bf16)
        row = at // ROWS * 2 * ROWS + at % ROWS
        g[row : row + strip] = out
        g[row + ROWS : row + ROWS + strip] = out
    table_high, table_low = halves(gather_ref[...])
    for at in range(0, channels, width):
        cols = slice(at, at + width)
        p, q, other = spec_ref[:BINS, cols], spec_ref[BINS:POINTS, cols], spec_ref[POINTS : 3 * BINS, cols]
        cross, pending, tail = None, None, None
        for block in range(blocks):
            into, back = bases[block]
            ghat = dot(into, g[block * 2 * ROWS : (block + 1) * 2 * ROWS, cols])
            cg, sg = ghat[:BINS], ghat[BINS:]
            place = (lane * blocks + block) * POINTS
            cx = xhat_ref[place : place + BINS, cols].astype(f32)
            sx = xhat_ref[place + BINS : place + POINTS, cols].astype(f32)
            terms = (cg * cx, sg * sx, sg * cx - cg * sx)
            cross = terms if cross is None else tuple(a + b for a, b in zip(cross, terms))
            vee = jnp.concatenate([cg * p - sg * q, sg * other + cg * q]).astype(bf16)
            part = dot(back[:, :POINTS], vee) + dot(back[:, POINTS:], vee)
            head, out, base = part[:EDGE], part[EDGE : EDGE + ROWS], block * ROWS
            if block == 0:
                edge_ref[:EDGE, cols] = head.astype(bf16)
                gi[:EDGE, cols] = out[:EDGE].astype(bf16)
            else:
                gi[base - EDGE : base, cols] = (pending + head).astype(bf16)
                gi[base : base + EDGE, cols] = (out[:EDGE] + tail).astype(bf16)
            gi[base + EDGE : base + ROWS - EDGE, cols] = out[EDGE : ROWS - EDGE].astype(bf16)
            pending, tail = out[ROWS - EDGE :], part[EDGE + ROWS :]
        gi[length - EDGE :, cols] = pending.astype(bf16)
        edge_ref[EDGE:, cols] = tail.astype(bf16)
        copy = pltpu.make_async_copy(gi.at[:, cols], gi_out.at[pl.ds(begin, length), cols], sems.at[at // width])
        copy.start()
        copies.append(copy)
        high, low = halves(jnp.concatenate(cross))
        value = dot(table_high, high) + dot(table_low, high) + dot(table_high, low)
        small_ref[:32, cols] = value + carry_ref[:32, cols]
    prod, grad = sums[:8], sums[8:]
    small_ref[32:40] = carry_ref[32:40] + jnp.concatenate(
        [
            jnp.sum(prod, axis=0, keepdims=True),
            jnp.sum(grad, axis=0, keepdims=True),
            jnp.zeros((6, channels), f32),
        ]
    )
    for copy in copies:
        copy.wait()


def layer_kernel(gate_ref, sw_ref, w_ref, *rest):
    rest[-1][...] = dot(sw_ref[...], w_ref[...]).astype(bf16)


def halves(value):
    high = value.astype(bf16)
    return high, (value - high.astype(f32)).astype(bf16)


def spectrum_kernel(table_ref, kernel_ref, gain_ref, bias_ref, spec_ref):
    channels = kernel_ref.shape[1]
    table_high, table_low = halves(table_ref[...])
    taps = jnp.concatenate([kernel_ref[...], jnp.zeros((32 - TAPS, channels), f32)])
    high, low = halves(taps)
    spec_ref[: 3 * BINS] = dot(table_high, high) + dot(table_low, high) + dot(table_high, low)
    spec_ref[3 * BINS :] = jnp.concatenate(
        [gain_ref[...].reshape(1, channels), bias_ref[...].reshape(1, channels), jnp.zeros((6, channels), f32)]
    )


def frame_rows(cot_ref, target, cols, blocks, edges, sems):
    length = blocks * ROWS
    if edges:
        spans = [(k * length + b * ROWS, ROWS) for k in range(cot_ref.shape[0] // length) for b in (0, blocks - 1)]
    else:
        spans = [(k * length + ROWS, length - 2 * ROWS) for k in range(cot_ref.shape[0] // length)]
    copies, at = [], 0
    for k, (start, size) in enumerate(spans):
        source = cot_ref.at[pl.ds(start, size), cols]
        copies.append(pltpu.make_async_copy(source, target.at[pl.ds(at, size)], sems.at[k]))
        at += size
    return copies


def outer_kernel(blocks, meta_ref, inner_ref, edge_ref, other_ref, cot_ref, cot_other_ref, acc_ref, left, right, sems):
    share, width = acc_ref.shape[0] // 4, acc_ref.shape[1]
    cols = pl.ds(pl.multiple_of(meta_ref[1] * width, width), width)
    loads = []
    for k, (source, cot, edges) in enumerate(
        ((inner_ref, cot_ref, False), (edge_ref, cot_ref, True), (other_ref, cot_other_ref, False))
    ):
        copies = [pltpu.make_async_copy(source, left.at[k], sems.at[k, 4])]
        copies += frame_rows(cot, right.at[k], cols, blocks, edges, sems.at[k])
        for copy in copies:
            copy.start()
        loads.append(copies)
    for k, copies in enumerate(loads):
        for copy in copies:
            copy.wait()
        for at in range(4):
            part = slice(at * share, (at + 1) * share)
            value = dot(left[k, part], right[k])
            acc_ref[part] = value if k == 0 else acc_ref[part] + value


def last_outer_kernel(blocks, meta_ref, acc_ref, sw_ref, cot_ref, own_ref, one_ref, two_ref, three_ref, chunks, left,
                      right, sems):
    share, width = acc_ref.shape[0] // 4, acc_ref.shape[1]
    piece = share // 4
    cols = pl.ds(pl.multiple_of(meta_ref[1] * width, width), width)
    copies = frame_rows(cot_ref, right, cols, blocks, True, sems)
    for at in range(4):
        rows = pl.ds(at * share, share)
        copies.append(pltpu.make_async_copy(sw_ref.at[rows], left.at[rows], sems.at[4 + at]))
    for copy in copies:
        copy.start()
    for copy in copies[:-4]:
        copy.wait()
    for at in range(4):
        part = slice(at * share, (at + 1) * share)
        copies[at - 4].wait()
        value = (acc_ref[part] + dot(left[part], right[...])).astype(bf16)
        for k in range(4):
            shift = lax.rem(k + 4 - meta_ref[2], 4)
            chunks[shift, at * piece : (at + 1) * piece] = value[k * piece : (k + 1) * piece]
    copies = [
        pltpu.make_async_copy(chunks.at[1 + k], ref, sems.at[k]) for k, ref in enumerate((one_ref, two_ref, three_ref))
    ]
    for copy in copies:
        copy.start()
    own_ref[...] = chunks[0]
    for copy in copies:
        copy.wait()


def first_sum_kernel(meta_ref, a_ref, b_ref, c_ref, d_ref, small_ref, away_ref, *rest):
    ends, (own_ref, own_small_ref, one_ref, two_ref, three_ref) = rest[:-5], rest[-5:]
    piece, width = own_ref.shape
    cols = pl.ds(pl.multiple_of(meta_ref[1] * width, width), width)
    high, low = halves(small_ref[:, cols] + away_ref[:, cols])
    half = high.shape[0]
    own_small_ref[:half], own_small_ref[half:] = high, low
    for shift, ref in enumerate((own_ref, one_ref, two_ref, three_ref)):
        rows = pl.ds(pl.multiple_of(lax.rem(meta_ref[3] + shift, 4) * piece, piece), piece)
        value = (a_ref[rows].astype(f32) + c_ref[rows].astype(f32)) + (b_ref[rows].astype(f32) + d_ref[rows].astype(f32))
        ref[:piece] = value.astype(ref.dtype)
        if shift > 0:
            ref[piece : piece + half] = high
            ref[piece + half : piece + 2 * half] = low
    for ref, begin in ((one_ref, EDGE), (three_ref, 0)):
        at = piece + 2 * half
        for side in range(2):
            for end in ends:
                ref[at : at + EDGE] = end[begin : begin + EDGE, side * width : (side + 1) * width]
                at += EDGE


def place_kernel(scale, meta_ref, *refs):
    out_ref, taps_ref, gain_ref, bias_ref = refs[-4:]
    width = refs[0].shape[1]
    piece = out_ref.shape[0] // 4
    half = (refs[0].shape[0] - piece) // 2
    small = []
    for side in range(2):
        core = meta_ref[1] if side == 0 else 1 - meta_ref[1]
        place = meta_ref[4] if side == 0 else meta_ref[5]
        cols = pl.ds(pl.multiple_of(core * width, width), width)
        got = refs[side * 4 : side * 4 + 4]
        for shift in range(4):
            rows = pl.ds(pl.multiple_of(lax.rem(place + 4 - shift, 4) * piece, piece), piece)
            out_ref[rows, cols] = got[shift][:piece].astype(f32) * scale
        terms = [ref[piece : piece + half].astype(f32) + ref[piece + half :].astype(f32) for ref in got]
        small.append(four(*terms) * scale)
    first = meta_ref[1] == 0
    for side in range(2):
        cols = slice(side * width, (side + 1) * width)
        value = jnp.where(first == (side == 0), small[0], small[1])
        taps_ref[:, cols] = value[:TAPS]
        gain_ref[cols] = value[32]
        bias_ref[cols] = value[33]


def whole(shape):
    return pl.BlockSpec(shape, lambda *i: (0,) * len(shape))


SMEM = pl.BlockSpec(memory_space=pltpu.SMEM)
HBM = pl.BlockSpec(memory_space=pltpu.HBM)
VMEM = pl.BlockSpec(memory_space=pltpu.VMEM)


def params(mebibytes):
    return pltpu.CompilerParams(vmem_limit_bytes=mebibytes << 20)


def cost(flops, moved):
    return pl.CostEstimate(flops=flops, bytes_accessed=moved, transcendentals=0)


def near(*arrays):
    return [pltpu.with_memory_space_constraint(a, pltpu.VMEM) for a in arrays]


def far(*arrays):
    return [pltpu.with_memory_space_constraint(a, pltpu.HBM) for a in arrays]


def forward(tasks, meta, lengths, flat, before, after, split, split_t, spec, kept, name, interpret=False):
    total, channels = flat.shape
    blocks = total // lengths.shape[0] // ROWS
    count = len(tasks)
    rows = count * ROWS
    return pl.pallas_call(
        functools.partial(forward_kernel, tasks, blocks),
        in_specs=[SMEM, SMEM] + [VMEM] * 6 + [HBM] * len(kept),
        out_specs=[HBM] * 4 + [VMEM],
        out_shape=[
            pltpu.HBM((total, channels), bf16),
            pltpu.HBM((total, channels), f32),
            pltpu.HBM((total, 128), f32),
            pltpu.HBM((total // ROWS * POINTS, channels), bf16),
            pltpu.HBM((channels, rows), bf16),
        ],
        scratch_shapes=[
            pltpu.VMEM((count, ROWS, channels), f32),
            pltpu.VMEM((rows, channels), bf16),
            pltpu.VMEM((rows, channels), f32),
            pltpu.VMEM((rows, 128), f32),
            pltpu.VMEM((count * POINTS, channels), bf16),
            pltpu.SemaphoreType.DMA((count, 4)),
        ],
        input_output_aliases={8 + k: k for k in range(len(kept))},
        compiler_params=params(32),
        cost_estimate=cost(9_000_000_000, rows * channels * 12),
        interpret=interpret,
        name=name,
    )(meta, lengths, *near(flat, before, after, split, split_t, spec), *kept)


def backward(lane, meta, lengths, cot, normed, istd, xhat, w, split, split_t, spec, gather, carry, gi, interpret=False):
    total, channels = cot.shape
    length = total // lengths.shape[0]
    blocks = length // ROWS
    kept = [] if gi is None else [gi]
    return pl.pallas_call(
        functools.partial(backward_kernel, lane, blocks),
        in_specs=[SMEM, SMEM] + [VMEM] * 10 + [HBM] * len(kept),
        out_specs=[HBM, VMEM, VMEM],
        out_shape=[
            pltpu.HBM((total, channels), bf16),
            jax.ShapeDtypeStruct((2 * EDGE, channels), bf16),
            jax.ShapeDtypeStruct((40, channels), f32),
        ],
        scratch_shapes=[
            pltpu.VMEM((length, channels), f32),
            pltpu.VMEM((2 * length, channels), bf16),
            pltpu.VMEM((length, channels), bf16),
            pltpu.VMEM((16, channels), f32),
            pltpu.SemaphoreType.DMA((3,)),
        ],
        input_output_aliases={12: 0} if kept else {},
        compiler_params=params(24),
        cost_estimate=cost(12_000_000_000, length * channels * 20),
        interpret=interpret,
        name=f"backward_{lane}",
    )(meta, lengths, *near(cot, normed, istd, xhat, w, split, split_t, spec, gather, carry), *kept)


def project(lane, lanes, gate, sw, w, layer, interpret=False):
    total, channels = sw.shape
    rows = 2 * ROWS
    steps = total // lanes // rows
    row = pl.BlockSpec((rows, channels), lambda i: (lane * steps + i, 0))
    kept = [] if layer is None else [layer]
    return pl.pallas_call(
        layer_kernel,
        grid=(steps,),
        in_specs=[HBM, row, VMEM] + [HBM] * len(kept),
        out_specs=row,
        out_shape=pltpu.HBM((total, channels), bf16),
        input_output_aliases={3: 0} if kept else {},
        compiler_params=params(24),
        cost_estimate=cost(2 * total // lanes * channels * channels, 4 * total * channels),
        interpret=interpret,
        name=f"layer_out_{lane}",
    )(*far(gate, sw), *near(w), *far(*kept))


def outer(meta, inner, edge, other, cot, cot_other, blocks):
    channels, rows = inner.shape
    width = channels // 2
    return pl.pallas_call(
        functools.partial(outer_kernel, blocks),
        in_specs=[SMEM] + [HBM] * 5,
        out_specs=VMEM,
        out_shape=pltpu.VMEM((channels, width), f32),
        scratch_shapes=[
            pltpu.VMEM((3, channels, rows), bf16),
            pltpu.VMEM((3, rows, width), bf16),
            pltpu.SemaphoreType.DMA((3, 5)),
        ],
        compiler_params=params(16),
        cost_estimate=cost(6_000_000_000, 10 * rows * channels),
        name="outer_most",
    )(meta, *far(inner, edge, other, cot, cot_other))


def last_outer(meta, acc, other, cot_other, blocks):
    channels, rows = other.shape
    width, share = channels // 2, channels // 4
    return pl.pallas_call(
        functools.partial(last_outer_kernel, blocks),
        in_specs=[SMEM, VMEM] + [HBM] * 2,
        out_specs=[VMEM] + [HBM] * 3,
        out_shape=[pltpu.VMEM((share, width), bf16)] + [pltpu.HBM((share, width), bf16)] * 3,
        scratch_shapes=[
            pltpu.VMEM((4, share, width), bf16),
            pltpu.VMEM((channels, rows), bf16),
            pltpu.VMEM((rows, width), bf16),
            pltpu.SemaphoreType.DMA((8,)),
        ],
        compiler_params=params(16),
        cost_estimate=cost(3_000_000_000, 10 * rows * channels),
        name="outer_last",
    )(meta, *near(acc), *far(other, cot_other))


def first_sum(meta, parts, small, away, ends):
    share, width = parts[0].shape
    piece = share // 4
    tall = piece + 2 * small.shape[0]
    edges = 2 * EDGE * len(ends)
    return pl.pallas_call(
        first_sum_kernel,
        in_specs=[SMEM] + [VMEM] * (6 + len(ends)),
        out_specs=[VMEM] * 5,
        out_shape=[
            jax.ShapeDtypeStruct((piece, width), f32),
            jax.ShapeDtypeStruct((tall - piece, width), bf16),
            pltpu.HBM((tall + edges, width), bf16),
            pltpu.HBM((tall, width), bf16),
            pltpu.HBM((tall + edges, width), bf16),
        ],
        compiler_params=params(12),
        name="sum_first",
    )(meta, *parts, small, away, *ends)


def place(meta, got, share, scale):
    width = got[0].shape[1]
    return pl.pallas_call(
        functools.partial(place_kernel, scale),
        in_specs=[SMEM] + [VMEM] * 8,
        out_specs=[VMEM] * 4,
        out_shape=[
            jax.ShapeDtypeStruct((share, 2 * width), f32),
            jax.ShapeDtypeStruct((TAPS, 2 * width), f32),
            jax.ShapeDtypeStruct((2 * width,), f32),
            jax.ShapeDtypeStruct((2 * width,), f32),
        ],
        compiler_params=params(12),
        name="place",
    )(meta, *got)


def shifts(size):
    up = [(i, i + 1) for i in range(size - 1)]
    return up, [(j, i) for i, j in up]


EVERY = ("dp", "seq")


def along(axes, shift):
    pairs = []
    for device in range(128):
        where = {"y": device % 4, "c": device // 4 % 2, "x": device // 8 % 4, "z": device // 32}
        axis = axes[where["c"]]
        moved = dict(where)
        moved[axis] = (where[axis] + shift) % (2 if axis == "c" else 4)
        pairs.append((device, ((moved["z"] * 4 + moved["x"]) * 2 + moved["c"]) * 4 + moved["y"]))
    return pairs


def swap(value):
    return lax.ppermute(value, EVERY, along("cc", 1))


def spread(values, axes):
    return [lax.ppermute(value, EVERY, along(axes, s + 1)) for s, value in enumerate(values)]


def four(own, one, two, three):
    own, one, two, three = (v.astype(f32) for v in (own, one, two, three))
    return (own + two) + (one + three)


def all_four(value, axes):
    return four(value, *spread([value] * 3, axes))


def both(value):
    return jnp.concatenate(halves(value))


def joined(value):
    rows = value.shape[0] // 2
    return value[:rows].astype(f32) + value[rows:].astype(f32)


def local(glu_out, lengths, kernel, norm_gain, norm_bias, w_out, cotangent, interpret=False):
    lanes, length, channels = glu_out.shape
    seq_count = lax.axis_size("seq")
    norm_scale = 1.0 / math.sqrt(lanes * lax.axis_size("dp") * length * seq_count)
    y = lax.axis_index("seq")
    dp = lax.axis_index("dp")
    core, x, z = lax.rem(dp, 2), lax.rem(lax.div(dp, 2), 4), lax.div(dp, 8)
    first = core == 0
    meta = jnp.stack(
        [
            y * length,
            core,
            jnp.where(first, x, z),
            y,
            jnp.where(first, x, z),
            jnp.where(first, z, x),
        ]
    ).astype(jnp.int32)
    up, down = shifts(seq_count)
    before = lax.ppermute(glu_out[:, length - EDGE :], "seq", up).reshape(lanes * EDGE, channels)
    after = lax.ppermute(glu_out[:, :EDGE], "seq", down).reshape(lanes * EDGE, channels)
    cot = cotangent.reshape(-1, channels)
    split, split_t, wide, deep = (jnp.asarray(t) for t in tables())
    spec = pl.pallas_call(
        spectrum_kernel,
        in_specs=[VMEM] * 4,
        out_specs=VMEM,
        out_shape=pltpu.VMEM((3 * BINS + 8, channels), f32),
        compiler_params=params(12),
        interpret=interpret,
        name="spectrum",
    )(wide, kernel, norm_gain, norm_bias)
    flat = glu_out.reshape(lanes * length, channels)
    blocks = length // ROWS
    inner = [(lane, block) for lane in range(lanes) for block in range(1, blocks - 1)]
    edge = [(lane, block) for lane in range(lanes) for block in (0, blocks - 1)]
    none = jnp.zeros((lanes * EDGE, channels), bf16)
    kept, turned_inner = (lambda *o: (o[:4], o[4]))(
        *forward(inner, meta, lengths, flat, none, none, split, split_t, spec, (), "conv_inner", interpret=interpret)
    )
    kept, turned_edge = (lambda *o: (o[:4], o[4]))(
        *forward(edge, meta, lengths, flat, before, after, split, split_t, spec, kept, "conv_edge", interpret=interpret)
    )
    sw, normed, istd, xhat = kept
    share, half = channels // seq_count, channels // 2
    whole_slice = lax.axis_size("dp") == 32
    if whole_slice:
        cot_other = swap(cot)
        acc = outer(meta, turned_inner, turned_edge, swap(turned_inner), cot, cot_other, blocks)
        parts = list(last_outer(meta, acc, swap(turned_edge), cot_other, blocks))
        sent = spread(parts[1:], "xz")
        cot, parts[0] = lax.optimization_barrier((cot, parts[0]))
    else:
        places = [jnp.concatenate([cot[(a * blocks + b) * ROWS :][:ROWS] for a, b in t]) for t in (inner, edge)]
        grad_w = lax.psum(dot(turned_inner, places[0]) + dot(turned_edge, places[1]), "seq") * norm_scale
        grad_w = lax.dynamic_slice_in_dim(grad_w, y * share, share, 0)
    small, gi, ends = jnp.zeros((40, channels), f32), None, []
    for lane in range(lanes):
        gi, end, small = backward(
            lane, meta, lengths, cot, normed, istd, xhat, w_out, split, split_t, spec, deep, small, gi,
            interpret=interpret,
        )
        ends.append(end)
    if whole_slice:
        piece, extra, *sent = first_sum(meta, [parts[0]] + sent, small, swap(small), ends)
        layer = project(0, lanes, extra, sw, w_out, None)
        one, two, three = spread(sent, "yy")
        three, layer = lax.optimization_barrier((three, layer))
        rows = piece.shape[0]
        tall = rows + extra.shape[0]
        piece = four(piece, *(v[:rows] for v in (one, two, three))).astype(bf16)
        extra = four(*(joined(v) for v in (extra, one[rows:tall], two[rows:tall], three[rows:tall])))
        before, after = (jnp.concatenate(jnp.split(v[tall:], 2), axis=1) for v in (one, three))
        sent = jnp.concatenate([piece, both(extra)])
        layer = project(1, lanes, sent, sw, w_out, layer)
        got = [sent] + spread([sent] * 3, "zx")
        got[3], layer = lax.optimization_barrier((got[3], layer))
        piece = four(*(v[:rows] for v in got)).astype(bf16)
        extra = four(*(joined(v[rows:]) for v in got))
        sent = jnp.concatenate([piece, both(extra)])
        got = [sent] + spread([sent] * 3, "xz")
        grad_w, taps, gain, bias = place(meta, got + [swap(v) for v in got], share, norm_scale)
    else:
        layer = None
        for lane in range(lanes):
            layer = project(lane, lanes, sw, sw, w_out, layer, interpret=interpret)
        heads = jnp.concatenate([e[:EDGE] for e in ends])
        tails = jnp.concatenate([e[EDGE:] for e in ends])
        before, after = lax.ppermute(tails, "seq", up), lax.ppermute(heads, "seq", down)
        small = lax.psum(small, "seq") * norm_scale
        taps, gain, bias = small[:TAPS], small[32], small[33]
    before = jnp.where(y == 0, 0.0, before.astype(f32)).astype(bf16).reshape(lanes, EDGE, channels)
    after = jnp.where(y == seq_count - 1, 0.0, after.astype(f32)).astype(bf16).reshape(lanes, EDGE, channels)
    gi = gi.reshape(lanes, length, channels)
    gi = gi.at[:, :EDGE].add(before).at[:, length - EDGE :].add(after)
    return (layer.reshape(lanes, length, channels), gi, grad_w, taps, gain, bias)


def solution(mesh):
    in_specs = (P("dp", "seq", None), P("dp", None), P(), P(), P(), P(), P("dp", "seq", None))
    out_specs = (P("dp", "seq", None), P("dp", "seq", None), P("seq", None), P(), P(), P())
    return jax.shard_map(local, mesh=mesh, in_specs=in_specs, out_specs=out_specs, check_vma=False)
```

```python
import functools
import math

import jax
import jax.numpy as jnp
import numpy as np
from jax import lax
from jax.experimental import pallas as pl
from jax.experimental.pallas import tpu as pltpu
from jax.sharding import PartitionSpec as P

EPSILON = 1e-05
TAPS = 31
HALF = TAPS // 2
ROWS = 128
EDGE = 16
WINDOW = ROWS + 2 * EDGE
POINTS = 256
BINS = POINTS // 2
f32, bf16 = jnp.float32, jnp.bfloat16


def tables():
    place = np.arange(POINTS)
    bins = np.arange(BINS)[:, None]
    cosines = math.sqrt(2.0 / POINTS) * np.cos(2 * np.pi * ((bins * place) % POINTS) / POINTS)
    sines = math.sqrt(2.0 / POINTS) * np.sin(2 * np.pi * ((bins * place) % POINTS) / POINTS)
    cosines[0] = 1.0 / math.sqrt(POINTS)
    sines[0] = (1.0 - 2.0 * (place % 2)) / math.sqrt(POINTS)
    basis = np.concatenate([cosines, sines])
    high = basis.astype(jnp.bfloat16)
    low = (basis - high.astype(np.float64)).astype(jnp.bfloat16)
    split = np.concatenate([high, low])
    lags = np.arange(TAPS) - HALF
    turn = 2 * np.pi * ((bins * lags) % POINTS) / POINTS
    real, imag = np.cos(turn), np.sin(turn)
    other = real.copy()
    other[0] = 1.0 - 2.0 * (np.abs(lags) % 2)
    spectrum = np.concatenate([real, imag, other]).astype(np.float32)
    gather = np.concatenate([real, other, -imag]).astype(np.float32)
    wide, deep = np.zeros((3 * BINS, 32), np.float32), np.zeros((32, 3 * BINS), np.float32)
    wide[:, :TAPS], deep[:TAPS] = spectrum, gather.T
    return split, np.ascontiguousarray(split.T), wide, deep


def gapped(lengths_ref, lane, first, shape, dim, skip):
    row = lax.broadcasted_iota(jnp.int32, shape, dim) + skip
    frame = first + row
    place, end = row, 0
    for utter in range(lengths_ref.shape[1] - 1):
        end = end + lengths_ref[lane, utter]
        place = place + jnp.where(frame >= end, jnp.where(first < end, HALF, 0), 0)
    return place


def chosen_columns(split, place):
    count = place.shape[1]
    one_hot = (lax.broadcasted_iota(jnp.int32, (POINTS, count), 0) == place).astype(f32).astype(bf16)
    return jnp.dot(split, one_hot, preferred_element_type=f32).astype(bf16)


def chosen_rows(split_t, place):
    count = place.shape[0]
    one_hot = (lax.broadcasted_iota(jnp.int32, (count, POINTS), 1) == place).astype(f32).astype(bf16)
    return jnp.dot(one_hot, split_t, preferred_element_type=f32).astype(bf16)


def dot(a, b):
    return jnp.dot(a, b, preferred_element_type=f32)


def sigmoid(a):
    return 0.5 * jnp.tanh(0.5 * a) + 0.5


def window(x_ref, before_ref, after_ref, task, blocks, cols):
    lane, block = task
    start = (lane * blocks + block) * ROWS
    halo = slice(lane * EDGE, (lane + 1) * EDGE)
    if block == 0:
        return jnp.concatenate([before_ref[halo, cols], x_ref[start : start + ROWS + EDGE, cols]])
    if block == blocks - 1:
        return jnp.concatenate([x_ref[start - EDGE : start + ROWS, cols], after_ref[halo, cols]])
    return x_ref[start - EDGE : start + ROWS + EDGE, cols]


def forward_kernel(tasks, blocks, meta_ref, lengths_ref, x_ref, before_ref, after_ref, split_ref, split_t_ref, spec_ref,
                   *rest):
    outs, (turned_ref, conv, sw, normed_all, istd, sems) = rest[-9:-6], rest[-6:]
    channels = x_ref.shape[1]
    gain, bias = spec_ref[3 * BINS : 3 * BINS + 1], spec_ref[3 * BINS + 1 : 3 * BINS + 2]
    strip, width = 16, channels
    bases, copies = [], []
    for lane, block in tasks:
        first = meta_ref[0] + (block * ROWS - EDGE)
        into = chosen_columns(split_ref[...], gapped(lengths_ref, lane, first, (1, WINDOW), 1, 0))
        back = chosen_rows(split_t_ref[...], gapped(lengths_ref, lane, first, (ROWS, 1), 0, EDGE))
        bases.append((into, jnp.concatenate([back[:, :POINTS], back[:, POINTS:]])))

    def transform(task):
        into, back = bases[task]
        for at in range(0, channels, width):
            cols = slice(at, at + width)
            pair = dot(into, window(x_ref, before_ref, after_ref, tasks[task], blocks, cols))
            real, imag = pair[:BINS] + pair[POINTS : POINTS + BINS], pair[BINS:POINTS] + pair[POINTS + BINS :]
            p, q, other = spec_ref[:BINS, cols], spec_ref[BINS:POINTS, cols], spec_ref[POINTS : 3 * BINS, cols]
            zed = jnp.concatenate([real * p + imag * q, imag * other - real * q]).astype(bf16)
            pair = dot(back, zed)
            conv[task, :, cols] = pair[:ROWS] + pair[ROWS:]

    def normalise(task):
        for at in range(0, ROWS, strip):
            place = slice(task * ROWS + at, task * ROWS + at + strip)
            value = conv[task, at : at + strip]
            centred = value - jnp.sum(value, axis=1, keepdims=True) * (1.0 / channels)
            variance = jnp.sum(centred * centred, axis=1, keepdims=True) * (1.0 / channels)
            inv_std = lax.rsqrt(variance + EPSILON)
            normed = centred * inv_std
            affine = normed * gain + bias
            sw[place] = (affine * sigmoid(affine)).astype(bf16)
            normed_all[place] = normed.astype(bf16)
            istd[place] = jnp.broadcast_to(inv_std, (strip, istd.shape[1]))
        own = slice(task * ROWS, (task + 1) * ROWS)
        turned_ref[:, own] = sw[own].T
        lane, block = tasks[task]
        for k, (source, target) in enumerate(zip((sw, normed_all, istd), outs)):
            size = ROWS
            copy = pltpu.make_async_copy(
                source.at[pl.ds(task * size, size)],
                target.at[pl.ds((lane * blocks + block) * size, size)],
                sems.at[task, k],
            )
            copy.start()
            copies.append(copy)

    for task in range(len(tasks) + 1):
        if task < len(tasks):
            transform(task)
        if task > 0:
            normalise(task - 1)
    for copy in copies:
        copy.wait()


def backward_kernel(lane, blocks, meta_ref, lengths_ref, cot_ref, normed_ref, istd_ref, x_ref, before_ref, after_ref, w_ref,
                    split_ref, split_t_ref, spec_ref, gather_ref, carry_ref, *rest):
    gi_out, edge_ref, small_ref, gs, g, gi, sums, sems = rest[-8:]
    channels = cot_ref.shape[1]
    length = blocks * ROWS
    begin = lane * length
    gain, bias = spec_ref[3 * BINS : 3 * BINS + 1], spec_ref[3 * BINS + 1 : 3 * BINS + 2]
    strip, width = 16, channels // 2
    bases, copies, seen = [], [], []
    for block in range(blocks):
        first = meta_ref[0] + (block * ROWS - EDGE)
        seen.append(chosen_columns(split_ref[:POINTS], gapped(lengths_ref, lane, first, (1, WINDOW), 1, 0)))
        into = chosen_columns(split_ref[...], gapped(lengths_ref, lane, first, (1, ROWS), 1, EDGE))
        into = jnp.concatenate([into[:POINTS], into[POINTS:]], axis=1)
        back = chosen_rows(split_t_ref[...], gapped(lengths_ref, lane, first, (WINDOW, 1), 0, 0))
        bases.append((into, jnp.concatenate([back[:, :POINTS], back[:, POINTS:]])))
    sums[...] = jnp.zeros_like(sums)
    gs[...] = lax.dot_general(
        cot_ref[begin : begin + length], w_ref[...], (((1,), (1,)), ((), ())), preferred_element_type=f32
    )
    for at in range(0, length, strip):
        place = slice(begin + at, begin + at + strip)
        normed = normed_ref[place].astype(f32)
        affine = normed * gain + bias
        gate = sigmoid(affine)
        grad = gs[at : at + strip] * gate * (1.0 + affine * (1.0 - gate))
        prod = grad * normed
        sums[:8] += prod[:8] + prod[8:]
        sums[8:] += grad[:8] + grad[8:]
        grad_normed = grad * gain
        mean = jnp.sum(grad_normed, axis=1, keepdims=True) * (1.0 / channels)
        along = jnp.sum(grad_normed * normed, axis=1, keepdims=True) * (1.0 / channels)
        out = (istd_ref[place, :1] * (grad_normed - mean - normed * along)).astype(bf16)
        row = at // ROWS * 2 * ROWS + at % ROWS
        g[row : row + strip] = out
        g[row + ROWS : row + ROWS + strip] = out
    table_high, table_low = halves(gather_ref[...])
    for at in range(0, channels, width):
        cols = slice(at, at + width)
        p, q, other = spec_ref[:BINS, cols], spec_ref[BINS:POINTS, cols], spec_ref[POINTS : 3 * BINS, cols]
        cross, pending, tail = None, None, None
        for block in range(blocks):
            into, back = bases[block]
            ghat = dot(into, g[block * 2 * ROWS : (block + 1) * 2 * ROWS, cols])
            cg, sg = ghat[:BINS], ghat[BINS:]
            rows = window(x_ref, before_ref, after_ref, (lane, block), blocks, cols)
            xhat = dot(seen[block], rows)
            cx, sx = xhat[:BINS], xhat[BINS:]
            terms = (cg * cx, sg * sx, sg * cx - cg * sx)
            cross = terms if cross is None else tuple(a + b for a, b in zip(cross, terms))
            vee = jnp.concatenate([cg * p - sg * q, sg * other + cg * q]).astype(bf16)
            pair = dot(back, vee)
            part = pair[:WINDOW] + pair[WINDOW:]
            head, out, base = part[:EDGE], part[EDGE : EDGE + ROWS], block * ROWS
            if block == 0:
                edge_ref[:EDGE, cols] = head.astype(bf16)
                gi[:EDGE, cols] = out[:EDGE].astype(bf16)
            else:
                gi[base - EDGE : base, cols] = (pending + head).astype(bf16)
                gi[base : base + EDGE, cols] = (out[:EDGE] + tail).astype(bf16)
            gi[base + EDGE : base + ROWS - EDGE, cols] = out[EDGE : ROWS - EDGE].astype(bf16)
            pending, tail = out[ROWS - EDGE :], part[EDGE + ROWS :]
        gi[length - EDGE :, cols] = pending.astype(bf16)
        edge_ref[EDGE:, cols] = tail.astype(bf16)
        copy = pltpu.make_async_copy(gi.at[:, cols], gi_out.at[pl.ds(begin, length), cols], sems.at[at // width])
        copy.start()
        copies.append(copy)
        high, low = halves(jnp.concatenate(cross))
        value = dot(table_high, high) + dot(table_low, high) + dot(table_high, low)
        small_ref[:32, cols] = value + carry_ref[:32, cols]
    prod, grad = sums[:8], sums[8:]
    small_ref[32:] = carry_ref[32:] + jnp.concatenate(
        [
            jnp.sum(prod, axis=0, keepdims=True),
            jnp.sum(grad, axis=0, keepdims=True),
            jnp.zeros((14, channels), f32),
        ]
    )
    for copy in copies:
        copy.wait()


def layer_kernel(gate_ref, sw_ref, w_ref, *rest):
    rest[-1][...] = dot(sw_ref[...], w_ref[...]).astype(bf16)


def halves(value):
    high = value.astype(bf16)
    return high, (value - high.astype(f32)).astype(bf16)


def spectrum_kernel(*refs):
    sources, spec_ref, targets, sems = refs[:4], refs[4], refs[5:9], refs[9]
    copies = [pltpu.make_async_copy(a, b, sems.at[k]) for k, (a, b) in enumerate(zip(sources, targets))]
    for copy in copies:
        copy.start()
    for copy in copies:
        copy.wait()
    table_ref, kernel_ref, gain_ref, bias_ref = targets
    channels = kernel_ref.shape[1]
    table_high, table_low = halves(table_ref[...])
    taps = jnp.concatenate([kernel_ref[...], jnp.zeros((32 - TAPS, channels), f32)])
    high, low = halves(taps)
    spec_ref[: 3 * BINS] = dot(table_high, high) + dot(table_low, high) + dot(table_high, low)
    spec_ref[3 * BINS :] = jnp.concatenate(
        [gain_ref[...].reshape(1, channels), bias_ref[...].reshape(1, channels), jnp.zeros((6, channels), f32)]
    )


def frame_rows(cot_ref, target, cols, blocks, edges, sems):
    length = blocks * ROWS
    if edges:
        spans = [(k * length + b * ROWS, ROWS) for k in range(cot_ref.shape[0] // length) for b in (0, blocks - 1)]
    else:
        spans = [(k * length + ROWS, length - 2 * ROWS) for k in range(cot_ref.shape[0] // length)]
    copies, at = [], 0
    for k, (start, size) in enumerate(spans):
        source = cot_ref.at[pl.ds(start, size), cols]
        copies.append(pltpu.make_async_copy(source, target.at[pl.ds(at, size)], sems.at[k]))
        at += size
    return copies


def outer_kernel(blocks, meta_ref, inner_ref, edge_ref, other_ref, cot_ref, cot_other_ref, acc_ref, left, right, sems):
    share, width = acc_ref.shape[0] // 4, acc_ref.shape[1]
    cols = pl.ds(pl.multiple_of(meta_ref[1] * width, width), width)
    loads = []
    for k, (source, cot, edges) in enumerate(
        ((inner_ref, cot_ref, False), (edge_ref, cot_ref, True), (other_ref, cot_other_ref, False))
    ):
        copies = [pltpu.make_async_copy(source, left.at[k], sems.at[k, 4])]
        copies += frame_rows(cot, right.at[k], cols, blocks, edges, sems.at[k])
        for copy in copies:
            copy.start()
        loads.append(copies)
    for k, copies in enumerate(loads):
        for copy in copies:
            copy.wait()
        for at in range(4):
            part = slice(at * share, (at + 1) * share)
            value = dot(left[k, part], right[k])
            acc_ref[part] = value if k == 0 else acc_ref[part] + value


def last_outer_kernel(blocks, meta_ref, acc_ref, sw_ref, cot_ref, own_ref, one_ref, two_ref, three_ref, chunks, left,
                      right, sems):
    share, width = acc_ref.shape[0] // 4, acc_ref.shape[1]
    piece = share // 4
    cols = pl.ds(pl.multiple_of(meta_ref[1] * width, width), width)
    copies = frame_rows(cot_ref, right, cols, blocks, True, sems)
    for at in range(4):
        rows = pl.ds(at * share, share)
        copies.append(pltpu.make_async_copy(sw_ref.at[rows], left.at[rows], sems.at[4 + at]))
    for copy in copies:
        copy.start()
    for copy in copies[:-4]:
        copy.wait()
    for at in range(4):
        part = slice(at * share, (at + 1) * share)
        copies[at - 4].wait()
        value = (acc_ref[part] + dot(left[part], right[...])).astype(bf16)
        for k in range(4):
            shift = lax.rem(k + 4 - meta_ref[2], 4)
            chunks[shift, at * piece : (at + 1) * piece] = value[k * piece : (k + 1) * piece]
    copies = [
        pltpu.make_async_copy(chunks.at[1 + k], ref, sems.at[k]) for k, ref in enumerate((one_ref, two_ref, three_ref))
    ]
    for copy in copies:
        copy.start()
    own_ref[...] = chunks[0]
    for copy in copies:
        copy.wait()


def first_sum_kernel(meta_ref, a_ref, b_ref, c_ref, d_ref, small_ref, away_ref, *rest):
    ends, (own_ref, own_small_ref, one_ref, two_ref, three_ref) = rest[:-5], rest[-5:]
    piece, width = own_ref.shape
    cols = pl.ds(pl.multiple_of(meta_ref[1] * width, width), width)
    half = own_small_ref.shape[0]
    small = (small_ref[:, cols] + away_ref[:, cols]).astype(bf16)
    own_small_ref[...] = small
    for shift, ref in enumerate((own_ref, one_ref, two_ref, three_ref)):
        rows = pl.ds(pl.multiple_of(lax.rem(meta_ref[3] + shift, 4) * piece, piece), piece)
        value = (a_ref[rows].astype(f32) + c_ref[rows].astype(f32)) + (b_ref[rows].astype(f32) + d_ref[rows].astype(f32))
        ref[:piece] = value.astype(ref.dtype)
        if shift > 0:
            ref[piece : piece + half] = small
    for ref, begin in ((one_ref, EDGE), (three_ref, 0)):
        at = piece + half
        for side in range(2):
            for end in ends:
                ref[at : at + EDGE] = end[begin : begin + EDGE, side * width : (side + 1) * width]
                at += EDGE


def place_kernel(scale, meta_ref, *refs):
    out_ref, taps_ref, gain_ref, bias_ref = refs[-4:]
    width = refs[0].shape[1]
    piece = out_ref.shape[0] // 4
    small = []
    for side in range(2):
        core = meta_ref[1] if side == 0 else 1 - meta_ref[1]
        place = meta_ref[4] if side == 0 else meta_ref[5]
        cols = pl.ds(pl.multiple_of(core * width, width), width)
        got = refs[side * 4 : side * 4 + 4]
        for shift in range(4):
            rows = pl.ds(pl.multiple_of(lax.rem(place + 4 - shift, 4) * piece, piece), piece)
            out_ref[rows, cols] = got[shift][:piece].astype(f32) * scale
        small.append(four(*(ref[piece:] for ref in got)) * scale)
    first = meta_ref[1] == 0
    for side in range(2):
        cols = slice(side * width, (side + 1) * width)
        value = jnp.where(first == (side == 0), small[0], small[1])
        taps_ref[:, cols] = value[:TAPS]
        gain_ref[cols] = value[32]
        bias_ref[cols] = value[33]


def whole(shape):
    return pl.BlockSpec(shape, lambda *i: (0,) * len(shape))


SMEM = pl.BlockSpec(memory_space=pltpu.SMEM)
HBM = pl.BlockSpec(memory_space=pltpu.HBM)
ANY = pl.BlockSpec(memory_space=pl.ANY)
VMEM = pl.BlockSpec(memory_space=pltpu.VMEM)


def params(mebibytes):
    return pltpu.CompilerParams(vmem_limit_bytes=mebibytes << 20)


def cost(flops, moved):
    return pl.CostEstimate(flops=flops, bytes_accessed=moved, transcendentals=0)


def near(*arrays):
    return [pltpu.with_memory_space_constraint(a, pltpu.VMEM) for a in arrays]


def forward(tasks, meta, lengths, flat, before, after, split, split_t, spec, kept, name, interpret=False):
    total, channels = flat.shape
    blocks = total // lengths.shape[0] // ROWS
    count = len(tasks)
    rows = count * ROWS
    return pl.pallas_call(
        functools.partial(forward_kernel, tasks, blocks),
        in_specs=[SMEM, SMEM] + [VMEM] * 6 + [HBM] * len(kept),
        out_specs=[HBM] * 3 + [VMEM],
        out_shape=[
            pltpu.HBM((total, channels), bf16),
            pltpu.HBM((total, channels), bf16),
            pltpu.HBM((total, 128), f32),
            pltpu.HBM((channels, rows), bf16),
        ],
        scratch_shapes=[
            pltpu.VMEM((count, ROWS, channels), f32),
            pltpu.VMEM((rows, channels), bf16),
            pltpu.VMEM((rows, channels), bf16),
            pltpu.VMEM((rows, 128), f32),
            pltpu.SemaphoreType.DMA((count, 3)),
        ],
        input_output_aliases={8 + k: k for k in range(len(kept))},
        compiler_params=params(32),
        cost_estimate=cost(9_000_000_000, rows * channels * 12),
        interpret=interpret,
        name=name,
    )(meta, lengths, *near(flat, before, after, split, split_t, spec), *kept)


def backward(lane, meta, lengths, cot, normed, istd, x, before, after, w, split, split_t, spec, gather, carry, gi, interpret=False):
    total, channels = cot.shape
    length = total // lengths.shape[0]
    blocks = length // ROWS
    kept = [] if gi is None else [gi]
    return pl.pallas_call(
        functools.partial(backward_kernel, lane, blocks),
        in_specs=[SMEM, SMEM] + [VMEM] * 12 + [HBM] * len(kept),
        out_specs=[HBM, VMEM, VMEM],
        out_shape=[
            pltpu.HBM((total, channels), bf16),
            jax.ShapeDtypeStruct((2 * EDGE, channels), bf16),
            jax.ShapeDtypeStruct((48, channels), f32),
        ],
        scratch_shapes=[
            pltpu.VMEM((length, channels), f32),
            pltpu.VMEM((2 * length, channels), bf16),
            pltpu.VMEM((length, channels), bf16),
            pltpu.VMEM((16, channels), f32),
            pltpu.SemaphoreType.DMA((3,)),
        ],
        input_output_aliases={14: 0} if kept else {},
        compiler_params=params(24),
        cost_estimate=cost(12_000_000_000, length * channels * 20),
        interpret=interpret,
        name=f"backward_{lane}",
    )(meta, lengths, *near(cot, normed, istd, x, before, after, w, split, split_t, spec, gather, carry), *kept)


def project(lane, lanes, gate, sw, w, layer, interpret=False):
    total, channels = sw.shape
    rows = 2 * ROWS
    steps = total // lanes // rows
    row = pl.BlockSpec((rows, channels), lambda i: (lane * steps + i, 0))
    kept = [] if layer is None else [layer]
    return pl.pallas_call(
        layer_kernel,
        grid=(steps,),
        in_specs=[ANY, row, VMEM] + [HBM] * len(kept),
        out_specs=row,
        out_shape=pltpu.HBM((total, channels), bf16),
        input_output_aliases={3: 0} if kept else {},
        compiler_params=params(24),
        cost_estimate=cost(2 * total // lanes * channels * channels, 4 * total * channels),
        interpret=interpret,
        name=f"layer_out_{lane}",
    )(gate, sw, *near(w), *kept)


def outer(meta, inner, edge, other, cot, cot_other, blocks):
    channels, rows = inner.shape
    width = channels // 2
    return pl.pallas_call(
        functools.partial(outer_kernel, blocks),
        in_specs=[SMEM] + [HBM] * 2 + [ANY, HBM, ANY],
        out_specs=VMEM,
        out_shape=pltpu.VMEM((channels, width), f32),
        scratch_shapes=[
            pltpu.VMEM((3, channels, rows), bf16),
            pltpu.VMEM((3, rows, width), bf16),
            pltpu.SemaphoreType.DMA((3, 5)),
        ],
        compiler_params=params(16),
        cost_estimate=cost(6_000_000_000, 10 * rows * channels),
        name="outer_most",
    )(meta, inner, edge, other, cot, cot_other)


def last_outer(meta, acc, other, cot_other, blocks):
    channels, rows = other.shape
    width, share = channels // 2, channels // 4
    return pl.pallas_call(
        functools.partial(last_outer_kernel, blocks),
        in_specs=[SMEM, VMEM] + [ANY] * 2,
        out_specs=[VMEM] + [HBM] * 3,
        out_shape=[pltpu.VMEM((share, width), bf16)] + [pltpu.HBM((share, width), bf16)] * 3,
        scratch_shapes=[
            pltpu.VMEM((4, share, width), bf16),
            pltpu.VMEM((channels, rows), bf16),
            pltpu.VMEM((rows, width), bf16),
            pltpu.SemaphoreType.DMA((8,)),
        ],
        compiler_params=params(16),
        cost_estimate=cost(3_000_000_000, 10 * rows * channels),
        name="outer_last",
    )(meta, *near(acc), other, cot_other)


def first_sum(meta, parts, small, away, ends):
    share, width = parts[0].shape
    piece = share // 4
    tall = piece + small.shape[0]
    edges = 2 * EDGE * len(ends)
    return pl.pallas_call(
        first_sum_kernel,
        in_specs=[SMEM] + [VMEM] * (6 + len(ends)),
        out_specs=[VMEM] * 5,
        out_shape=[
            jax.ShapeDtypeStruct((piece, width), f32),
            jax.ShapeDtypeStruct((tall - piece, width), bf16),
            pltpu.HBM((tall + edges, width), bf16),
            pltpu.HBM((tall, width), bf16),
            pltpu.HBM((tall + edges, width), bf16),
        ],
        compiler_params=params(12),
        name="sum_first",
    )(meta, *parts, small, away, *ends)


def place(meta, got, share, scale):
    width = got[0].shape[1]
    return pl.pallas_call(
        functools.partial(place_kernel, scale),
        in_specs=[SMEM] + [VMEM] * 8,
        out_specs=[VMEM] * 4,
        out_shape=[
            jax.ShapeDtypeStruct((share, 2 * width), f32),
            jax.ShapeDtypeStruct((TAPS, 2 * width), f32),
            jax.ShapeDtypeStruct((2 * width,), f32),
            jax.ShapeDtypeStruct((2 * width,), f32),
        ],
        compiler_params=params(12),
        name="place",
    )(meta, *got)


def shifts(size):
    up = [(i, i + 1) for i in range(size - 1)]
    return up, [(j, i) for i, j in up]


EVERY = ("dp", "seq")


def along(axes, shift):
    pairs = []
    for device in range(128):
        where = {"y": device % 4, "c": device // 4 % 2, "x": device // 8 % 4, "z": device // 32}
        axis = axes[where["c"]]
        moved = dict(where)
        moved[axis] = (where[axis] + shift) % (2 if axis == "c" else 4)
        pairs.append((device, ((moved["z"] * 4 + moved["x"]) * 2 + moved["c"]) * 4 + moved["y"]))
    return pairs


def swap(value):
    return lax.ppermute(value, EVERY, along("cc", 1))


def spread(values, axes):
    return [lax.ppermute(value, EVERY, along(axes, s + 1)) for s, value in enumerate(values)]


def four(own, one, two, three):
    own, one, two, three = (v.astype(f32) for v in (own, one, two, three))
    return (own + two) + (one + three)


def all_four(value, axes):
    return four(value, *spread([value] * 3, axes))


def local(glu_out, lengths, kernel, norm_gain, norm_bias, w_out, cotangent, interpret=False):
    lanes, length, channels = glu_out.shape
    seq_count = lax.axis_size("seq")
    norm_scale = 1.0 / math.sqrt(lanes * lax.axis_size("dp") * length * seq_count)
    y = lax.axis_index("seq")
    dp = lax.axis_index("dp")
    core, x, z = lax.rem(dp, 2), lax.rem(lax.div(dp, 2), 4), lax.div(dp, 8)
    first = core == 0
    meta = jnp.stack(
        [
            y * length,
            core,
            jnp.where(first, x, z),
            y,
            jnp.where(first, x, z),
            jnp.where(first, z, x),
        ]
    ).astype(jnp.int32)
    up, down = shifts(seq_count)
    before = lax.ppermute(glu_out[:, length - EDGE :], "seq", up).reshape(lanes * EDGE, channels)
    after = lax.ppermute(glu_out[:, :EDGE], "seq", down).reshape(lanes * EDGE, channels)
    cot = cotangent.reshape(-1, channels)
    split, split_t, wide, deep = (jnp.asarray(t) for t in tables())
    spec = pl.pallas_call(
        spectrum_kernel,
        in_specs=[HBM] * 4,
        out_specs=VMEM,
        out_shape=pltpu.VMEM((3 * BINS + 8, channels), f32),
        scratch_shapes=[pltpu.VMEM(a.shape, f32) for a in (wide, kernel, norm_gain, norm_bias)]
        + [pltpu.SemaphoreType.DMA((4,))],
        compiler_params=params(12),
        interpret=interpret,
        name="spectrum",
    )(wide, kernel, norm_gain, norm_bias)
    flat = glu_out.reshape(lanes * length, channels)
    blocks = length // ROWS
    inner = [(lane, block) for lane in range(lanes) for block in range(1, blocks - 1)]
    edge = [(lane, block) for lane in range(lanes) for block in (0, blocks - 1)]
    none = jnp.zeros((lanes * EDGE, channels), bf16)
    kept, turned_inner = (lambda *o: (o[:3], o[3]))(
        *forward(inner, meta, lengths, flat, none, none, split, split_t, spec, (), "conv_inner", interpret=interpret)
    )
    kept, turned_edge = (lambda *o: (o[:3], o[3]))(
        *forward(edge, meta, lengths, flat, before, after, split, split_t, spec, kept, "conv_edge", interpret=interpret)
    )
    sw, normed, istd = kept
    share, half = channels // seq_count, channels // 2
    whole_slice = lax.axis_size("dp") == 32
    if whole_slice:
        cot_other = swap(cot)
        acc = outer(meta, turned_inner, turned_edge, swap(turned_inner), cot, cot_other, blocks)
        parts = list(last_outer(meta, acc, swap(turned_edge), cot_other, blocks))
        sent = spread(parts[1:], "xz")
        cot, parts[0] = lax.optimization_barrier((cot, parts[0]))
    else:
        places = [jnp.concatenate([cot[(a * blocks + b) * ROWS :][:ROWS] for a, b in t]) for t in (inner, edge)]
        grad_w = lax.psum(dot(turned_inner, places[0]) + dot(turned_edge, places[1]), "seq") * norm_scale
        grad_w = lax.dynamic_slice_in_dim(grad_w, y * share, share, 0)
    small, gi, ends = jnp.zeros((48, channels), f32), None, []
    for lane in range(lanes):
        gi, end, small = backward(
            lane, meta, lengths, cot, normed, istd, flat, before, after, w_out, split, split_t, spec, deep, small, gi,
            interpret=interpret,
        )
        ends.append(end)
    if whole_slice:
        piece, extra, *sent = first_sum(meta, [parts[0]] + sent, small, swap(small), ends)
        layer = project(0, lanes, extra, sw, w_out, None)
        one, two, three = spread(sent, "yy")
        three, layer = lax.optimization_barrier((three, layer))
        rows = piece.shape[0]
        tall = rows + extra.shape[0]
        piece = four(piece, *(v[:rows] for v in (one, two, three))).astype(bf16)
        extra = four(extra, one[rows:tall], two[rows:tall], three[rows:tall]).astype(bf16)
        after_tail, before_head = (jnp.concatenate(jnp.split(v[tall:], 2), axis=1) for v in (three, one))
        sent = jnp.concatenate([piece, extra])
        layer = project(1, lanes, sent, sw, w_out, layer)
        got = [sent] + spread([sent] * 3, "zx")
        got[3], layer = lax.optimization_barrier((got[3], layer))
        sent = four(*got).astype(bf16)
        got = [sent] + spread([sent] * 3, "xz")
        grad_w, taps, gain, bias = place(meta, got + [swap(v) for v in got], share, norm_scale)
    else:
        layer = None
        for lane in range(lanes):
            layer = project(lane, lanes, sw, sw, w_out, layer, interpret=interpret)
        heads = jnp.concatenate([e[:EDGE] for e in ends])
        tails = jnp.concatenate([e[EDGE:] for e in ends])
        before_head, after_tail = lax.ppermute(tails, "seq", up), lax.ppermute(heads, "seq", down)
        small = lax.psum(small, "seq") * norm_scale
        taps, gain, bias = small[:TAPS], small[32], small[33]
    before = jnp.where(y == 0, 0.0, before_head.astype(f32)).astype(bf16).reshape(lanes, EDGE, channels)
    after = jnp.where(y == seq_count - 1, 0.0, after_tail.astype(f32)).astype(bf16).reshape(lanes, EDGE, channels)
    gi = gi.reshape(lanes, length, channels)
    gi = gi.at[:, :EDGE].add(before).at[:, length - EDGE :].add(after)
    return (layer.reshape(lanes, length, channels), gi, grad_w, taps, gain, bias)


def solution(mesh):
    in_specs = (P("dp", "seq", None), P("dp", None), P(), P(), P(), P(), P("dp", "seq", None))
    out_specs = (P("dp", "seq", None), P("dp", "seq", None), P("seq", None), P(), P(), P())
    return jax.shard_map(local, mesh=mesh, in_specs=in_specs, out_specs=out_specs, check_vma=False)
```

```python
import functools
import math

import jax
import jax.numpy as jnp
import numpy as np
from jax import lax
from jax.experimental import pallas as pl
from jax.experimental.pallas import tpu as pltpu
from jax.sharding import PartitionSpec as P

EPSILON = 1e-05
TAPS = 31
HALF = TAPS // 2
ROWS = 128
EDGE = 16
WINDOW = ROWS + 2 * EDGE
POINTS = 256
BINS = POINTS // 2
f32, bf16 = jnp.float32, jnp.bfloat16


def tables():
    place = np.arange(POINTS)
    bins = np.arange(BINS)[:, None]
    cosines = math.sqrt(2.0 / POINTS) * np.cos(2 * np.pi * ((bins * place) % POINTS) / POINTS)
    sines = math.sqrt(2.0 / POINTS) * np.sin(2 * np.pi * ((bins * place) % POINTS) / POINTS)
    cosines[0] = 1.0 / math.sqrt(POINTS)
    sines[0] = (1.0 - 2.0 * (place % 2)) / math.sqrt(POINTS)
    basis = np.concatenate([cosines, sines])
    high = basis.astype(jnp.bfloat16)
    low = (basis - high.astype(np.float64)).astype(jnp.bfloat16)
    split = np.concatenate([high, low])
    lags = np.arange(TAPS) - HALF
    turn = 2 * np.pi * ((bins * lags) % POINTS) / POINTS
    real, imag = np.cos(turn), np.sin(turn)
    other = real.copy()
    other[0] = 1.0 - 2.0 * (np.abs(lags) % 2)
    spectrum = np.concatenate([real, imag, other]).astype(np.float32)
    gather = np.concatenate([real, other, -imag]).astype(np.float32)
    wide, deep = np.zeros((3 * BINS, 32), np.float32), np.zeros((32, 3 * BINS), np.float32)
    wide[:, :TAPS], deep[:TAPS] = spectrum, gather.T
    return split, np.ascontiguousarray(split.T), wide, deep


def gapped(lengths_ref, lane, first, shape, dim, skip):
    row = lax.broadcasted_iota(jnp.int32, shape, dim) + skip
    frame = first + row
    place, end = row, 0
    for utter in range(lengths_ref.shape[1] - 1):
        end = end + lengths_ref[lane, utter]
        place = place + jnp.where(frame >= end, jnp.where(first < end, HALF, 0), 0)
    return place


def chosen_columns(split, place):
    count = place.shape[1]
    one_hot = (lax.broadcasted_iota(jnp.int32, (POINTS, count), 0) == place).astype(f32).astype(bf16)
    return jnp.dot(split, one_hot, preferred_element_type=f32).astype(bf16)


def chosen_rows(split_t, place):
    count = place.shape[0]
    one_hot = (lax.broadcasted_iota(jnp.int32, (count, POINTS), 1) == place).astype(f32).astype(bf16)
    return jnp.dot(one_hot, split_t, preferred_element_type=f32).astype(bf16)


def dot(a, b):
    return jnp.dot(a, b, preferred_element_type=f32)


def sigmoid(a):
    return 0.5 * jnp.tanh(0.5 * a) + 0.5


def window(x_ref, before_ref, after_ref, task, blocks, cols):
    lane, block = task
    start = (lane * blocks + block) * ROWS
    halo = slice(lane * EDGE, (lane + 1) * EDGE)
    if block == 0:
        return jnp.concatenate([before_ref[halo, cols], x_ref[start : start + ROWS + EDGE, cols]])
    if block == blocks - 1:
        return jnp.concatenate([x_ref[start - EDGE : start + ROWS, cols], after_ref[halo, cols]])
    return x_ref[start - EDGE : start + ROWS + EDGE, cols]


def forward_kernel(tasks, blocks, meta_ref, lengths_ref, x_ref, before_ref, after_ref, split_ref, split_t_ref, spec_ref,
                   *rest):
    outs, (turned_ref, conv, sw, normed_all, istd, sems) = rest[-9:-6], rest[-6:]
    channels = x_ref.shape[1]
    gain, bias = spec_ref[3 * BINS : 3 * BINS + 1], spec_ref[3 * BINS + 1 : 3 * BINS + 2]
    strip, width = 16, channels
    bases, copies = [], []
    for lane, block in tasks:
        first = meta_ref[0] + (block * ROWS - EDGE)
        into = chosen_columns(split_ref[...], gapped(lengths_ref, lane, first, (1, WINDOW), 1, 0))
        back = chosen_rows(split_t_ref[...], gapped(lengths_ref, lane, first, (ROWS, 1), 0, EDGE))
        bases.append((into, jnp.concatenate([back[:, :POINTS], back[:, POINTS:]])))

    def transform(task):
        into, back = bases[task]
        for at in range(0, channels, width):
            cols = slice(at, at + width)
            pair = dot(into, window(x_ref, before_ref, after_ref, tasks[task], blocks, cols))
            real, imag = pair[:BINS] + pair[POINTS : POINTS + BINS], pair[BINS:POINTS] + pair[POINTS + BINS :]
            p, q, other = spec_ref[:BINS, cols], spec_ref[BINS:POINTS, cols], spec_ref[POINTS : 3 * BINS, cols]
            zed = jnp.concatenate([real * p + imag * q, imag * other - real * q]).astype(bf16)
            pair = dot(back, zed)
            conv[task, :, cols] = pair[:ROWS] + pair[ROWS:]

    def normalise(task):
        for at in range(0, ROWS, strip):
            place = slice(task * ROWS + at, task * ROWS + at + strip)
            value = conv[task, at : at + strip]
            centred = value - jnp.sum(value, axis=1, keepdims=True) * (1.0 / channels)
            variance = jnp.sum(centred * centred, axis=1, keepdims=True) * (1.0 / channels)
            inv_std = lax.rsqrt(variance + EPSILON)
            normed = centred * inv_std
            affine = normed * gain + bias
            sw[place] = (affine * sigmoid(affine)).astype(bf16)
            normed_all[place] = normed.astype(bf16)
            istd[place] = jnp.broadcast_to(inv_std, (strip, istd.shape[1]))
        own = slice(task * ROWS, (task + 1) * ROWS)
        turned_ref[:, own] = sw[own].T
        lane, block = tasks[task]
        for k, (source, target) in enumerate(zip((sw, normed_all, istd), outs)):
            size = ROWS
            copy = pltpu.make_async_copy(
                source.at[pl.ds(task * size, size)],
                target.at[pl.ds((lane * blocks + block) * size, size)],
                sems.at[task, k],
            )
            copy.start()
            copies.append(copy)

    for task in range(len(tasks) + 1):
        if task < len(tasks):
            transform(task)
        if task > 0:
            normalise(task - 1)
    for copy in copies:
        copy.wait()


def backward_kernel(lane, blocks, meta_ref, lengths_ref, cot_ref, normed_ref, istd_ref, x_ref, before_ref, after_ref, w_ref,
                    split_ref, split_t_ref, spec_ref, gather_ref, carry_ref, *rest):
    gi_out, edge_ref, small_ref, gs, g, gi, sums, sems = rest[-8:]
    channels = cot_ref.shape[1]
    length = blocks * ROWS
    begin = lane * length
    gain, bias = spec_ref[3 * BINS : 3 * BINS + 1], spec_ref[3 * BINS + 1 : 3 * BINS + 2]
    strip, width = 16, channels // 2
    bases, copies, seen = [], [], []
    for block in range(blocks):
        first = meta_ref[0] + (block * ROWS - EDGE)
        seen.append(chosen_columns(split_ref[:POINTS], gapped(lengths_ref, lane, first, (1, WINDOW), 1, 0)))
        into = chosen_columns(split_ref[...], gapped(lengths_ref, lane, first, (1, ROWS), 1, EDGE))
        into = jnp.concatenate([into[:POINTS], into[POINTS:]], axis=1)
        back = chosen_rows(split_t_ref[...], gapped(lengths_ref, lane, first, (WINDOW, 1), 0, 0))
        bases.append((into, jnp.concatenate([back[:, :POINTS], back[:, POINTS:]])))
    sums[...] = jnp.zeros_like(sums)
    gs[...] = lax.dot_general(
        cot_ref[begin : begin + length], w_ref[...], (((1,), (1,)), ((), ())), preferred_element_type=f32
    )
    for at in range(0, length, strip):
        place = slice(begin + at, begin + at + strip)
        normed = normed_ref[place].astype(f32)
        affine = normed * gain + bias
        gate = sigmoid(affine)
        grad = gs[at : at + strip] * gate * (1.0 + affine * (1.0 - gate))
        prod = grad * normed
        sums[:8] += prod[:8] + prod[8:]
        sums[8:] += grad[:8] + grad[8:]
        grad_normed = grad * gain
        mean = jnp.sum(grad_normed, axis=1, keepdims=True) * (1.0 / channels)
        along = jnp.sum(grad_normed * normed, axis=1, keepdims=True) * (1.0 / channels)
        out = (istd_ref[place, :1] * (grad_normed - mean - normed * along)).astype(bf16)
        row = at // ROWS * 2 * ROWS + at % ROWS
        g[row : row + strip] = out
        g[row + ROWS : row + ROWS + strip] = out
    table_high, table_low = halves(gather_ref[...])
    for at in range(0, channels, width):
        cols = slice(at, at + width)
        p, q, other = spec_ref[:BINS, cols], spec_ref[BINS:POINTS, cols], spec_ref[POINTS : 3 * BINS, cols]
        cross, pending, tail = None, None, None
        for block in range(blocks):
            into, back = bases[block]
            ghat = dot(into, g[block * 2 * ROWS : (block + 1) * 2 * ROWS, cols])
            cg, sg = ghat[:BINS], ghat[BINS:]
            rows = window(x_ref, before_ref, after_ref, (lane, block), blocks, cols)
            xhat = dot(seen[block], rows)
            cx, sx = xhat[:BINS], xhat[BINS:]
            terms = (cg * cx, sg * sx, sg * cx - cg * sx)
            cross = terms if cross is None else tuple(a + b for a, b in zip(cross, terms))
            vee = jnp.concatenate([cg * p - sg * q, sg * other + cg * q]).astype(bf16)
            pair = dot(back, vee)
            part = pair[:WINDOW] + pair[WINDOW:]
            head, out, base = part[:EDGE], part[EDGE : EDGE + ROWS], block * ROWS
            if block == 0:
                edge_ref[:EDGE, cols] = head.astype(bf16)
                gi[:EDGE, cols] = out[:EDGE].astype(bf16)
            else:
                gi[base - EDGE : base, cols] = (pending + head).astype(bf16)
                gi[base : base + EDGE, cols] = (out[:EDGE] + tail).astype(bf16)
            gi[base + EDGE : base + ROWS - EDGE, cols] = out[EDGE : ROWS - EDGE].astype(bf16)
            pending, tail = out[ROWS - EDGE :], part[EDGE + ROWS :]
        gi[length - EDGE :, cols] = pending.astype(bf16)
        edge_ref[EDGE:, cols] = tail.astype(bf16)
        copy = pltpu.make_async_copy(gi.at[:, cols], gi_out.at[pl.ds(begin, length), cols], sems.at[at // width])
        copy.start()
        copies.append(copy)
        high, low = halves(jnp.concatenate(cross))
        value = dot(table_high, high) + dot(table_low, high) + dot(table_high, low)
        small_ref[:32, cols] = value + carry_ref[:32, cols]
    prod, grad = sums[:8], sums[8:]
    small_ref[32:] = carry_ref[32:] + jnp.concatenate(
        [
            jnp.sum(prod, axis=0, keepdims=True),
            jnp.sum(grad, axis=0, keepdims=True),
            jnp.zeros((14, channels), f32),
        ]
    )
    for copy in copies:
        copy.wait()


def layer_kernel(gate_ref, sw_ref, w_ref, *rest):
    rest[-1][...] = dot(sw_ref[...], w_ref[...]).astype(bf16)


def halves(value):
    high = value.astype(bf16)
    return high, (value - high.astype(f32)).astype(bf16)


def spectrum_kernel(*refs):
    sources, spec_ref, targets, sems = refs[:4], refs[4], refs[5:9], refs[9]
    copies = [pltpu.make_async_copy(a, b, sems.at[k]) for k, (a, b) in enumerate(zip(sources, targets))]
    for copy in copies:
        copy.start()
    for copy in copies:
        copy.wait()
    table_ref, kernel_ref, gain_ref, bias_ref = targets
    channels = kernel_ref.shape[1]
    table_high, table_low = halves(table_ref[...])
    taps = jnp.concatenate([kernel_ref[...], jnp.zeros((32 - TAPS, channels), f32)])
    high, low = halves(taps)
    spec_ref[: 3 * BINS] = dot(table_high, high) + dot(table_low, high) + dot(table_high, low)
    spec_ref[3 * BINS :] = jnp.concatenate(
        [gain_ref[...].reshape(1, channels), bias_ref[...].reshape(1, channels), jnp.zeros((6, channels), f32)]
    )


def frame_rows(cot_ref, target, cols, blocks, edges, sems):
    length = blocks * ROWS
    if edges:
        spans = [(k * length + b * ROWS, ROWS) for k in range(cot_ref.shape[0] // length) for b in (0, blocks - 1)]
    else:
        spans = [(k * length + ROWS, length - 2 * ROWS) for k in range(cot_ref.shape[0] // length)]
    copies, at = [], 0
    for k, (start, size) in enumerate(spans):
        source = cot_ref.at[pl.ds(start, size), cols]
        copies.append(pltpu.make_async_copy(source, target.at[pl.ds(at, size)], sems.at[k]))
        at += size
    return copies


def outer_kernel(blocks, meta_ref, inner_ref, edge_ref, other_ref, cot_ref, cot_other_ref, acc_ref, left, right, sems):
    share, width = acc_ref.shape[0] // 4, acc_ref.shape[1]
    cols = pl.ds(pl.multiple_of(meta_ref[1] * width, width), width)
    loads = []
    for k, (source, cot, edges) in enumerate(
        ((inner_ref, cot_ref, False), (edge_ref, cot_ref, True), (other_ref, cot_other_ref, False))
    ):
        copies = [pltpu.make_async_copy(source, left.at[k], sems.at[k, 4])]
        copies += frame_rows(cot, right.at[k], cols, blocks, edges, sems.at[k])
        for copy in copies:
            copy.start()
        loads.append(copies)
    for k, copies in enumerate(loads):
        for copy in copies:
            copy.wait()
        for at in range(4):
            part = slice(at * share, (at + 1) * share)
            value = dot(left[k, part], right[k])
            acc_ref[part] = value if k == 0 else acc_ref[part] + value


def last_outer_kernel(blocks, meta_ref, acc_ref, sw_ref, cot_ref, own_ref, one_ref, two_ref, three_ref, chunks, left,
                      right, sems):
    share, width = acc_ref.shape[0] // 4, acc_ref.shape[1]
    piece = share // 4
    cols = pl.ds(pl.multiple_of(meta_ref[1] * width, width), width)
    copies = frame_rows(cot_ref, right, cols, blocks, True, sems)
    for at in range(4):
        rows = pl.ds(at * share, share)
        copies.append(pltpu.make_async_copy(sw_ref.at[rows], left.at[rows], sems.at[4 + at]))
    for copy in copies:
        copy.start()
    for copy in copies[:-4]:
        copy.wait()
    for at in range(4):
        part = slice(at * share, (at + 1) * share)
        copies[at - 4].wait()
        value = (acc_ref[part] + dot(left[part], right[...])).astype(bf16)
        for k in range(4):
            shift = lax.rem(k + 4 - meta_ref[2], 4)
            chunks[shift, at * piece : (at + 1) * piece] = value[k * piece : (k + 1) * piece]
    copies = [
        pltpu.make_async_copy(chunks.at[1 + k], ref, sems.at[k]) for k, ref in enumerate((one_ref, two_ref, three_ref))
    ]
    for copy in copies:
        copy.start()
    own_ref[...] = chunks[0]
    for copy in copies:
        copy.wait()


def first_sum_kernel(meta_ref, a_ref, b_ref, c_ref, d_ref, small_ref, away_ref, *rest):
    ends, outs = rest[:-4], rest[-4:]
    width = a_ref.shape[1]
    piece = a_ref.shape[0] // 4
    tall = piece + small_ref.shape[0]
    cols = pl.ds(pl.multiple_of(meta_ref[1] * width, width), width)
    small = (small_ref[:, cols] + away_ref[:, cols]).astype(bf16)
    for shift, ref in enumerate(outs):
        rows = pl.ds(pl.multiple_of(lax.rem(meta_ref[3] + shift, 4) * piece, piece), piece)
        ref[:piece] = four(a_ref[rows], b_ref[rows], c_ref[rows], d_ref[rows]).astype(bf16)
        ref[piece:tall] = small
    for ref, begin in ((outs[1], EDGE), (outs[3], 0)):
        at = tall
        for side in range(2):
            for end in ends:
                ref[at : at + EDGE] = end[begin : begin + EDGE, side * width : (side + 1) * width]
                at += EDGE


def place_kernel(scale, meta_ref, *refs):
    out_ref, taps_ref, gain_ref, bias_ref = refs[-4:]
    width = refs[0].shape[1]
    piece = out_ref.shape[0] // 4
    small = []
    for side in range(2):
        core = meta_ref[1] if side == 0 else 1 - meta_ref[1]
        place = meta_ref[4] if side == 0 else meta_ref[5]
        cols = pl.ds(pl.multiple_of(core * width, width), width)
        got = refs[side * 4 : side * 4 + 4]
        for shift in range(4):
            rows = pl.ds(pl.multiple_of(lax.rem(place + 4 - shift, 4) * piece, piece), piece)
            out_ref[rows, cols] = got[shift][:piece].astype(f32) * scale
        small.append(four(*(ref[piece:] for ref in got)) * scale)
    first = meta_ref[1] == 0
    for side in range(2):
        cols = slice(side * width, (side + 1) * width)
        value = jnp.where(first == (side == 0), small[0], small[1])
        taps_ref[:, cols] = value[:TAPS]
        gain_ref[cols] = value[32]
        bias_ref[cols] = value[33]


def whole(shape):
    return pl.BlockSpec(shape, lambda *i: (0,) * len(shape))


SMEM = pl.BlockSpec(memory_space=pltpu.SMEM)
HBM = pl.BlockSpec(memory_space=pltpu.HBM)
ANY = pl.BlockSpec(memory_space=pl.ANY)
VMEM = pl.BlockSpec(memory_space=pltpu.VMEM)


def params(mebibytes):
    return pltpu.CompilerParams(vmem_limit_bytes=mebibytes << 20)


def cost(flops, moved):
    return pl.CostEstimate(flops=flops, bytes_accessed=moved, transcendentals=0)


def near(*arrays):
    return [pltpu.with_memory_space_constraint(a, pltpu.VMEM) for a in arrays]


def far(*arrays):
    return [pltpu.with_memory_space_constraint(a, pltpu.HBM) for a in arrays]


def forward(tasks, meta, lengths, flat, before, after, split, split_t, spec, kept, name, interpret=False):
    total, channels = flat.shape
    blocks = total // lengths.shape[0] // ROWS
    count = len(tasks)
    rows = count * ROWS
    return pl.pallas_call(
        functools.partial(forward_kernel, tasks, blocks),
        in_specs=[SMEM, SMEM] + [VMEM] * 6 + [HBM] * len(kept),
        out_specs=[HBM] * 3 + [VMEM],
        out_shape=[
            pltpu.HBM((total, channels), bf16),
            pltpu.HBM((total, channels), bf16),
            pltpu.HBM((total, 128), f32),
            pltpu.HBM((channels, rows), bf16),
        ],
        scratch_shapes=[
            pltpu.VMEM((count, ROWS, channels), f32),
            pltpu.VMEM((rows, channels), bf16),
            pltpu.VMEM((rows, channels), bf16),
            pltpu.VMEM((rows, 128), f32),
            pltpu.SemaphoreType.DMA((count, 3)),
        ],
        input_output_aliases={8 + k: k for k in range(len(kept))},
        compiler_params=params(32),
        cost_estimate=cost(9_000_000_000, rows * channels * 12),
        interpret=interpret,
        name=name,
    )(meta, lengths, *near(flat, before, after, split, split_t, spec), *kept)


def backward(lane, meta, lengths, cot, normed, istd, x, before, after, w, split, split_t, spec, gather, carry, gi, interpret=False):
    total, channels = cot.shape
    length = total // lengths.shape[0]
    blocks = length // ROWS
    kept = [] if gi is None else [gi]
    return pl.pallas_call(
        functools.partial(backward_kernel, lane, blocks),
        in_specs=[SMEM, SMEM] + [VMEM] * 12 + [HBM] * len(kept),
        out_specs=[HBM, VMEM, VMEM],
        out_shape=[
            pltpu.HBM((total, channels), bf16),
            jax.ShapeDtypeStruct((2 * EDGE, channels), bf16),
            jax.ShapeDtypeStruct((48, channels), f32),
        ],
        scratch_shapes=[
            pltpu.VMEM((length, channels), f32),
            pltpu.VMEM((2 * length, channels), bf16),
            pltpu.VMEM((length, channels), bf16),
            pltpu.VMEM((16, channels), f32),
            pltpu.SemaphoreType.DMA((3,)),
        ],
        input_output_aliases={14: 0} if kept else {},
        compiler_params=params(24),
        cost_estimate=cost(12_000_000_000, length * channels * 20),
        interpret=interpret,
        name=f"backward_{lane}",
    )(meta, lengths, *near(cot, normed, istd, x, before, after, w, split, split_t, spec, gather, carry), *kept)


def project(lane, lanes, gate, sw, w, layer, interpret=False):
    total, channels = sw.shape
    rows = 2 * ROWS
    steps = total // lanes // rows
    row = pl.BlockSpec((rows, channels), lambda i: (lane * steps + i, 0))
    kept = [] if layer is None else [layer]
    return pl.pallas_call(
        layer_kernel,
        grid=(steps,),
        in_specs=[ANY, row, VMEM] + [HBM] * len(kept),
        out_specs=row,
        out_shape=pltpu.HBM((total, channels), bf16),
        input_output_aliases={3: 0} if kept else {},
        compiler_params=params(24),
        cost_estimate=cost(2 * total // lanes * channels * channels, 4 * total * channels),
        interpret=interpret,
        name=f"layer_out_{lane}",
    )(gate, sw, *near(w), *kept)


def outer(meta, inner, edge, other, cot, cot_other, blocks):
    channels, rows = inner.shape
    width = channels // 2
    return pl.pallas_call(
        functools.partial(outer_kernel, blocks),
        in_specs=[SMEM] + [HBM] * 2 + [ANY, HBM, ANY],
        out_specs=VMEM,
        out_shape=pltpu.VMEM((channels, width), f32),
        scratch_shapes=[
            pltpu.VMEM((3, channels, rows), bf16),
            pltpu.VMEM((3, rows, width), bf16),
            pltpu.SemaphoreType.DMA((3, 5)),
        ],
        compiler_params=params(16),
        cost_estimate=cost(6_000_000_000, 10 * rows * channels),
        name="outer_most",
    )(meta, *far(inner, edge), other, *far(cot), cot_other)


def last_outer(meta, acc, other, cot_other, blocks):
    channels, rows = other.shape
    width, share = channels // 2, channels // 4
    return pl.pallas_call(
        functools.partial(last_outer_kernel, blocks),
        in_specs=[SMEM, VMEM, ANY, ANY],
        out_specs=[VMEM] + [HBM] * 3,
        out_shape=[pltpu.VMEM((share, width), bf16)] + [pltpu.HBM((share, width), bf16)] * 3,
        scratch_shapes=[
            pltpu.VMEM((4, share, width), bf16),
            pltpu.VMEM((channels, rows), bf16),
            pltpu.VMEM((rows, width), bf16),
            pltpu.SemaphoreType.DMA((8,)),
        ],
        compiler_params=params(16),
        cost_estimate=cost(3_000_000_000, 10 * rows * channels),
        name="outer_last",
    )(meta, *near(acc), other, cot_other)


def first_sum(meta, parts, small, away, ends):
    share, width = parts[0].shape
    piece = share // 4
    tall = piece + small.shape[0]
    edges = 2 * EDGE * len(ends)
    return pl.pallas_call(
        first_sum_kernel,
        in_specs=[SMEM] + [VMEM] * (6 + len(ends)),
        out_specs=[VMEM] * 4,
        out_shape=[
            jax.ShapeDtypeStruct((tall, width), bf16),
            pltpu.HBM((tall + edges, width), bf16),
            pltpu.HBM((tall, width), bf16),
            pltpu.HBM((tall + edges, width), bf16),
        ],
        compiler_params=params(12),
        name="sum_first",
    )(meta, *parts, small, away, *ends)


def place(meta, got, share, scale):
    width = got[0].shape[1]
    return pl.pallas_call(
        functools.partial(place_kernel, scale),
        in_specs=[SMEM] + [VMEM] * 8,
        out_specs=[VMEM] * 4,
        out_shape=[
            jax.ShapeDtypeStruct((share, 2 * width), f32),
            jax.ShapeDtypeStruct((TAPS, 2 * width), f32),
            jax.ShapeDtypeStruct((2 * width,), f32),
            jax.ShapeDtypeStruct((2 * width,), f32),
        ],
        compiler_params=params(12),
        name="place",
    )(meta, *got)


def shifts(size):
    up = [(i, i + 1) for i in range(size - 1)]
    return up, [(j, i) for i, j in up]


EVERY = ("dp", "seq")


def along(axes, shift):
    pairs = []
    for device in range(128):
        where = {"y": device % 4, "c": device // 4 % 2, "x": device // 8 % 4, "z": device // 32}
        axis = axes[where["c"]]
        moved = dict(where)
        moved[axis] = (where[axis] + shift) % (2 if axis == "c" else 4)
        pairs.append((device, ((moved["z"] * 4 + moved["x"]) * 2 + moved["c"]) * 4 + moved["y"]))
    return pairs


def swap(value):
    return lax.ppermute(value, EVERY, along("cc", 1))


def spread(values, axes):
    return [lax.ppermute(value, EVERY, along(axes, s + 1)) for s, value in enumerate(values)]


def four(own, one, two, three):
    own, one, two, three = (v.astype(f32) for v in (own, one, two, three))
    return (own + two) + (one + three)


def all_four(value, axes):
    return four(value, *spread([value] * 3, axes))


def local(glu_out, lengths, kernel, norm_gain, norm_bias, w_out, cotangent, interpret=False):
    lanes, length, channels = glu_out.shape
    seq_count = lax.axis_size("seq")
    norm_scale = 1.0 / math.sqrt(lanes * lax.axis_size("dp") * length * seq_count)
    y = lax.axis_index("seq")
    dp = lax.axis_index("dp")
    core, x, z = lax.rem(dp, 2), lax.rem(lax.div(dp, 2), 4), lax.div(dp, 8)
    first = core == 0
    meta = jnp.stack(
        [
            y * length,
            core,
            jnp.where(first, x, z),
            y,
            jnp.where(first, x, z),
            jnp.where(first, z, x),
        ]
    ).astype(jnp.int32)
    up, down = shifts(seq_count)
    before = lax.ppermute(glu_out[:, length - EDGE :], "seq", up).reshape(lanes * EDGE, channels)
    after = lax.ppermute(glu_out[:, :EDGE], "seq", down).reshape(lanes * EDGE, channels)
    cot = cotangent.reshape(-1, channels)
    split, split_t, wide, deep = (jnp.asarray(t) for t in tables())
    spec = pl.pallas_call(
        spectrum_kernel,
        in_specs=[HBM] * 4,
        out_specs=VMEM,
        out_shape=pltpu.VMEM((3 * BINS + 8, channels), f32),
        scratch_shapes=[pltpu.VMEM(a.shape, f32) for a in (wide, kernel, norm_gain, norm_bias)]
        + [pltpu.SemaphoreType.DMA((4,))],
        compiler_params=params(12),
        interpret=interpret,
        name="spectrum",
    )(*far(wide, kernel, norm_gain, norm_bias))
    flat = glu_out.reshape(lanes * length, channels)
    blocks = length // ROWS
    inner = [(lane, block) for lane in range(lanes) for block in range(1, blocks - 1)]
    edge = [(lane, block) for lane in range(lanes) for block in (0, blocks - 1)]
    none = jnp.zeros((lanes * EDGE, channels), bf16)
    kept, turned_inner = (lambda *o: (o[:3], o[3]))(
        *forward(inner, meta, lengths, flat, none, none, split, split_t, spec, (), "conv_inner", interpret=interpret)
    )
    kept, turned_edge = (lambda *o: (o[:3], o[3]))(
        *forward(edge, meta, lengths, flat, before, after, split, split_t, spec, kept, "conv_edge", interpret=interpret)
    )
    sw, normed, istd = kept
    share, half = channels // seq_count, channels // 2
    whole_slice = lax.axis_size("dp") == 32
    if whole_slice:
        cot_other = swap(cot)
        acc = outer(meta, turned_inner, turned_edge, swap(turned_inner), cot, cot_other, blocks)
        parts = list(last_outer(meta, acc, swap(turned_edge), cot_other, blocks))
        sent = spread(parts[1:], "xz")
        cot, parts[0] = lax.optimization_barrier((cot, parts[0]))
    else:
        places = [jnp.concatenate([cot[(a * blocks + b) * ROWS :][:ROWS] for a, b in t]) for t in (inner, edge)]
        grad_w = lax.psum(dot(turned_inner, places[0]) + dot(turned_edge, places[1]), "seq") * norm_scale
        grad_w = lax.dynamic_slice_in_dim(grad_w, y * share, share, 0)
    small, gi, ends = jnp.zeros((48, channels), f32), None, []
    for lane in range(lanes):
        gi, end, small = backward(
            lane, meta, lengths, cot, normed, istd, flat, before, after, w_out, split, split_t, spec, deep, small, gi,
            interpret=interpret,
        )
        ends.append(end)
    if whole_slice:
        own, *sent = first_sum(meta, parts[:1] + sent, small, swap(small), ends)
        layer = project(0, lanes, own, sw, w_out, None)
        one, two, three = spread(sent, "yy")
        three, layer = lax.optimization_barrier((three, layer))
        tall = own.shape[0]
        after_tail, before_head = (jnp.concatenate(jnp.split(v[tall:], 2), axis=1) for v in (three, one))
        sent = four(own, one[:tall], two, three[:tall]).astype(bf16)
        layer = project(1, lanes, sent, sw, w_out, layer)
        got = [sent] + spread([sent] * 3, "zx")
        got[3], layer = lax.optimization_barrier((got[3], layer))
        sent = four(*got).astype(bf16)
        got = [sent] + spread([sent] * 3, "xz")
        grad_w, taps, gain, bias = place(meta, got + [swap(v) for v in got], share, norm_scale)
    else:
        layer = None
        for lane in range(lanes):
            layer = project(lane, lanes, sw, sw, w_out, layer, interpret=interpret)
        heads = jnp.concatenate([e[:EDGE] for e in ends])
        tails = jnp.concatenate([e[EDGE:] for e in ends])
        before_head, after_tail = lax.ppermute(tails, "seq", up), lax.ppermute(heads, "seq", down)
        small = lax.psum(small, "seq") * norm_scale
        taps, gain, bias = small[:TAPS], small[32], small[33]
    before = jnp.where(y == 0, 0.0, before_head.astype(f32)).astype(bf16).reshape(lanes, EDGE, channels)
    after = jnp.where(y == seq_count - 1, 0.0, after_tail.astype(f32)).astype(bf16).reshape(lanes, EDGE, channels)
    gi = gi.reshape(lanes, length, channels)
    gi = gi.at[:, :EDGE].add(before).at[:, length - EDGE :].add(after)
    return (layer.reshape(lanes, length, channels), gi, grad_w, taps, gain, bias)


def solution(mesh):
    in_specs = (P("dp", "seq", None), P("dp", None), P(), P(), P(), P(), P("dp", "seq", None))
    out_specs = (P("dp", "seq", None), P("dp", "seq", None), P("seq", None), P(), P(), P())
    return jax.shard_map(local, mesh=mesh, in_specs=in_specs, out_specs=out_specs, check_vma=False)
```

```python
import functools
import math

import jax
import jax.numpy as jnp
import numpy as np
from jax import lax
from jax.experimental import pallas as pl
from jax.experimental.pallas import tpu as pltpu
from jax.sharding import PartitionSpec as P

EPSILON = 1e-05
TAPS = 31
HALF = TAPS // 2
ROWS = 128
EDGE = 16
WINDOW = ROWS + 2 * EDGE
POINTS = 256
BINS = POINTS // 2
f32, bf16 = jnp.float32, jnp.bfloat16


def tables():
    place = np.arange(POINTS)
    bins = np.arange(BINS)[:, None]
    cosines = math.sqrt(2.0 / POINTS) * np.cos(2 * np.pi * ((bins * place) % POINTS) / POINTS)
    sines = math.sqrt(2.0 / POINTS) * np.sin(2 * np.pi * ((bins * place) % POINTS) / POINTS)
    cosines[0] = 1.0 / math.sqrt(POINTS)
    sines[0] = (1.0 - 2.0 * (place % 2)) / math.sqrt(POINTS)
    basis = np.concatenate([cosines, sines])
    high = basis.astype(jnp.bfloat16)
    low = (basis - high.astype(np.float64)).astype(jnp.bfloat16)
    split = np.concatenate([high, low])
    lags = np.arange(TAPS) - HALF
    turn = 2 * np.pi * ((bins * lags) % POINTS) / POINTS
    real, imag = np.cos(turn), np.sin(turn)
    other = real.copy()
    other[0] = 1.0 - 2.0 * (np.abs(lags) % 2)
    spectrum = np.concatenate([real, imag, other]).astype(np.float32)
    gather = np.concatenate([real, other, -imag]).astype(np.float32)
    wide, deep = np.zeros((3 * BINS, 32), np.float32), np.zeros((32, 3 * BINS), np.float32)
    wide[:, :TAPS], deep[:TAPS] = spectrum, gather.T
    return split, np.ascontiguousarray(split.T), wide, deep


def gapped(lengths_ref, lane, first, shape, dim, skip):
    row = lax.broadcasted_iota(jnp.int32, shape, dim) + skip
    frame = first + row
    place, end = row, 0
    for utter in range(lengths_ref.shape[1] - 1):
        end = end + lengths_ref[lane, utter]
        place = place + jnp.where(frame >= end, jnp.where(first < end, HALF, 0), 0)
    return place


def chosen_columns(split, place):
    count = place.shape[1]
    one_hot = (lax.broadcasted_iota(jnp.int32, (POINTS, count), 0) == place).astype(f32).astype(bf16)
    return jnp.dot(split, one_hot, preferred_element_type=f32).astype(bf16)


def chosen_rows(split_t, place):
    count = place.shape[0]
    one_hot = (lax.broadcasted_iota(jnp.int32, (count, POINTS), 1) == place).astype(f32).astype(bf16)
    return jnp.dot(one_hot, split_t, preferred_element_type=f32).astype(bf16)


def dot(a, b):
    return jnp.dot(a, b, preferred_element_type=f32)


def sigmoid(a):
    return 0.5 * jnp.tanh(0.5 * a) + 0.5


def window(x_ref, before_ref, after_ref, task, blocks, cols):
    lane, block = task
    start = (lane * blocks + block) * ROWS
    halo = slice(lane * EDGE, (lane + 1) * EDGE)
    if block == 0:
        return jnp.concatenate([before_ref[halo, cols], x_ref[start : start + ROWS + EDGE, cols]])
    if block == blocks - 1:
        return jnp.concatenate([x_ref[start - EDGE : start + ROWS, cols], after_ref[halo, cols]])
    return x_ref[start - EDGE : start + ROWS + EDGE, cols]


def forward_kernel(tasks, blocks, meta_ref, lengths_ref, x_ref, before_ref, after_ref, split_ref, split_t_ref, spec_ref,
                   *rest):
    outs, (turned_ref, conv, sw, normed_all, istd, sems) = rest[-9:-6], rest[-6:]
    channels = x_ref.shape[1]
    gain, bias = spec_ref[3 * BINS : 3 * BINS + 1], spec_ref[3 * BINS + 1 : 3 * BINS + 2]
    strip, width = 16, channels
    bases, copies = [], []
    for lane, block in tasks:
        first = meta_ref[0] + (block * ROWS - EDGE)
        into = chosen_columns(split_ref[...], gapped(lengths_ref, lane, first, (1, WINDOW), 1, 0))
        back = chosen_rows(split_t_ref[...], gapped(lengths_ref, lane, first, (ROWS, 1), 0, EDGE))
        bases.append((into, jnp.concatenate([back[:, :POINTS], back[:, POINTS:]])))

    def transform(task):
        into, back = bases[task]
        for at in range(0, channels, width):
            cols = slice(at, at + width)
            pair = dot(into, window(x_ref, before_ref, after_ref, tasks[task], blocks, cols))
            real, imag = pair[:BINS] + pair[POINTS : POINTS + BINS], pair[BINS:POINTS] + pair[POINTS + BINS :]
            p, q, other = spec_ref[:BINS, cols], spec_ref[BINS:POINTS, cols], spec_ref[POINTS : 3 * BINS, cols]
            zed = jnp.concatenate([real * p + imag * q, imag * other - real * q]).astype(bf16)
            pair = dot(back, zed)
            conv[task, :, cols] = pair[:ROWS] + pair[ROWS:]

    def normalise(task):
        for at in range(0, ROWS, strip):
            place = slice(task * ROWS + at, task * ROWS + at + strip)
            value = conv[task, at : at + strip]
            centred = value - jnp.sum(value, axis=1, keepdims=True) * (1.0 / channels)
            variance = jnp.sum(centred * centred, axis=1, keepdims=True) * (1.0 / channels)
            inv_std = lax.rsqrt(variance + EPSILON)
            normed = centred * inv_std
            affine = normed * gain + bias
            sw[place] = (affine * sigmoid(affine)).astype(bf16)
            normed_all[place] = normed.astype(bf16)
            istd[place] = jnp.broadcast_to(inv_std, (strip, istd.shape[1]))
        own = slice(task * ROWS, (task + 1) * ROWS)
        turned_ref[:, own] = sw[own].T
        lane, block = tasks[task]
        for k, (source, target) in enumerate(zip((sw, normed_all, istd), outs)):
            size = ROWS
            copy = pltpu.make_async_copy(
                source.at[pl.ds(task * size, size)],
                target.at[pl.ds((lane * blocks + block) * size, size)],
                sems.at[task, k],
            )
            copy.start()
            copies.append(copy)

    for task in range(len(tasks) + 1):
        if task < len(tasks):
            transform(task)
        if task > 0:
            normalise(task - 1)
    for copy in copies:
        copy.wait()


def backward_kernel(lane, blocks, meta_ref, lengths_ref, cot_ref, normed_ref, istd_ref, x_ref, before_ref, after_ref, w_ref,
                    split_ref, split_t_ref, spec_ref, gather_ref, carry_ref, *rest):
    gi_out, edge_ref, small_ref, gs, g, gi, sums, sems = rest[-8:]
    channels = cot_ref.shape[1]
    length = blocks * ROWS
    begin = lane * length
    gain, bias = spec_ref[3 * BINS : 3 * BINS + 1], spec_ref[3 * BINS + 1 : 3 * BINS + 2]
    strip, width = 16, channels // 2
    bases, copies, seen = [], [], []
    for block in range(blocks):
        first = meta_ref[0] + (block * ROWS - EDGE)
        seen.append(chosen_columns(split_ref[:POINTS], gapped(lengths_ref, lane, first, (1, WINDOW), 1, 0)))
        into = chosen_columns(split_ref[...], gapped(lengths_ref, lane, first, (1, ROWS), 1, EDGE))
        into = jnp.concatenate([into[:POINTS], into[POINTS:]], axis=1)
        back = chosen_rows(split_t_ref[...], gapped(lengths_ref, lane, first, (WINDOW, 1), 0, 0))
        bases.append((into, jnp.concatenate([back[:, :POINTS], back[:, POINTS:]])))
    sums[...] = jnp.zeros_like(sums)
    gs[...] = lax.dot_general(
        cot_ref[begin : begin + length], w_ref[...], (((1,), (1,)), ((), ())), preferred_element_type=f32
    )
    for at in range(0, length, strip):
        place = slice(begin + at, begin + at + strip)
        normed = normed_ref[place].astype(f32)
        affine = normed * gain + bias
        gate = sigmoid(affine)
        grad = gs[at : at + strip] * gate * (1.0 + affine * (1.0 - gate))
        prod = grad * normed
        sums[:8] += prod[:8] + prod[8:]
        sums[8:] += grad[:8] + grad[8:]
        grad_normed = grad * gain
        mean = jnp.sum(grad_normed, axis=1, keepdims=True) * (1.0 / channels)
        along = jnp.sum(grad_normed * normed, axis=1, keepdims=True) * (1.0 / channels)
        out = (istd_ref[place, :1] * (grad_normed - mean - normed * along)).astype(bf16)
        row = at // ROWS * 2 * ROWS + at % ROWS
        g[row : row + strip] = out
        g[row + ROWS : row + ROWS + strip] = out
    table_high, table_low = halves(gather_ref[...])
    for at in range(0, channels, width):
        cols = slice(at, at + width)
        p, q, other = spec_ref[:BINS, cols], spec_ref[BINS:POINTS, cols], spec_ref[POINTS : 3 * BINS, cols]
        cross, pending, tail = None, None, None
        for block in range(blocks):
            into, back = bases[block]
            ghat = dot(into, g[block * 2 * ROWS : (block + 1) * 2 * ROWS, cols])
            cg, sg = ghat[:BINS], ghat[BINS:]
            rows = window(x_ref, before_ref, after_ref, (lane, block), blocks, cols)
            xhat = dot(seen[block], rows)
            cx, sx = xhat[:BINS], xhat[BINS:]
            terms = (cg * cx, sg * sx, sg * cx - cg * sx)
            cross = terms if cross is None else tuple(a + b for a, b in zip(cross, terms))
            vee = jnp.concatenate([cg * p - sg * q, sg * other + cg * q]).astype(bf16)
            pair = dot(back, vee)
            part = pair[:WINDOW] + pair[WINDOW:]
            head, out, base = part[:EDGE], part[EDGE : EDGE + ROWS], block * ROWS
            if block == 0:
                edge_ref[:EDGE, cols] = head.astype(bf16)
                gi[:EDGE, cols] = out[:EDGE].astype(bf16)
            else:
                gi[base - EDGE : base, cols] = (pending + head).astype(bf16)
                gi[base : base + EDGE, cols] = (out[:EDGE] + tail).astype(bf16)
            gi[base + EDGE : base + ROWS - EDGE, cols] = out[EDGE : ROWS - EDGE].astype(bf16)
            pending, tail = out[ROWS - EDGE :], part[EDGE + ROWS :]
        gi[length - EDGE :, cols] = pending.astype(bf16)
        edge_ref[EDGE:, cols] = tail.astype(bf16)
        copy = pltpu.make_async_copy(gi.at[:, cols], gi_out.at[pl.ds(begin, length), cols], sems.at[at // width])
        copy.start()
        copies.append(copy)
        high, low = halves(jnp.concatenate(cross))
        value = dot(table_high, high) + dot(table_low, high) + dot(table_high, low)
        small_ref[:32, cols] = value + carry_ref[:32, cols]
    prod, grad = sums[:8], sums[8:]
    small_ref[32:] = carry_ref[32:] + jnp.concatenate(
        [
            jnp.sum(prod, axis=0, keepdims=True),
            jnp.sum(grad, axis=0, keepdims=True),
            jnp.zeros((14, channels), f32),
        ]
    )
    for copy in copies:
        copy.wait()


def layer_kernel(gate_ref, sw_ref, w_ref, *rest):
    rest[-1][...] = dot(sw_ref[...], w_ref[...]).astype(bf16)


def halves(value):
    high = value.astype(bf16)
    return high, (value - high.astype(f32)).astype(bf16)


def spectrum_kernel(*refs):
    sources, spec_ref, targets, sems = refs[:4], refs[4], refs[5:9], refs[9]
    copies = [pltpu.make_async_copy(a, b, sems.at[k]) for k, (a, b) in enumerate(zip(sources, targets))]
    for copy in copies:
        copy.start()
    for copy in copies:
        copy.wait()
    table_ref, kernel_ref, gain_ref, bias_ref = targets
    channels = kernel_ref.shape[1]
    table_high, table_low = halves(table_ref[...])
    taps = jnp.concatenate([kernel_ref[...], jnp.zeros((32 - TAPS, channels), f32)])
    high, low = halves(taps)
    spec_ref[: 3 * BINS] = dot(table_high, high) + dot(table_low, high) + dot(table_high, low)
    spec_ref[3 * BINS :] = jnp.concatenate(
        [gain_ref[...].reshape(1, channels), bias_ref[...].reshape(1, channels), jnp.zeros((6, channels), f32)]
    )


def frame_rows(cot_ref, target, cols, blocks, edges, sems):
    length = blocks * ROWS
    if edges:
        spans = [(k * length + b * ROWS, ROWS) for k in range(cot_ref.shape[0] // length) for b in (0, blocks - 1)]
    else:
        spans = [(k * length + ROWS, length - 2 * ROWS) for k in range(cot_ref.shape[0] // length)]
    copies, at = [], 0
    for k, (start, size) in enumerate(spans):
        source = cot_ref.at[pl.ds(start, size), cols]
        copies.append(pltpu.make_async_copy(source, target.at[pl.ds(at, size)], sems.at[k]))
        at += size
    return copies


def outer_kernel(blocks, meta_ref, inner_ref, edge_ref, other_ref, cot_ref, cot_other_ref, acc_ref, left, right, sems):
    share, width = acc_ref.shape[0] // 4, acc_ref.shape[1]
    cols = pl.ds(pl.multiple_of(meta_ref[1] * width, width), width)
    loads = []
    for k, (source, cot, edges) in enumerate(
        ((inner_ref, cot_ref, False), (edge_ref, cot_ref, True), (other_ref, cot_other_ref, False))
    ):
        copies = [pltpu.make_async_copy(source, left.at[k], sems.at[k, 4])]
        copies += frame_rows(cot, right.at[k], cols, blocks, edges, sems.at[k])
        for copy in copies:
            copy.start()
        loads.append(copies)
    for k, copies in enumerate(loads):
        for copy in copies:
            copy.wait()
        for at in range(4):
            part = slice(at * share, (at + 1) * share)
            value = dot(left[k, part], right[k])
            acc_ref[part] = value if k == 0 else acc_ref[part] + value


def last_outer_kernel(blocks, meta_ref, acc_ref, sw_ref, cot_ref, own_ref, one_ref, two_ref, three_ref, chunks, left,
                      right, sems):
    share, width = acc_ref.shape[0] // 4, acc_ref.shape[1]
    piece = share // 4
    cols = pl.ds(pl.multiple_of(meta_ref[1] * width, width), width)
    copies = frame_rows(cot_ref, right, cols, blocks, True, sems)
    for at in range(4):
        rows = pl.ds(at * share, share)
        copies.append(pltpu.make_async_copy(sw_ref.at[rows], left.at[rows], sems.at[4 + at]))
    for copy in copies:
        copy.start()
    for copy in copies[:-4]:
        copy.wait()
    for at in range(4):
        part = slice(at * share, (at + 1) * share)
        copies[at - 4].wait()
        value = (acc_ref[part] + dot(left[part], right[...])).astype(bf16)
        for k in range(4):
            shift = lax.rem(k + 4 - meta_ref[2], 4)
            chunks[shift, at * piece : (at + 1) * piece] = value[k * piece : (k + 1) * piece]
    copies = [
        pltpu.make_async_copy(chunks.at[1 + k], ref, sems.at[k]) for k, ref in enumerate((one_ref, two_ref, three_ref))
    ]
    for copy in copies:
        copy.start()
    own_ref[...] = chunks[0]
    for copy in copies:
        copy.wait()


def first_sum_kernel(meta_ref, a_ref, b_ref, c_ref, d_ref, small_ref, away_ref, *rest):
    ends, outs = rest[:-4], rest[-4:]
    width = a_ref.shape[1]
    piece = a_ref.shape[0] // 4
    tall = piece + small_ref.shape[0]
    cols = pl.ds(pl.multiple_of(meta_ref[1] * width, width), width)
    small = (small_ref[:, cols] + away_ref[:, cols]).astype(bf16)
    for shift, ref in enumerate(outs):
        rows = pl.ds(pl.multiple_of(lax.rem(meta_ref[3] + shift, 4) * piece, piece), piece)
        ref[:piece] = four(a_ref[rows], b_ref[rows], c_ref[rows], d_ref[rows]).astype(bf16)
        ref[piece:tall] = small
    for ref, begin in ((outs[1], EDGE), (outs[3], 0)):
        at = tall
        for side in range(2):
            for end in ends:
                ref[at : at + EDGE] = end[begin : begin + EDGE, side * width : (side + 1) * width]
                at += EDGE


def place_kernel(scale, meta_ref, *refs):
    out_ref, taps_ref, gain_ref, bias_ref = refs[-4:]
    width = refs[0].shape[1]
    piece = out_ref.shape[0] // 4
    small = []
    for side in range(2):
        core = meta_ref[1] if side == 0 else 1 - meta_ref[1]
        place = meta_ref[4] if side == 0 else meta_ref[5]
        cols = pl.ds(pl.multiple_of(core * width, width), width)
        got = refs[side * 4 : side * 4 + 4]
        for shift in range(4):
            rows = pl.ds(pl.multiple_of(lax.rem(place + 4 - shift, 4) * piece, piece), piece)
            out_ref[rows, cols] = got[shift][:piece].astype(f32) * scale
        small.append(four(*(ref[piece:] for ref in got)) * scale)
    first = meta_ref[1] == 0
    for side in range(2):
        cols = slice(side * width, (side + 1) * width)
        value = jnp.where(first == (side == 0), small[0], small[1])
        taps_ref[:, cols] = value[:TAPS]
        gain_ref[cols] = value[32]
        bias_ref[cols] = value[33]


def whole(shape):
    return pl.BlockSpec(shape, lambda *i: (0,) * len(shape))


SMEM = pl.BlockSpec(memory_space=pltpu.SMEM)
HBM = pl.BlockSpec(memory_space=pltpu.HBM)
ANY = pl.BlockSpec(memory_space=pl.ANY)
VMEM = pl.BlockSpec(memory_space=pltpu.VMEM)


def params(mebibytes):
    return pltpu.CompilerParams(vmem_limit_bytes=mebibytes << 20)


def cost(flops, moved):
    return pl.CostEstimate(flops=flops, bytes_accessed=moved, transcendentals=0)


def near(*arrays):
    return [pltpu.with_memory_space_constraint(a, pltpu.VMEM) for a in arrays]


def far(*arrays):
    return [pltpu.with_memory_space_constraint(a, pltpu.HBM) for a in arrays]


def forward(tasks, meta, lengths, flat, before, after, split, split_t, spec, kept, name, interpret=False):
    total, channels = flat.shape
    blocks = total // lengths.shape[0] // ROWS
    count = len(tasks)
    rows = count * ROWS
    return pl.pallas_call(
        functools.partial(forward_kernel, tasks, blocks),
        in_specs=[SMEM, SMEM] + [VMEM] * 6 + [HBM] * len(kept),
        out_specs=[HBM] * 3 + [VMEM],
        out_shape=[
            pltpu.HBM((total, channels), bf16),
            pltpu.HBM((total, channels), bf16),
            pltpu.HBM((total, 128), f32),
            pltpu.HBM((channels, rows), bf16),
        ],
        scratch_shapes=[
            pltpu.VMEM((count, ROWS, channels), f32),
            pltpu.VMEM((rows, channels), bf16),
            pltpu.VMEM((rows, channels), bf16),
            pltpu.VMEM((rows, 128), f32),
            pltpu.SemaphoreType.DMA((count, 3)),
        ],
        input_output_aliases={8 + k: k for k in range(len(kept))},
        compiler_params=params(32),
        cost_estimate=cost(25_000_000_000, rows * channels * 12),
        interpret=interpret,
        name=name,
    )(meta, lengths, *near(flat, before, after, split, split_t, spec), *kept)


def backward(lane, meta, lengths, cot, normed, istd, x, before, after, w, split, split_t, spec, gather, carry, gi, interpret=False):
    total, channels = cot.shape
    length = total // lengths.shape[0]
    blocks = length // ROWS
    kept = [] if gi is None else [gi]
    return pl.pallas_call(
        functools.partial(backward_kernel, lane, blocks),
        in_specs=[SMEM, SMEM] + [VMEM] * 12 + [HBM] * len(kept),
        out_specs=[HBM, VMEM, VMEM],
        out_shape=[
            pltpu.HBM((total, channels), bf16),
            jax.ShapeDtypeStruct((2 * EDGE, channels), bf16),
            jax.ShapeDtypeStruct((48, channels), f32),
        ],
        scratch_shapes=[
            pltpu.VMEM((length, channels), f32),
            pltpu.VMEM((2 * length, channels), bf16),
            pltpu.VMEM((length, channels), bf16),
            pltpu.VMEM((16, channels), f32),
            pltpu.SemaphoreType.DMA((3,)),
        ],
        input_output_aliases={14: 0} if kept else {},
        compiler_params=params(24),
        cost_estimate=cost(12_000_000_000, length * channels * 20),
        interpret=interpret,
        name=f"backward_{lane}",
    )(meta, lengths, *near(cot, normed, istd, x, before, after, w, split, split_t, spec, gather, carry), *kept)


def project(lane, lanes, gate, sw, w, layer, interpret=False):
    total, channels = sw.shape
    rows = 2 * ROWS
    steps = total // lanes // rows
    row = pl.BlockSpec((rows, channels), lambda i: (lane * steps + i, 0))
    kept = [] if layer is None else [layer]
    return pl.pallas_call(
        layer_kernel,
        grid=(steps,),
        in_specs=[ANY, row, VMEM] + [HBM] * len(kept),
        out_specs=row,
        out_shape=pltpu.HBM((total, channels), bf16),
        input_output_aliases={3: 0} if kept else {},
        compiler_params=params(24),
        cost_estimate=cost(2 * total // lanes * channels * channels, 4 * total * channels),
        interpret=interpret,
        name=f"layer_out_{lane}",
    )(gate, sw, *near(w), *kept)


def outer(meta, inner, edge, other, cot, cot_other, blocks):
    channels, rows = inner.shape
    width = channels // 2
    return pl.pallas_call(
        functools.partial(outer_kernel, blocks),
        in_specs=[SMEM] + [HBM] * 2 + [ANY, HBM, ANY],
        out_specs=VMEM,
        out_shape=pltpu.VMEM((channels, width), f32),
        scratch_shapes=[
            pltpu.VMEM((3, channels, rows), bf16),
            pltpu.VMEM((3, rows, width), bf16),
            pltpu.SemaphoreType.DMA((3, 5)),
        ],
        compiler_params=params(16),
        cost_estimate=cost(6_000_000_000, 10 * rows * channels),
        name="outer_most",
    )(meta, *far(inner, edge), other, *far(cot), cot_other)


def last_outer(meta, acc, other, cot_other, blocks):
    channels, rows = other.shape
    width, share = channels // 2, channels // 4
    return pl.pallas_call(
        functools.partial(last_outer_kernel, blocks),
        in_specs=[SMEM, VMEM, ANY, ANY],
        out_specs=[VMEM] + [HBM] * 3,
        out_shape=[pltpu.VMEM((share, width), bf16)] + [pltpu.HBM((share, width), bf16)] * 3,
        scratch_shapes=[
            pltpu.VMEM((4, share, width), bf16),
            pltpu.VMEM((channels, rows), bf16),
            pltpu.VMEM((rows, width), bf16),
            pltpu.SemaphoreType.DMA((8,)),
        ],
        compiler_params=params(16),
        cost_estimate=cost(3_000_000_000, 10 * rows * channels),
        name="outer_last",
    )(meta, *near(acc), other, cot_other)


def first_sum(meta, parts, small, away, ends):
    share, width = parts[0].shape
    piece = share // 4
    tall = piece + small.shape[0]
    edges = 2 * EDGE * len(ends)
    return pl.pallas_call(
        first_sum_kernel,
        in_specs=[SMEM] + [VMEM] * (6 + len(ends)),
        out_specs=[VMEM] * 4,
        out_shape=[
            jax.ShapeDtypeStruct((tall, width), bf16),
            pltpu.HBM((tall + edges, width), bf16),
            pltpu.HBM((tall, width), bf16),
            pltpu.HBM((tall + edges, width), bf16),
        ],
        compiler_params=params(12),
        name="sum_first",
    )(meta, *parts, small, away, *ends)


def place(meta, got, share, scale):
    width = got[0].shape[1]
    return pl.pallas_call(
        functools.partial(place_kernel, scale),
        in_specs=[SMEM] + [VMEM] * 8,
        out_specs=[VMEM] * 4,
        out_shape=[
            jax.ShapeDtypeStruct((share, 2 * width), f32),
            jax.ShapeDtypeStruct((TAPS, 2 * width), f32),
            jax.ShapeDtypeStruct((2 * width,), f32),
            jax.ShapeDtypeStruct((2 * width,), f32),
        ],
        compiler_params=params(12),
        name="place",
    )(meta, *got)


def shifts(size):
    up = [(i, i + 1) for i in range(size - 1)]
    return up, [(j, i) for i, j in up]


EVERY = ("dp", "seq")


def along(axes, shift):
    pairs = []
    for device in range(128):
        where = {"y": device % 4, "c": device // 4 % 2, "x": device // 8 % 4, "z": device // 32}
        axis = axes[where["c"]]
        moved = dict(where)
        moved[axis] = (where[axis] + shift) % (2 if axis == "c" else 4)
        pairs.append((device, ((moved["z"] * 4 + moved["x"]) * 2 + moved["c"]) * 4 + moved["y"]))
    return pairs


def swap(value):
    return lax.ppermute(value, EVERY, along("cc", 1))


def spread(values, axes):
    return [lax.ppermute(value, EVERY, along(axes, s + 1)) for s, value in enumerate(values)]


def four(own, one, two, three):
    own, one, two, three = (v.astype(f32) for v in (own, one, two, three))
    return (own + two) + (one + three)


def all_four(value, axes):
    return four(value, *spread([value] * 3, axes))


def local(glu_out, lengths, kernel, norm_gain, norm_bias, w_out, cotangent, interpret=False):
    lanes, length, channels = glu_out.shape
    seq_count = lax.axis_size("seq")
    norm_scale = 1.0 / math.sqrt(lanes * lax.axis_size("dp") * length * seq_count)
    y = lax.axis_index("seq")
    dp = lax.axis_index("dp")
    core, x, z = lax.rem(dp, 2), lax.rem(lax.div(dp, 2), 4), lax.div(dp, 8)
    first = core == 0
    meta = jnp.stack(
        [
            y * length,
            core,
            jnp.where(first, x, z),
            y,
            jnp.where(first, x, z),
            jnp.where(first, z, x),
        ]
    ).astype(jnp.int32)
    up, down = shifts(seq_count)
    before = lax.ppermute(glu_out[:, length - EDGE :], "seq", up).reshape(lanes * EDGE, channels)
    after = lax.ppermute(glu_out[:, :EDGE], "seq", down).reshape(lanes * EDGE, channels)
    cot = cotangent.reshape(-1, channels)
    split, split_t, wide, deep = (jnp.asarray(t) for t in tables())
    spec = pl.pallas_call(
        spectrum_kernel,
        in_specs=[HBM] * 4,
        out_specs=VMEM,
        out_shape=pltpu.VMEM((3 * BINS + 8, channels), f32),
        scratch_shapes=[pltpu.VMEM(a.shape, f32) for a in (wide, kernel, norm_gain, norm_bias)]
        + [pltpu.SemaphoreType.DMA((4,))],
        compiler_params=params(12),
        interpret=interpret,
        name="spectrum",
    )(*far(wide, kernel, norm_gain, norm_bias))
    flat = glu_out.reshape(lanes * length, channels)
    blocks = length // ROWS
    inner = [(lane, block) for lane in range(lanes) for block in range(1, blocks - 1)]
    edge = [(lane, block) for lane in range(lanes) for block in (0, blocks - 1)]
    none = jnp.zeros((lanes * EDGE, channels), bf16)
    kept, turned_inner = (lambda *o: (o[:3], o[3]))(
        *forward(inner, meta, lengths, flat, none, none, split, split_t, spec, (), "conv_inner", interpret=interpret)
    )
    kept, turned_edge = (lambda *o: (o[:3], o[3]))(
        *forward(edge, meta, lengths, flat, before, after, split, split_t, spec, kept, "conv_edge", interpret=interpret)
    )
    sw, normed, istd = kept
    share, half = channels // seq_count, channels // 2
    whole_slice = lax.axis_size("dp") == 32
    if whole_slice:
        cot_other = swap(cot)
        acc = outer(meta, turned_inner, turned_edge, swap(turned_inner), cot, cot_other, blocks)
        acc, late = lax.optimization_barrier((acc, turned_edge))
        parts = list(last_outer(meta, acc, swap(late), cot_other, blocks))
        sent = spread(parts[1:], "xz")
        cot, parts[0] = lax.optimization_barrier((cot, parts[0]))
    else:
        places = [jnp.concatenate([cot[(a * blocks + b) * ROWS :][:ROWS] for a, b in t]) for t in (inner, edge)]
        grad_w = lax.psum(dot(turned_inner, places[0]) + dot(turned_edge, places[1]), "seq") * norm_scale
        grad_w = lax.dynamic_slice_in_dim(grad_w, y * share, share, 0)
    small, gi, ends = jnp.zeros((48, channels), f32), None, []
    for lane in range(lanes):
        gi, end, small = backward(
            lane, meta, lengths, cot, normed, istd, flat, before, after, w_out, split, split_t, spec, deep, small, gi,
            interpret=interpret,
        )
        ends.append(end)
    if whole_slice:
        own, *sent = first_sum(meta, parts[:1] + sent, small, swap(small), ends)
        layer = project(0, lanes, own, sw, w_out, None)
        one, two, three = spread(sent, "yy")
        three, layer = lax.optimization_barrier((three, layer))
        tall = own.shape[0]
        after_tail, before_head = (jnp.concatenate(jnp.split(v[tall:], 2), axis=1) for v in (three, one))
        sent = four(own, one[:tall], two, three[:tall]).astype(bf16)
        layer = project(1, lanes, sent, sw, w_out, layer)
        got = [sent] + spread([sent] * 3, "zx")
        got[3], layer = lax.optimization_barrier((got[3], layer))
        sent = four(*got).astype(bf16)
        got = [sent] + spread([sent] * 3, "xz")
        grad_w, taps, gain, bias = place(meta, got + [swap(v) for v in got], share, norm_scale)
    else:
        layer = None
        for lane in range(lanes):
            layer = project(lane, lanes, sw, sw, w_out, layer, interpret=interpret)
        heads = jnp.concatenate([e[:EDGE] for e in ends])
        tails = jnp.concatenate([e[EDGE:] for e in ends])
        before_head, after_tail = lax.ppermute(tails, "seq", up), lax.ppermute(heads, "seq", down)
        small = lax.psum(small, "seq") * norm_scale
        taps, gain, bias = small[:TAPS], small[32], small[33]
    before = jnp.where(y == 0, 0.0, before_head.astype(f32)).astype(bf16).reshape(lanes, EDGE, channels)
    after = jnp.where(y == seq_count - 1, 0.0, after_tail.astype(f32)).astype(bf16).reshape(lanes, EDGE, channels)
    gi = gi.reshape(lanes, length, channels)
    gi = gi.at[:, :EDGE].add(before).at[:, length - EDGE :].add(after)
    return (layer.reshape(lanes, length, channels), gi, grad_w, taps, gain, bias)


def solution(mesh):
    in_specs = (P("dp", "seq", None), P("dp", None), P(), P(), P(), P(), P("dp", "seq", None))
    out_specs = (P("dp", "seq", None), P("dp", "seq", None), P("seq", None), P(), P(), P())
    return jax.shard_map(local, mesh=mesh, in_specs=in_specs, out_specs=out_specs, check_vma=False)
```
